32 devices in a mesh: wide: 16 (over z, y, x), narrow: 2 (over core).
Axes of the slice: x: 2, y: 2, z: 4, core: 2. Of those that a mesh axis runs over, the one named last changes fastest.
Arguments:
- tokens: bfloat16 [32768, 768], P(('wide', 'narrow')), may hold values from -6 to 6
- seq_lengths: int32 [32, 4], P(('wide', 'narrow')), may hold values from 0 to 1024, as said below
- w_query: bfloat16 [768, 768], P('wide'), may hold values from -0.21875 to 0.21875
- w_key: bfloat16 [768, 768], P('wide'), may hold values from -0.21875 to 0.21875
- w_value: bfloat16 [768, 768], P('wide'), may hold values from -0.21875 to 0.21875
- w_out: bfloat16 [768, 768], P('wide'), may hold values from -0.625 to 0.625
- w_gate: bfloat16 [768, 2048], P('wide'), may hold values from -0.21875 to 0.21875
- w_up: bfloat16 [768, 2048], P('wide'), may hold values from -0.21875 to 0.21875
- w_down: bfloat16 [2048, 768], P('wide'), may hold values from -0.25 to 0.25
- attn_gain: bfloat16 [768], P('wide'), may hold values from 0.5 to 1.5
- ffn_gain: bfloat16 [768], P('wide'), may hold values from 0.5 to 1.5
- cotangent: bfloat16 [32768, 768], P(('wide', 'narrow')), may hold values from -6 to 6
Outputs:
- output: bfloat16 [32768, 768], P(('wide', 'narrow'))
- grad_tokens: bfloat16 [32768, 768], P(('wide', 'narrow'))
- grad_w_query: float32 [768, 768], P('wide')
- grad_w_key: float32 [768, 768], P('wide')
- grad_w_value: float32 [768, 768], P('wide')
- grad_w_out: float32 [768, 768], P('wide')
- grad_w_gate: float32 [768, 2048], P('wide')
- grad_w_up: float32 [768, 2048], P('wide')
- grad_w_down: float32 [2048, 768], P('wide')
- grad_attn_gain: float32 [768], P('wide')
- grad_ffn_gain: float32 [768], P('wide')
The draws below stay inside these ranges and needn't reach their ends.
Inputs may be any that keep to these rules, and one draw needn't show every extreme that they name: `seq_lengths`: each row lists the lengths of one device's sequences, each 0, 256, 512 or 1024, summing to 1024, zeros last; some device holds one sequence of 1024.
All inputs are finite; a program needn't handle non-finite values.
Results may differ from the reference program's by a relative error of at most 0.017.
Values may be sent and summed in bfloat16 or wider, within the bound.
A program may use at most 320 MiB of HBM per device.

```python
import math
import jax
import jax.numpy as jnp
from jax import lax

D = 768
HEADS = 12
HEAD_DIM = 64
FF = 2048
TOK_DEV = 1024
SLOTS = 4
TOKENS = 32768
N_WIDE = 16
N_NARROW = 2


def draw_seq_lengths(key, part):
    key = jax.random.fold_in(key, 7)
    quarter = TOK_DEV // 4
    patterns = jnp.array([[4, 0, 0, 0], [2, 2, 0, 0], [2, 1, 1, 0], [1, 1, 1, 1], [1, 2, 1, 0]], jnp.int32)
    devices_all = N_WIDE * N_NARROW
    pattern = jax.random.randint(key, (devices_all,), 0, 5)
    chosen = jax.random.randint(jax.random.fold_in(key, 1), (), 0, devices_all)
    pattern = jnp.where(jnp.arange(devices_all) == chosen, 0, pattern)
    return patterns[pattern] * quarter


def level_of(rng, dims, split, least, top_value):
    level = 1.0
    for position, blocks in split:
        heights = jax.random.uniform(jax.random.fold_in(jax.random.fold_in(rng, 6), position), (blocks,), jnp.float32, least / len(split), top_value / len(split))
        level = level * jnp.repeat(jnp.exp(heights), dims[position] // blocks).reshape((-1,) + (1,) * (len(dims) - 1 - position))
    return level


def gaussian(key, shape, spread, reach, cuts=(), held_as=jnp.bfloat16):
    values = spread * jax.random.normal(key, shape, jnp.float32)
    if cuts:
        values = values * level_of(key, shape, cuts, -0.22, 0.18)
    return jnp.clip(values, -reach, reach).astype(held_as)


def setup_inputs(seed: int = 0) -> dict:
    key_list = jax.random.split(jax.random.key(seed), 13)
    return {
        "tokens": gaussian(key_list[0], (TOKENS, D), 1.0, 6.0, ((0, 32),)),
        "seq_lengths": draw_seq_lengths(jax.random.fold_in(key_list[12], 71), 0),
        "w_query": gaussian(key_list[2], (D, D), D ** -0.5, 0.21875, ((0, 16),)),
        "w_key": gaussian(key_list[3], (D, D), D ** -0.5, 0.21875, ((0, 16),)),
        "w_value": gaussian(key_list[4], (D, D), D ** -0.5, 0.21875, ((0, 16),)),
        "w_out": gaussian(key_list[5], (D, D), (D // 8) ** -0.5, 0.625, ((0, 16),)),
        "w_gate": gaussian(key_list[6], (D, FF), D ** -0.5, 0.21875, ((0, 16),)),
        "w_up": gaussian(key_list[7], (D, FF), D ** -0.5, 0.21875, ((0, 16),)),
        "w_down": gaussian(key_list[8], (FF, D), (FF // 4) ** -0.5, 0.25, ((0, 16),)),
        "attn_gain": jnp.clip(1.0 + 0.1 * jax.random.normal(key_list[9], (D,), jnp.float32), 0.5, 1.5).astype(jnp.bfloat16),
        "ffn_gain": jnp.clip(1.0 + 0.1 * jax.random.normal(key_list[10], (D,), jnp.float32), 0.5, 1.5).astype(jnp.bfloat16),
        "cotangent": gaussian(key_list[11], (TOKENS, D), 1.0, 6.0, ((0, 32),)),
    }


HIGHEST = lax.Precision.HIGHEST
EPS = 1e-06

@jax.custom_vjp
def low(v):
    return lax.optimization_barrier(v.astype(jnp.bfloat16)).astype(jnp.float32)

@jax.custom_vjp
def low_back(v):
    return v

def low_keep(v):
    return (low(v), None)

def low_pass(kept, grad):
    return (grad,)

def back_keep(v):
    return (v, None)

def back_low(kept, grad):
    return (low(grad),)
low.defvjp(low_keep, low_pass)
low_back.defvjp(back_keep, back_low)

def layout(lengths, tok_count):
    seq_ends = jnp.cumsum(lengths).astype(jnp.int32)
    starts = (seq_ends - lengths).astype(jnp.int32)
    places = jnp.arange(tok_count, dtype=jnp.int32)
    segment = lax.optimization_barrier(jnp.sum((places[:, None] >= seq_ends[None, :]).astype(jnp.int32), axis=1)).astype(jnp.int32)
    slot_ids = jnp.arange(lengths.shape[0], dtype=jnp.int32)
    starts_at = lax.optimization_barrier(jnp.sum(jnp.where(segment[:, None] == slot_ids[None, :], starts[None, :], 0), axis=1)).astype(jnp.int32)
    return (segment, places - starts_at)

def rope_tables(positions, head_dim):
    half_dim = head_dim // 2
    column = jnp.arange(half_dim, dtype=jnp.float32)
    frequency = jnp.exp(column * (-2.0 * math.log(10000.0) / head_dim))
    angles = positions.astype(jnp.float32)[:, None] * frequency[None, :]
    angles = jnp.concatenate([angles, angles], axis=1)
    return (jnp.cos(angles), jnp.sin(angles))

def rotate(values, cosine, sine):
    half_dim = values.shape[-1] // 2
    turned = jnp.concatenate([-values[..., half_dim:], values[..., :half_dim]], axis=-1)
    return values * cosine[:, None, :] + turned * sine[:, None, :]

def norm_gain(values, gain):
    return values * lax.rsqrt(lax.optimization_barrier(jnp.mean(values * values, axis=-1, keepdims=True)) + EPS) * gain

def attend(queries, key_rows, value_rows, segment):
    tok_count = queries.shape[0]
    block_rows = min(512, tok_count)
    scale = HEAD_DIM ** (-0.5)
    row_index = jnp.arange(tok_count, dtype=jnp.int32)

    def one_block(entries):
        query_blk, seg_blk, row_blk = entries
        scores = jnp.einsum('qhd,khd->hqk', query_blk, key_rows, precision=HIGHEST) * scale
        scores = low_back(scores)
        allowed = (seg_blk[:, None] == segment[None, :]) & (row_index[None, :] <= row_blk[:, None])
        scores = jnp.where(allowed[None], scores, -1e+30)
        probs = jax.nn.softmax(scores, axis=-1)
        return jnp.einsum('hqk,khd->qhd', low(probs), value_rows, precision=HIGHEST)
    blocks = tok_count // block_rows
    entries = (queries.reshape(blocks, block_rows, HEADS, HEAD_DIM), segment.reshape(blocks, block_rows), row_index.reshape(blocks, block_rows))
    result = lax.map(jax.checkpoint(one_block), entries)
    return result.reshape(tok_count, HEADS * HEAD_DIM)

def mm(left, right):
    return jnp.dot(left, right, precision=HIGHEST)

def layer(inputs, lengths, w_query, w_key, w_value, w_out, w_gate, w_up, w_down, attn_gain, ffn_gain):
    tok_count = inputs.shape[0]
    segment, positions = layout(lengths, tok_count)
    cosine, sine = rope_tables(positions, HEAD_DIM)
    h_one = low(norm_gain(inputs, attn_gain))
    q_pre = low_back(mm(h_one, w_query)).reshape(tok_count, HEADS, HEAD_DIM)
    k_pre = low_back(mm(h_one, w_key)).reshape(tok_count, HEADS, HEAD_DIM)
    queries = low(rotate(q_pre, cosine, sine))
    key_rows = low(rotate(k_pre, cosine, sine))
    value_rows = low(low_back(mm(h_one, w_value))).reshape(tok_count, HEADS, HEAD_DIM)
    attended = low(low_back(attend(queries, key_rows, value_rows, segment)))
    middle = inputs + low_back(mm(attended, w_out))
    h_two = low(norm_gain(middle, ffn_gain))
    gate = low_back(mm(h_two, w_gate))
    upward = low_back(mm(h_two, w_up))
    hidden = low(jax.nn.silu(gate) * upward)
    return middle + low_back(mm(hidden, w_down))

def reference(tokens, seq_lengths, w_query, w_key, w_value, w_out, w_gate, w_up, w_down, attn_gain, ffn_gain, cotangent):
    weights = tuple((w.astype(jnp.float32) for w in (w_query, w_key, w_value, w_out, w_gate, w_up, w_down, attn_gain, ffn_gain)))
    group = 4
    steps_all = N_WIDE * N_NARROW // group
    inputs_all = tokens.astype(jnp.float32).reshape(steps_all, group, TOK_DEV, D)
    cot_all = cotangent.astype(jnp.float32).reshape(steps_all, group, TOK_DEV, D)
    lens_all = seq_lengths.reshape(steps_all, group, SLOTS)

    def group_step(totals, entries):
        inputs_grp, lens_grp, cot_grp = entries

        def forward(inputs_in, *params):
            return jax.vmap(lambda rows_in, lens_in: layer(rows_in, lens_in, *params))(inputs_in, lens_grp)
        result, backward = jax.vjp(forward, inputs_grp, *weights)
        gradients = backward(cot_grp)
        totals = tuple((a + b for a, b in zip(totals, gradients[1:])))
        return (totals, (result.astype(jnp.bfloat16), gradients[0].astype(jnp.bfloat16)))
    zero_grads = tuple((jnp.zeros_like(w) for w in weights))
    totals, (outputs, grad_rows) = lax.scan(group_step, zero_grads, (inputs_all, lens_all, cot_all))
    return (outputs.reshape(TOKENS, D), grad_rows.reshape(TOKENS, D), totals[0], totals[1], totals[2], totals[3], totals[4], totals[5], totals[6], totals[7], totals[8])
```

```python
import functools
import math

import jax
import jax.numpy as jnp
from jax import lax
from jax.experimental import pallas as pl
from jax.experimental.pallas import tpu as pltpu
from jax.sharding import PartitionSpec as P

HEADS = 12
EPS = 1e-06
NEG = -1e30
BF = jnp.bfloat16
F32 = jnp.float32
MESH = pl.DeviceIdType.MESH
VMEM_BYTES = 60 * 2**20


def nn(left, right):
    return jnp.dot(left, right, preferred_element_type=F32)


def nt(left, right):
    return lax.dot_general(left, right, (((1,), (1,)), ((), ())), preferred_element_type=F32)


def flat(values):
    return values.reshape(-1, values.shape[-1])


def sigmoid(v):
    return 1.0 / (1.0 + jnp.exp(-v))


def three_way(v):
    high = v.astype(BF)
    rest = v - high.astype(F32)
    mid = rest.astype(BF)
    return high, mid, (rest - mid.astype(F32)).astype(BF)


class Place:
    def __init__(self):
        wide = lax.axis_index("wide")
        self.c = lax.axis_index("narrow")
        self.w = wide
        self.z = wide // 4
        self.p = lax.rem(wide, 4)
        across_y = lax.rem(self.p + 2, 4)
        across_x = self.p + 1 - 2 * lax.rem(self.p, 2)
        self.q1 = (1 - self.c) * across_y + self.c * across_x
        self.q2 = (1 - self.c) * across_x + self.c * across_y
        self.q3 = 3 - self.p
        self.first = {"wide": self.z * 4 + self.q1}
        self.second = {"wide": self.z * 4 + self.q2}
        self.other = {"narrow": 1 - self.c}

    def z_at(self, d):
        return lax.rem(self.z + d + 4, 4)

    def z_dev(self, d):
        return {"wide": self.z_at(d) * 4 + self.p}


def enter(place):
    sem = pltpu.get_barrier_semaphore()
    for d in range(1, 16):
        pl.semaphore_signal(sem, inc=1, device_id={"wide": lax.rem(place.w + d, 16)}, device_id_type=MESH)
    pl.semaphore_signal(sem, inc=1, device_id=place.other, device_id_type=MESH)
    pl.semaphore_wait(sem, 16)


def remote(src, dst, send, recv, device):
    return pltpu.make_async_remote_copy(
        src_ref=src, dst_ref=dst, send_sem=send, recv_sem=recv, device_id=device, device_id_type=MESH
    )


def lane_of(rows, lanes=128):
    return lax.broadcasted_iota(jnp.int32, (rows, lanes), 1)


def spread(index):
    row = lax.broadcasted_iota(jnp.int32, (128, 768), 0)
    col = lax.broadcasted_iota(jnp.int32, (128, 768), 1)
    return jnp.where((col == row + 48 * index) & (row < 48), 1.0, 0.0).astype(BF)


class Gather:
    def __init__(self, place, buf, start, width, rows, send, recv):
        self.place = place
        r0, rn = rows

        def part(z, q, core):
            col = pl.ds(pl.multiple_of(start + core * width, 128), width)
            return buf.at[z, q, pl.ds(r0, rn), col]

        def block(q, core):
            col = pl.ds(pl.multiple_of(start + core * width, 128), width)
            return buf.at[:, q, pl.ds(r0, rn), col]

        self.part, self.block, self.send, self.recv = part, block, send, recv

    def copy(self, k, ref, device):
        return remote(ref, ref, self.send.at[k], self.recv.at[k], device)


def block_steps(unit):
    pc = unit.place
    me = pc.c
    zs = [unit.copy(d - 1, unit.part(pc.z, pc.p, me), pc.z_dev(d)) for d in (1, 2, 3)]
    own = unit.block(pc.p, me)
    to_first = unit.copy(3, own, pc.first)
    to_second = unit.copy(4, own, pc.second)
    on_second = unit.copy(5, unit.block(pc.q1, me), pc.second)
    cores = [unit.copy(6 + i, unit.block(q, me), pc.other) for i, q in enumerate((pc.p, pc.q1, pc.q2, pc.q3))]

    def s0():
        for copy in zs:
            copy.start()

    def s1():
        for copy in zs:
            copy.wait_recv()
        to_first.start()
        to_second.start()
        cores[0].start()

    def s2():
        to_first.wait_recv()
        on_second.start()
        cores[1].start()

    def s3():
        to_second.wait_recv()
        cores[2].start()

    def s4():
        on_second.wait_recv()
        cores[3].start()

    def s5():
        for copy in cores:
            copy.wait_recv()
        for copy in [*zs, to_first, to_second, on_second, *cores]:
            copy.wait_send()

    return [s0, s1, s2, s3, s4, s5]


def piece_gather(unit):
    pc = unit.place
    me = pc.c
    planes = (pc.p, pc.q1, pc.q2, pc.q3)
    zs = [unit.copy(d - 1, unit.part(pc.z, pc.p, me), pc.z_dev(d)) for d in (1, 2, 3)]
    first = [unit.copy(3 + d, unit.part(pc.z_at(-d), pc.p, me), pc.first) for d in range(4)]
    second = [unit.copy(7 + d, unit.part(pc.z_at(-d), pc.p, me), pc.second) for d in range(4)]
    onward = [unit.copy(11 + d, unit.part(pc.z_at(-d), pc.q1, me), pc.second) for d in range(4)]
    cores = [[unit.copy(15 + 4 * i + d, unit.part(pc.z_at(-d), q, me), pc.other) for d in range(4)] for i, q in enumerate(planes)]
    for copy in zs:
        copy.start()
    first[0].start()
    second[0].start()
    cores[0][0].start()
    order = (0, 1, 3, 2)
    for n, d in enumerate(order):
        if n:
            zs[d - 1].wait_recv()
            first[d].start()
            second[d].start()
            cores[0][d].start()
        if n:
            before = order[n - 1]
            first[before].wait_recv()
            onward[before].start()
            cores[1][before].start()
            second[before].wait_recv()
            cores[2][before].start()
    last = order[-1]
    first[last].wait_recv()
    onward[last].start()
    cores[1][last].start()
    second[last].wait_recv()
    cores[2][last].start()
    for d in order:
        onward[d].wait_recv()
        cores[3][d].start()
    for line in cores:
        for copy in line:
            copy.wait_recv()
    for copy in [*zs, *first, *second, *onward, *sum(cores, [])]:
        copy.wait_send()


def pair_at(j):
    return lax.rem(j, 2) * 1152 + (j // 2) * 384


def fold(units):
    depth = len(units[0])
    slots = []
    for n in range(len(units) + depth - 1):
        steps = []
        if n < len(units):
            steps.append(units[n][0])
        for s in range(depth - 1, 0, -1):
            if 0 <= n - s < len(units):
                steps.append(units[n - s][s])
        slots.append(steps)
    return slots


def run_all(steps):
    for step in steps:
        step()


def turned(values, lane, back):
    up = pltpu.roll(values, 96, 1)
    down = pltpu.roll(values, 32, 1)
    low = lax.rem(lane, 64) < 32
    return jnp.where(low, up, -down) if back else jnp.where(low, -up, down)


def fore_kernel(
    lens, x_ref, dy_ref, gt_hbm, wq, wk, wv, wo, wg, wu, wd,
    q_out, k_out, v_out, o_out, do_out, h1t_out, lse_out, seg_out, rope_out, w_out, dx2_out, gain_out, gg_out, y_out, gu_sum, d_sum, o_sum,
    w_s, wo_s, wgu_s, wd_s, gain_s, gains, x2_s, y_s, dh2_s, h1t_s, q_s, k_s, v_s, o_s, lse_s, seg_s, rope_s,
    hidt_s, dgu_s, gg_s, yb_s, gu_st, d_st, o_st, gu_r, d_r, o_r,
    wsend, wrecv, usend, urecv, gsend, grecv, rsend, rrecv, lsem, osem,
):
    pc = Place()
    tok = x_ref.shape[0]
    blocks = tok // 256
    loads = []

    def load(src, dst):
        copy = pltpu.make_async_copy(src, dst, lsem.at[len(loads)])
        copy.start()
        loads.append(copy)

    def half(start, width):
        return pl.ds(pl.multiple_of(start + pc.c * width, 128), width)

    load(gt_hbm, gain_s.at[pc.w])
    for m in range(3):
        for n, w in enumerate((wq, wk, wv)):
            load(w.at[:, half(m * 256, 128)], w_s.at[pc.z, pc.p, :, pl.ds(pl.multiple_of(pc.c * 1152 + m * 384 + n * 128, 128), 128)])
    early = len(loads)
    load(wo.at[:, half(0, 384)], wo_s.at[pc.z, pc.p, :, half(0, 384)])
    load(wd.at[:, half(0, 384)], wd_s.at[pc.z, pc.p, :, half(0, 384)])
    for u in range(4):
        for n, w in enumerate((wg, wu)):
            load(w.at[:, half(u * 512, 256)], wgu_s.at[pc.z, pc.p, :, pl.ds(pl.multiple_of(u * 1024 + n * 256 + pc.c * 512, 128), 256)])
    enter(pc)
    for copy in loads[:early]:
        copy.wait()
    gain_copies = [
        remote(gain_s.at[pc.w], gain_s.at[pc.w], gsend.at[d - 1], grecv.at[d - 1], {"wide": lax.rem(pc.w + d, 16)}) for d in range(1, 16)
    ]
    for copy in gain_copies:
        copy.start()
    for copy in loads[early:]:
        copy.wait()
    ends, total = [], jnp.int32(0)
    for s in range(4):
        total = total + lens[0, s]
        ends.append(total)

    def tables(r, carry):
        rs = pl.ds(pl.multiple_of(r * 256, 256), 256)
        lane = lane_of(256)
        place = lax.broadcasted_iota(jnp.int32, (256, 128), 0) + r * 256
        seg = jnp.zeros((256, 128), jnp.int32)
        start = jnp.zeros((256, 128), jnp.int32)
        for s in range(4):
            past = place >= ends[s]
            seg = seg + past.astype(jnp.int32)
            start = jnp.where(past, ends[s], start)
        column = lax.rem(lane, 32).astype(F32)
        angle = (place - start).astype(F32) * jnp.exp(column * (-2.0 * math.log(10000.0) / 64))
        rope_s[0, rs, :] = jnp.cos(angle)
        rope_s[1, rs, :] = jnp.sin(angle)
        seg_s[0, rs, :] = jnp.where((lane == seg) | (lane >= 4), 0.0, NEG).astype(BF)
        seg_s[1, rs, :] = jnp.where((lane == seg) | ((lane >= 4) & (lane < 7)), 1.0, 0.0).astype(BF)
        return carry

    unit_qkv = Gather(pc, w_s, 0, 1152, (0, 48), wsend, wrecv)
    lax.fori_loop(0, blocks, tables, 0)
    piece_gather(unit_qkv)
    for copy in gain_copies:
        copy.wait_recv()

    def gain_rows(w, rows):
        return rows + nn(gain_s[w], spread(w))

    gains[...] = lax.fori_loop(0, 16, gain_rows, jnp.zeros((16, 768), F32))
    units = [
        Gather(pc, wo_s, 0, 384, (0, 48), usend.at[0], urecv.at[0]),
        Gather(pc, wd_s, 0, 384, (0, 64), usend.at[1], urecv.at[1]),
        Gather(pc, wd_s, 0, 384, (64, 64), usend.at[2], urecv.at[2]),
    ] + [Gather(pc, wgu_s, 1024 * u, 512, (0, 48), usend.at[3 + u], urecv.at[3 + u]) for u in range(4)]
    slots = fold([block_steps(u) for u in units])
    outs = []

    def store(src, dst):
        copy = pltpu.make_async_copy(src, dst, osem.at[len(outs)])
        copy.start()
        outs.append(copy)
        return copy

    run_all(slots[0])
    store(gains, gain_out)
    w_copy = store(w_s, w_out)
    store(seg_s, seg_out)
    store(rope_s, rope_out)

    def project(r, carry):
        rs = pl.ds(pl.multiple_of(r * 256, 256), 256)
        lane = lane_of(256)
        x = x_ref[rs, :].astype(F32)
        h1 = (x * lax.rsqrt(jnp.mean(x * x, axis=1, keepdims=True) + EPS) * gains[0:1, :]).astype(BF)
        h1t_s[:, rs] = h1.T
        cos, sin = rope_s[0, rs, :], rope_s[1, rs, :]
        for half in range(2):
            pre = nn(h1, flat(w_s[:, :, :, half * 1152 : (half + 1) * 1152]))
            for m in range(3):
                cs = pl.ds((2 * m + half) * 128, 128)
                qp, kp, vp = (pre[:, m * 384 + n * 128 : m * 384 + (n + 1) * 128] for n in range(3))
                q_s[rs, cs] = ((qp * cos + turned(qp, lane, False) * sin).astype(BF).astype(F32) * 0.125).astype(BF)
                k_s[rs, cs] = (kp * cos + turned(kp, lane, False) * sin).astype(BF)
                v_s[rs, cs] = vp.astype(BF)
        return carry

    lax.fori_loop(0, blocks, project, 0)
    kept = [store(q_s, q_out), store(k_s, k_out), store(v_s, v_out), store(h1t_s, h1t_out)]
    run_all(slots[1])

    def pair(j, carry):
        for t in range(6):
            pl.when(j == t)(functools.partial(run_all, slots[2 + t]))
        cs = pl.ds(pl.multiple_of(j * 128, 128), 128)
        lane = lane_of(256)
        below = lax.broadcasted_iota(jnp.int32, (256, 256), 0) >= lax.broadcasted_iota(jnp.int32, (256, 256), 1)
        for i in range(blocks):
            rs, before = pl.ds(i * 256, 256), pl.ds(0, i * 256)
            qt = q_s[rs, cs]
            parts = []
            for h in range(2):
                qm = jnp.where((lane < 64) == (h == 0), qt, BF(0))
                qm = jnp.concatenate([qm, seg_s[0, rs, :]], axis=1)
                sd = jnp.where(below, nt(qm, jnp.concatenate([k_s[rs, cs], seg_s[1, rs, :]], axis=1)), NEG)
                top = jnp.max(sd, axis=1, keepdims=True)
                if i:
                    so = nt(qm, jnp.concatenate([k_s[before, cs], seg_s[1, before, :]], axis=1))
                    top = jnp.maximum(top, jnp.max(so, axis=1, keepdims=True))
                pd = jnp.exp(sd - top)
                mass = jnp.sum(pd, axis=1, keepdims=True)
                acc = nn(pd.astype(BF), v_s[rs, cs])
                if i:
                    po = jnp.exp(so - top)
                    mass = mass + jnp.sum(po, axis=1, keepdims=True)
                    acc = acc + nn(po.astype(BF), v_s[before, cs])
                parts.append(acc * (1.0 / mass))
                lse_s[rs, :] = jnp.where(lane == 2 * j + h, top + jnp.log(mass), lse_s[rs, :])
            o_s[rs, cs] = jnp.where(lane < 64, parts[0], parts[1]).astype(BF)
        return carry

    lse_s[...] = jnp.zeros_like(lse_s)
    lax.fori_loop(0, 6, pair, 0)
    store(o_s, o_out)
    store(lse_s, lse_out)
    for copy in kept:
        copy.wait()
    h2_s, h2t_s, dxb_s, do_s = q_s, h1t_s, k_s, v_s
    gain2 = gains[1:2, :]

    def middle(r, carry):
        rs = pl.ds(pl.multiple_of(r * 256, 256), 256)
        x2 = x_ref[rs, :].astype(F32) + nn(o_s[rs, :], flat(wo_s[...]))
        x2_s[rs, :] = x2
        h2 = (x2 * lax.rsqrt(jnp.mean(x2 * x2, axis=1, keepdims=True) + EPS) * gain2).astype(BF)
        h2_s[rs, :] = h2
        h2t_s[:, rs] = h2.T
        return carry

    lax.fori_loop(0, blocks, middle, 0)

    def swap(buf, width, got, k):
        far = pl.ds(pl.multiple_of((1 - pc.c) * width, 128), width)
        return remote(buf.at[..., far], got, rsend.at[k], rrecv.at[k], pc.other)

    def near(buf, width):
        return buf[..., pl.ds(pl.multiple_of(pc.c * width, 128), width)]

    gu_swap = [swap(gu_st.at[u % 2], 512, gu_r.at[u], u) for u in range(4)]
    d_swap = [swap(d_st.at[u % 2], 384, d_r.at[u], 4 + u) for u in range(4)]

    def settle(u):
        gu_swap[u].wait_recv()
        d_swap[u].wait_recv()
        for z in range(4):
            mine = gu_st[u % 2, z, :, :, pl.ds(pl.multiple_of(pc.c * 512, 128), 512)]
            gu_r[u, z] = (gu_r[u, z].astype(F32) + mine.astype(F32)).astype(BF)
        mine = d_st[u % 2, :, :, pl.ds(pl.multiple_of(pc.c * 384, 128), 384)]
        d_r[u] = (d_r[u].astype(F32) + mine.astype(F32)).astype(BF)
        store(gu_r.at[u], gu_sum.at[u])
        store(d_r.at[u], d_sum.at[u])
        gu_swap[u].wait_send()
        d_swap[u].wait_send()

    for u in range(4):
        run_all(slots[8 + u])
        wgu = pl.ds(u * 1024, 1024)

        def mix(r, carry):
            rs = pl.ds(pl.multiple_of(r * 256, 256), 256)
            both = nn(h2_s[rs, :], flat(wgu_s[:, :, :, wgu]))
            dhid = nt(dy_ref[rs, :], flat(wd_s[u]))
            hids, grads = [], []
            for n in range(2):
                gate, up = both[:, n * 512 : n * 512 + 256], both[:, n * 512 + 256 : n * 512 + 512]
                dh = dhid[:, n * 256 : n * 256 + 256]
                sig = sigmoid(gate)
                silu = gate * sig
                hids.append((silu * up).astype(BF))
                grads.append((dh * up * sig * (1.0 + gate * (1.0 - sig))).astype(BF))
                grads.append((dh * silu).astype(BF))
            hid = jnp.concatenate(hids, axis=1)
            dgu = jnp.concatenate(grads, axis=1)
            hidt_s[:, rs] = hid.T
            dgu_s[rs, :] = dgu
            yv = nn(hid, flat(wd_s[u]))
            dv = nt(dgu, flat(wgu_s[:, :, :, wgu]))
            if u == 0:
                y_s[rs, :] = x2_s[rs, :] + yv
                dh2_s[rs, :] = dv
            else:
                y_s[rs, :] += yv
                dh2_s[rs, :] += dv
            return carry

        lax.fori_loop(0, blocks, mix, 0)
        if u >= 2:
            settle(u - 2)

        def weight_gu(z, carry):
            rows = nn(h2t_s[pl.ds(pl.multiple_of(z * 192, 64), 192), :], dgu_s[...])
            gu_st[u % 2, z] = rows.astype(BF).reshape(4, 48, 1024)
            return carry

        lax.fori_loop(0, 4, weight_gu, 0)

        def weight_d(k, carry):
            rows = nn(hidt_s[pl.ds(pl.multiple_of(k * 256, 256), 256), :], dy_ref[...])
            d_st[u % 2, pl.ds(k * 2, 2)] = rows.astype(BF).reshape(2, 128, 768)
            return carry

        lax.fori_loop(0, 2, weight_d, 0)
        gu_swap[u].start()
        d_swap[u].start()

    gg_s[...] = jnp.zeros_like(gg_s)

    def back(r, carry):
        rs = pl.ds(pl.multiple_of(r * 256, 256), 256)
        yb_s[rs, :] = y_s[rs, :].astype(BF)
        x2, dh2 = x2_s[rs, :], dh2_s[rs, :]
        r2 = lax.rsqrt(jnp.mean(x2 * x2, axis=1, keepdims=True) + EPS)
        n2 = x2 * r2
        e2 = dh2 * gain2
        gg_s[0:1, :] += jnp.sum(dh2 * n2, axis=0, keepdims=True)
        dx2 = dy_ref[rs, :].astype(F32) + r2 * (e2 - n2 * jnp.mean(e2 * n2, axis=1, keepdims=True))
        x2_s[rs, :] = dx2
        dxb = dx2.astype(BF)
        dxb_s[rs, :] = dxb
        do_s[rs, :] = nt(dxb, flat(wo_s[...])).astype(BF)
        h2t_s[:, rs] = o_s[rs, :].T
        return carry

    lax.fori_loop(0, blocks, back, 0)
    store(yb_s, y_out)
    store(x2_s, dx2_out)
    store(do_s, do_out)
    store(gg_s, gg_out)
    settle(2)

    def weight_o(z, carry):
        rows = nn(h2t_s[pl.ds(pl.multiple_of(z * 192, 64), 192), :], dxb_s[...])
        o_st[z] = rows.astype(BF).reshape(4, 48, 768)
        return carry

    lax.fori_loop(0, 4, weight_o, 0)
    o_swap = swap(o_st, 384, o_r, 8)
    o_swap.start()
    settle(3)
    o_swap.wait_recv()
    mine = o_st[:, :, :, pl.ds(pl.multiple_of(pc.c * 384, 128), 384)]
    o_r[...] = (o_r[...].astype(F32) + mine.astype(F32)).astype(BF)
    store(o_r, o_sum)
    o_swap.wait_send()
    for copy in gain_copies:
        copy.wait_send()
    for copy in outs:
        if not any(copy is done for done in kept):
            copy.wait()


class Reduce:
    def __init__(self, place, keep, r1, r2, r3, total, other_total, send, recv, far1, far2, near):
        pc = place
        self.pc, self.keep, self.r1, self.r2, self.r3, self.total = pc, keep, r1, r2, r3, total
        self.to_first = [remote(ref, r1.at[:, i], send.at[i], recv.at[i], pc.first) for i, ref in enumerate((far1, far2))]
        self.near = near
        self.to_second = remote(keep.at[:, 1], r2, send.at[2], recv.at[2], pc.second)
        self.zs = [remote(keep.at[pc.z_at(d), 0], r3.at[d - 1], send.at[2 + d], recv.at[2 + d], pc.z_dev(d)) for d in (1, 2, 3)]
        self.to_core = remote(total, other_total, send.at[6], recv.at[6], pc.other)

    def steps(self, begin, finish):
        pc = self.pc

        def r1():
            begin()
            for copy in self.to_first:
                copy.start()

        def r2():
            for copy in self.near:
                copy.wait()
            for copy in self.to_first:
                copy.wait_recv()

            def add(z, carry):
                self.keep[z] = (self.keep[z].astype(F32) + self.r1[z].astype(F32)).astype(BF)
                return carry

            lax.fori_loop(0, 4, add, 0)
            self.to_second.start()

        def r3():
            self.to_second.wait_recv()

            def add(z, carry):
                self.keep[z, 0] = (self.keep[z, 0].astype(F32) + self.r2[z].astype(F32)).astype(BF)
                return carry

            lax.fori_loop(0, 4, add, 0)
            for copy in self.zs:
                copy.start()

        def r4():
            for copy in self.zs:
                copy.wait_recv()
            total = self.keep[pc.z, 0].astype(F32)
            for d in range(3):
                total = total + self.r3[d].astype(F32)
            self.total[...] = total
            self.to_core.start()

        def r5():
            self.to_core.wait()
            finish()
            for copy in [*self.to_first, self.to_second, *self.zs]:
                copy.wait_send()

        return [r1, r2, r3, r4, r5]


def hind_kernel(
    q_hbm, k_hbm, v_hbm, o_hbm, do_hbm, lse_hbm, seg_hbm, rope_hbm, h1t_hbm, w_hbm, x_hbm, dx2_hbm, gain_ref, gg_ref, gu_sum, d_sum, o_sum,
    gx_ref, gwq, gwk, gwv, gwo, gwg, gwu, gwd, gg_out,
    q_s, k_s, v_s, o_s, do_s, lse_s, seg_s, rope_s, h1t_s, w_s, x_s, dx2_s, dqkv_s, dk_s, dv_s,
    gq_s, gq_r, gu_k, gu_1, gu_2, gu_3, gu_t, d_k, d_1, d_2, d_3, d_t, o_k, o_1, o_2, o_3, o_t, qk_k, qk_1, qk_2, qk_3, qk_t,
    gg1_s, gg_st, gg_r, gg_c,
    lsem, nsem, ssend, srecv, qsend, qrecv, gsend, grecv,
):
    pc = Place()
    tok = x_s.shape[0]
    blocks = tok // 256
    loads = []

    def load(src, dst):
        copy = pltpu.make_async_copy(src, dst, lsem.at[len(loads)])
        copy.start()
        loads.append(copy)
        return copy

    for src, dst in ((q_hbm, q_s), (k_hbm, k_s), (v_hbm, v_s), (o_hbm, o_s), (do_hbm, do_s), (lse_hbm, lse_s), (seg_hbm, seg_s), (rope_hbm, rope_s)):
        load(src, dst)
    early = len(loads)
    for src, dst in ((h1t_hbm, h1t_s), (w_hbm, w_s), (x_hbm, x_s), (dx2_hbm, dx2_s)):
        load(src, dst)
    enter(pc)

    nears = []

    def start_near(copies):
        for copy in copies:
            copy.start()

    def unit(n, parts, keep, r1, r2, r3, total, finish, source=None):
        near = []
        if source is None:
            near = [pltpu.make_async_copy(parts(q), keep.at[:, i], nsem.at[n, i]) for i, q in enumerate((pc.p, pc.q2))]
        red = Reduce(pc, keep, r1, r2, r3, total.at[0], total.at[1], ssend.at[n], srecv.at[n], parts(pc.q1), parts(pc.q3), near)

        def begin():
            if source is not None:
                source()
            start_near(near)

        return red.steps(begin, finish)

    def halves(ref):
        mine, others = ref[0], ref[1]
        zero = pc.c == 0
        return jnp.where(zero, mine, others), jnp.where(zero, others, mine)

    units = []
    for u in range(4):

        def finish_gu(u=u):
            low, high = halves(gu_t.at[u])
            for n, part in enumerate((low, high)):
                gwg[:, pl.ds(u * 512 + n * 256, 256)] = part[:, :256]
                gwu[:, pl.ds(u * 512 + n * 256, 256)] = part[:, 256:]

        units.append(unit(u, lambda q, u=u: gu_sum.at[u, :, q], gu_k.at[u], gu_1.at[u], gu_2.at[u], gu_3.at[u], gu_t.at[u], finish_gu))

    def finish_o():
        low, high = halves(o_t)
        gwo[:, 0:384] = low
        gwo[:, 384:768] = high

    units.append(unit(4, lambda q: o_sum.at[:, q], o_k, o_1, o_2, o_3, o_t, finish_o))

    def finish_d():
        low, high = halves(d_t)
        gwd[:, 0:384] = low
        gwd[:, 384:768] = high

    units.append(unit(5, lambda q: d_sum.at[:, q], d_k, d_1, d_2, d_3, d_t, finish_d))

    q_swaps = [remote(gq_s.at[2 * m + 1 - pc.c], gq_r.at[m], qsend.at[m], qrecv.at[m], pc.other) for m in range(3)]

    for m in range(3):

        def finish_q(m=m):
            low, high = halves(qk_t.at[m])
            for n, part in enumerate((low, high)):
                cs = pl.ds((2 * m + n) * 128, 128)
                gwq[:, cs] = part[:, 0:128]
                gwk[:, cs] = part[:, 128:256]
                gwv[:, cs] = part[:, 256:384]

        def source(m=m):
            q_swaps[m].wait_recv()
            mine = 2 * m + pc.c

            def add(z, carry):
                got = gq_r[m, z]
                gq_r[m, z] = (got.astype(F32) + gq_s[mine, z].astype(F32)).astype(BF)
                return carry

            lax.fori_loop(0, 4, add, 0)
            for i, q in enumerate((pc.p, pc.q2)):
                qk_k[m, :, i] = gq_r[m, :, q]
            q_swaps[m].wait_send()

        units.append(unit(6 + m, lambda q, m=m: gq_r.at[m, :, q], qk_k.at[m], qk_1.at[m], qk_2.at[m], qk_3.at[m], qk_t.at[m], finish_q, source))
    slots = fold(units)
    ticks = {0: 0, 1: 1, 3: 2, 4: 3, 6: 4, 7: 5, 9: 6, 11: 7}

    run_all(slots[0])
    for copy in loads[:early]:
        copy.wait()
    ones = (lane_of(tok) < 3).astype(BF)

    def pair(j, carry):
        cs = pl.ds(pl.multiple_of(j * 128, 128), 128)
        lane = lane_of(256)
        above = lax.broadcasted_iota(jnp.int32, (256, 256), 0) <= lax.broadcasted_iota(jnp.int32, (256, 256), 1)
        at = pair_at(j)
        dk_s[...] = jnp.zeros_like(dk_s)
        dv_s[...] = jnp.zeros_like(dv_s)
        vaug = jnp.concatenate([v_s[:, cs], ones], axis=1)
        kaug = jnp.concatenate([k_s[:, cs], seg_s[1]], axis=1)
        kt = k_s[:, cs].T
        for i in range(blocks):
            if i in (1, 3):
                for tick, slot in ticks.items():
                    if slot and tick % 2 == i // 2:
                        pl.when(j == tick // 2)(functools.partial(run_all, slots[slot]))
            rs, first, last = pl.ds(i * 256, 256), i * 256, (i + 1) * 256
            qt, dt = q_s[rs, cs], do_s[rs, cs]
            prod = dt.astype(F32) * o_s[rs, cs].astype(F32)
            parts = []
            for h in range(2):
                mask = (lane < 64) == (h == 0)
                qm, dm = jnp.where(mask, qt, BF(0)), jnp.where(mask, dt, BF(0))
                delta = jnp.sum(jnp.where(mask, prod, 0.0), axis=1, keepdims=True)
                lse = jnp.sum(jnp.where(lane == 2 * j + h, lse_s[rs, :], 0.0), axis=1, keepdims=True)
                a0, a1, a2 = three_way(-lse)
                qa = jnp.where(lane == 4, a0, jnp.where(lane == 5, a1, jnp.where(lane == 6, a2, seg_s[0, rs, :])))
                b0, b1, b2 = three_way(-delta)
                da = jnp.where(lane == 0, b0, jnp.where(lane == 1, b1, jnp.where(lane == 2, b2, BF(0))))
                qaug, daug = jnp.concatenate([qm, qa], axis=1), jnp.concatenate([dm, da], axis=1)
                pd = jnp.exp(jnp.where(above, nt(kaug[first:last], qaug), NEG))
                dsd = (pd * nt(vaug[first:last], daug)).astype(BF)
                dv_s[rs, :] += nn(pd.astype(BF), dm)
                dk_s[rs, :] += nn(dsd, qm)
                dq = nn(kt[h * 64 : h * 64 + 64, first:last], dsd)
                if i:
                    before = pl.ds(0, first)
                    po = jnp.exp(nt(kaug[:first], qaug))
                    dso = (po * nt(vaug[:first], daug)).astype(BF)
                    dv_s[before, :] += nn(po.astype(BF), dm)
                    dk_s[before, :] += nn(dso, qm)
                    dq = dq + nn(kt[h * 64 : h * 64 + 64, :first], dso)
                parts.append(dq)
            dq = jnp.concatenate(parts, axis=0).T * 0.125
            dq = dq * rope_s[0, rs, :] + turned(dq * rope_s[1, rs, :], lane, True)
            dqkv_s[rs, pl.ds(pl.multiple_of(at, 128), 128)] = dq.astype(BF)

        def finish(r, carry):
            rs = pl.ds(pl.multiple_of(r * 256, 256), 256)
            dk = dk_s[rs, :]
            dk = dk * rope_s[0, rs, :] + turned(dk * rope_s[1, rs, :], lane, True)
            dqkv_s[rs, pl.ds(pl.multiple_of(at + 128, 128), 128)] = dk.astype(BF)
            dqkv_s[rs, pl.ds(pl.multiple_of(at + 256, 128), 128)] = dv_s[rs, :].astype(BF)
            return carry

        lax.fori_loop(0, blocks, finish, 0)
        pl.when(j == 0)(loads[early].wait)

        def weight(z, carry):
            rows = nn(h1t_s[pl.ds(pl.multiple_of(z * 192, 64), 192), :], dqkv_s[:, pl.ds(pl.multiple_of(at, 128), 384)])
            gq_s[j, z] = rows.astype(BF).reshape(4, 48, 384)
            return carry

        lax.fori_loop(0, 4, weight, 0)
        for m in range(3):
            pl.when((j // 2 == m) & (lax.rem(j, 2) != pc.c))(q_swaps[m].start)
        return carry

    lax.fori_loop(0, 6, pair, 0)
    run_all(slots[8])
    for copy in loads[early + 1 :]:
        copy.wait()
    gg1_s[...] = jnp.zeros_like(gg1_s)
    gain1 = gain_ref[0:1, :]

    def last(r, carry):
        rs = pl.ds(pl.multiple_of(r * 256, 256), 256)
        dh1 = nt(dqkv_s[rs, :], flat(w_s[...]))
        x = x_s[rs, :].astype(F32)
        r1 = lax.rsqrt(jnp.mean(x * x, axis=1, keepdims=True) + EPS)
        n1 = x * r1
        e1 = dh1 * gain1
        gg1_s[0:1, :] += jnp.sum(dh1 * n1, axis=0, keepdims=True)
        gx_ref[rs, :] = (dx2_s[rs, :] + r1 * (e1 - n1 * jnp.mean(e1 * n1, axis=1, keepdims=True))).astype(BF)
        for t in range(4):
            pl.when(r == t)(functools.partial(run_all, slots[9 + t]))
        return carry

    lax.fori_loop(0, blocks, last, 0)
    row = lax.broadcasted_iota(jnp.int32, (16, 768), 0)
    terms = jnp.zeros((16, 768), BF)
    for n, sums in enumerate((gg1_s, gg_ref)):
        for k, term in enumerate(three_way(sums[0:1, :])):
            terms = jnp.where(row == 8 * n + k, term, terms)

    def cut(w, carry):
        gg_st[w] = nt(terms, spread(w))
        return carry

    lax.fori_loop(0, 16, cut, 0)
    copies = []
    for d in range(1, 16):
        to = lax.rem(pc.w + d, 16)
        copy = remote(gg_st.at[to], gg_r.at[d - 1], gsend.at[d - 1], grecv.at[d - 1], {"wide": to})
        copy.start()
        copies.append(copy)
    total = gg_st[pc.w]
    for d in range(1, 16):
        copies[d - 1].wait_recv()
        total = total + gg_r[d - 1]
    gg_c[0] = total
    to_core = remote(gg_c.at[0], gg_c.at[1], gsend.at[15], grecv.at[15], pc.other)
    to_core.start()
    to_core.wait()
    gg_out[...] = gg_c[0] + gg_c[1]
    for copy in copies:
        copy.wait_send()


def shape(dims, dtype=BF):
    return jax.ShapeDtypeStruct(dims, dtype)


def fast_body(tokens, seq_lengths, w_query, w_key, w_value, w_out, w_gate, w_up, w_down, attn_gain, ffn_gain, cotangent):
    tok, width = tokens.shape
    any_spec, vmem_spec = pl.BlockSpec(memory_space=pl.ANY), pl.BlockSpec(memory_space=pltpu.VMEM)
    dma = pltpu.SemaphoreType.DMA
    vm = pltpu.VMEM
    tile = jnp.pad(jnp.stack([attn_gain, ffn_gain]), ((0, 14), (0, 128 - attn_gain.shape[0])))
    fore = pl.pallas_call(
        fore_kernel,
        out_shape=[
            shape((tok, width)), shape((tok, width)), shape((tok, width)), shape((tok, width)), shape((tok, width)),
            shape((width, tok)), shape((tok, 128), F32), shape((2, tok, 128)), shape((2, tok, 128), F32),
            shape((4, 4, 48, 2304)), shape((tok, width), F32), shape((16, width), F32), shape((8, width), F32), shape((tok, width)),
            shape((4, 4, 4, 48, 512)), shape((4, 4, 128, 384)), shape((4, 4, 48, 384)),
        ],
        in_specs=[pl.BlockSpec(memory_space=pltpu.SMEM), vmem_spec, vmem_spec] + [any_spec] * 8,
        out_specs=[any_spec] * 17,
        scratch_shapes=[
            vm((4, 4, 48, 2304), BF), vm((4, 4, 48, 768), BF), vm((4, 4, 48, 4096), BF), vm((4, 4, 128, 768), BF), vm((16, 16, 128), BF), vm((16, width), F32),
            vm((tok, width), F32), vm((tok, width), F32), vm((tok, width), F32), vm((width, tok), BF),
            vm((tok, width), BF), vm((tok, width), BF), vm((tok, width), BF), vm((tok, width), BF),
            vm((tok, 128), F32), vm((2, tok, 128), BF), vm((2, tok, 128), F32),
            vm((512, tok), BF), vm((tok, 1024), BF), vm((8, width), F32), vm((tok, width), BF),
            vm((2, 4, 4, 48, 1024), BF), vm((2, 4, 128, 768), BF), vm((4, 4, 48, 768), BF),
            vm((4, 4, 4, 48, 512), BF), vm((4, 4, 128, 384), BF), vm((4, 4, 48, 384), BF),
            dma((31,)), dma((31,)), dma((7, 10)), dma((7, 10)), dma((15,)), dma((15,)), dma((9,)), dma((9,)), dma((20,)), dma((24,)),
        ],
        compiler_params=pltpu.CompilerParams(collective_id=0, has_side_effects=True, vmem_limit_bytes=VMEM_BYTES),
        name="fore",
    )
    (q, k, v, o, do, h1t, lse, seg, rope, wqkv, dx2, gains, gg2, output, gu_sum, d_sum, o_sum) = fore(
        seq_lengths, tokens, cotangent, tile, w_query, w_key, w_value, w_out, w_gate, w_up, w_down
    )
    hind = pl.pallas_call(
        hind_kernel,
        out_shape=[shape((tok, width))] + [shape((48, width), F32)] * 4 + [shape((48, 2048), F32)] * 2 + [shape((128, width), F32), shape((16, 128), F32)],
        in_specs=[any_spec] * 12 + [vmem_spec] * 2 + [any_spec] * 3,
        out_specs=[vmem_spec] * 9,
        scratch_shapes=[
            vm((tok, width), BF), vm((tok, width), BF), vm((tok, width), BF), vm((tok, width), BF), vm((tok, width), BF),
            vm((tok, 128), F32), vm((2, tok, 128), BF), vm((2, tok, 128), F32), vm((width, tok), BF), vm((4, 4, 48, 2304), BF),
            vm((tok, width), BF), vm((tok, width), F32), vm((tok, 2304), BF), vm((tok, 128), F32), vm((tok, 128), F32),
            vm((6, 4, 4, 48, 384), BF), vm((3, 4, 4, 48, 384), BF),
            vm((4, 4, 2, 48, 512), BF), vm((4, 4, 2, 48, 512), BF), vm((4, 4, 48, 512), BF), vm((4, 3, 48, 512), BF), vm((4, 2, 48, 512), F32),
            vm((4, 2, 128, 384), BF), vm((4, 2, 128, 384), BF), vm((4, 128, 384), BF), vm((3, 128, 384), BF), vm((2, 128, 384), F32),
            vm((4, 2, 48, 384), BF), vm((4, 2, 48, 384), BF), vm((4, 48, 384), BF), vm((3, 48, 384), BF), vm((2, 48, 384), F32),
            vm((3, 4, 2, 48, 384), BF), vm((3, 4, 2, 48, 384), BF), vm((3, 4, 48, 384), BF), vm((3, 3, 48, 384), BF), vm((3, 2, 48, 384), F32),
            vm((8, width), F32), vm((16, 16, 128), F32), vm((15, 16, 128), F32), vm((2, 16, 128), F32),
            dma((12,)), dma((6, 2)), dma((9, 7)), dma((9, 7)), dma((3,)), dma((3,)), dma((16,)), dma((16,)),
        ],
        compiler_params=pltpu.CompilerParams(collective_id=1, has_side_effects=True, vmem_limit_bytes=VMEM_BYTES),
        name="hind",
    )
    gx, gwq, gwk, gwv, gwo, gwg, gwu, gwd, gg = hind(q, k, v, o, do, lse, seg, rope, h1t, wqkv, tokens, dx2, gains, gg2, gu_sum, d_sum, o_sum)
    count = attn_gain.shape[0]
    return (output, gx, gwq, gwk, gwv, gwo, gwg, gwu, gwd, gg[0:3, :count].sum(axis=0), gg[8:11, :count].sum(axis=0))


def layout(lengths, tok_count):
    slots = jnp.arange(lengths.shape[0])
    seq_ends = jnp.sum(jnp.where(slots[:, None] <= slots[None, :], lengths[:, None], 0), axis=0)
    starts = seq_ends - lengths
    places = jnp.arange(tok_count, dtype=jnp.int32)
    segment = jnp.sum((places[:, None] >= seq_ends[None, :]).astype(jnp.int32), axis=1)
    slot_ids = jnp.arange(lengths.shape[0], dtype=jnp.int32)
    starts_at = jnp.sum(
        jnp.where(segment[:, None] == slot_ids[None, :], starts[None, :], 0), axis=1
    )
    return (segment, places - starts_at)


def rope_tables(positions, head_dim):
    half_dim = head_dim // 2
    column = jnp.arange(half_dim, dtype=jnp.float32)
    frequency = jnp.exp(column * (-2.0 * math.log(10000.0) / head_dim))
    angles = positions.astype(jnp.float32)[:, None] * frequency[None, :]
    angles = jnp.concatenate([angles, angles], axis=1)
    return (jnp.cos(angles), jnp.sin(angles))


def rotate(values, cosine, sine):
    half_dim = values.shape[-1] // 2
    turned = jnp.concatenate([-values[..., half_dim:], values[..., :half_dim]], axis=-1)
    return values * cosine[:, None, :] + turned * sine[:, None, :]


def norm_gain(values, gain):
    return values * lax.rsqrt(jnp.mean(values * values, axis=-1, keepdims=True) + EPS) * gain


def swiglu(gate, upward):
    return jax.nn.silu(gate) * upward


def outer_sum(left, right):
    return lax.dot_general(
        left, right, (((0,), (0,)), ((), ())), preferred_element_type=jnp.float32
    )


def back_dot(rows_in, weight):
    return lax.dot_general(
        rows_in, weight, (((1,), (1,)), ((), ())), preferred_element_type=jnp.float32
    )


def block_scores(query_blk, key_rows, segment, row_index, row_start, scale):
    blk_rows = query_blk.shape[0]
    scores = (
        jnp.einsum("qhd,khd->hqk", query_blk, key_rows, preferred_element_type=jnp.float32) * scale
    )
    seg_blk = segment[row_start : row_start + blk_rows]
    row_blk = row_index[row_start : row_start + blk_rows]
    allowed = (seg_blk[:, None] == segment[None, :]) & (row_index[None, :] <= row_blk[:, None])
    return jnp.where(allowed[None], scores, -1e30)


def attend_forward(queries, key_rows, value_rows, segment):
    tok_count, head_count, head_dim = queries.shape
    scale = head_dim ** (-0.5)
    block_rows = min(512, tok_count)
    row_index = jnp.arange(tok_count, dtype=jnp.int32)
    outputs, totals = ([], [])
    for row_start in range(0, tok_count, block_rows):
        query_blk = queries[row_start : row_start + block_rows]
        scores = block_scores(query_blk, key_rows, segment, row_index, row_start, scale)
        peak = jnp.max(scores, axis=-1, keepdims=True)
        expd = jnp.exp(scores - peak)
        row_mass = jnp.sum(expd, axis=-1, keepdims=True)
        probs_low = (expd / row_mass).astype(jnp.bfloat16)
        outputs.append(
            jnp.einsum("hqk,khd->qhd", probs_low, value_rows, preferred_element_type=jnp.float32)
        )
        totals.append(peak[..., 0] + jnp.log(row_mass[..., 0]))
    return (jnp.concatenate(outputs, axis=0), jnp.concatenate(totals, axis=1))


def attend_backward(queries, key_rows, value_rows, log_total, grad_rows, segment):
    tok_count, head_count, head_dim = queries.shape
    scale = head_dim ** (-0.5)
    block_rows = min(512, tok_count)
    row_index = jnp.arange(tok_count, dtype=jnp.int32)
    grad_keys = jnp.zeros((tok_count, head_count, head_dim), jnp.float32)
    grad_values = jnp.zeros((tok_count, head_count, head_dim), jnp.float32)
    grad_queries = []
    for row_start in range(0, tok_count, block_rows):
        query_blk = queries[row_start : row_start + block_rows]
        grad_blk = grad_rows[row_start : row_start + block_rows]
        scores = block_scores(query_blk, key_rows, segment, row_index, row_start, scale)
        probs = jnp.exp(scores - log_total[:, row_start : row_start + block_rows, None])
        probs_low = probs.astype(jnp.bfloat16)
        grad_probs = jnp.einsum(
            "qhd,khd->hqk", grad_blk, value_rows, preferred_element_type=jnp.float32
        )
        inner = jnp.sum(probs * grad_probs, axis=-1, keepdims=True)
        grad_scores = (probs * (grad_probs - inner)).astype(jnp.bfloat16)
        grad_queries.append(
            jnp.einsum("hqk,khd->qhd", grad_scores, key_rows, preferred_element_type=jnp.float32)
            * scale
        )
        grad_keys = (
            grad_keys
            + jnp.einsum("hqk,qhd->khd", grad_scores, query_blk, preferred_element_type=jnp.float32)
            * scale
        )
        grad_values = grad_values + jnp.einsum(
            "hqk,qhd->khd", probs_low, grad_blk, preferred_element_type=jnp.float32
        )
    return (jnp.concatenate(grad_queries, axis=0), grad_keys, grad_values)


def plain_body(
    tokens,
    seq_lengths,
    w_query,
    w_key,
    w_value,
    w_out,
    w_gate,
    w_up,
    w_down,
    attn_gain,
    ffn_gain,
    cotangent,
):
    gathered = (
        lax.all_gather(w_query, "wide", axis=0, tiled=True),
        lax.all_gather(w_key, "wide", axis=0, tiled=True),
        lax.all_gather(w_value, "wide", axis=0, tiled=True),
        lax.all_gather(w_out, "wide", axis=0, tiled=True),
        lax.all_gather(w_gate, "wide", axis=0, tiled=True),
        lax.all_gather(w_up, "wide", axis=0, tiled=True),
        lax.all_gather(w_down, "wide", axis=0, tiled=True),
        lax.all_gather(attn_gain, "wide", axis=0, tiled=True),
        lax.all_gather(ffn_gain, "wide", axis=0, tiled=True),
    )
    (
        full_query,
        full_key,
        full_value,
        full_out,
        full_gate,
        full_up,
        full_down,
        gain_one,
        gain_two,
    ) = gathered
    gain_one = gain_one.astype(jnp.float32)
    gain_two = gain_two.astype(jnp.float32)
    tok_count, d_model = tokens.shape
    head_count = HEADS
    head_dim = d_model // head_count
    segment, positions = layout(seq_lengths[0], tok_count)
    cosine, sine = rope_tables(positions, head_dim)
    inputs = tokens.astype(jnp.float32)
    h_one = norm_gain(inputs, gain_one).astype(jnp.bfloat16)
    q_pre = jnp.dot(h_one, full_query, preferred_element_type=jnp.float32).reshape(
        tok_count, head_count, head_dim
    )
    k_pre = jnp.dot(h_one, full_key, preferred_element_type=jnp.float32).reshape(
        tok_count, head_count, head_dim
    )
    queries = rotate(q_pre, cosine, sine).astype(jnp.bfloat16)
    key_rows = rotate(k_pre, cosine, sine).astype(jnp.bfloat16)
    value_rows = (
        jnp.dot(h_one, full_value, preferred_element_type=jnp.float32)
        .astype(jnp.bfloat16)
        .reshape(tok_count, head_count, head_dim)
    )
    attended, log_total = attend_forward(queries, key_rows, value_rows, segment)
    attended = attended.reshape(tok_count, d_model).astype(jnp.bfloat16)
    middle = inputs + jnp.dot(attended, full_out, preferred_element_type=jnp.float32)
    h_two = norm_gain(middle, gain_two).astype(jnp.bfloat16)
    gate = jnp.dot(h_two, full_gate, preferred_element_type=jnp.float32)
    upward = jnp.dot(h_two, full_up, preferred_element_type=jnp.float32)
    hidden = swiglu(gate, upward).astype(jnp.bfloat16)
    result = middle + jnp.dot(hidden, full_down, preferred_element_type=jnp.float32)
    output = result.astype(jnp.bfloat16)
    grad_out_rows = cotangent.astype(jnp.float32)
    grad_down = outer_sum(hidden, cotangent)
    grad_hidden = back_dot(cotangent, full_down)
    mix_value, mix_back = jax.vjp(swiglu, gate, upward)
    grad_gate_f, grad_up_f = mix_back(grad_hidden)
    grad_gate_rows = grad_gate_f.astype(jnp.bfloat16)
    grad_up_rows = grad_up_f.astype(jnp.bfloat16)
    grad_gate = outer_sum(h_two, grad_gate_rows)
    grad_up = outer_sum(h_two, grad_up_rows)
    grad_h_two = back_dot(grad_gate_rows, full_gate) + back_dot(grad_up_rows, full_up)
    norm_value_two, norm_back_two = jax.vjp(norm_gain, middle, gain_two)
    grad_mid_norm, grad_gain_two = norm_back_two(grad_h_two)
    grad_middle = grad_out_rows + grad_mid_norm
    grad_mid_low = grad_middle.astype(jnp.bfloat16)
    grad_out_proj = outer_sum(attended, grad_mid_low)
    grad_attended = (
        back_dot(grad_mid_low, full_out)
        .astype(jnp.bfloat16)
        .reshape(tok_count, head_count, head_dim)
    )
    grad_q, grad_k, grad_v = attend_backward(
        queries, key_rows, value_rows, log_total, grad_attended, segment
    )
    rot_value, rot_back = jax.vjp(lambda turned_in: rotate(turned_in, cosine, sine), q_pre)
    grad_q_pre = rot_back(grad_q)[0].astype(jnp.bfloat16).reshape(tok_count, d_model)
    grad_k_pre = rot_back(grad_k)[0].astype(jnp.bfloat16).reshape(tok_count, d_model)
    grad_v_low = grad_v.astype(jnp.bfloat16).reshape(tok_count, d_model)
    grad_query = outer_sum(h_one, grad_q_pre)
    grad_key = outer_sum(h_one, grad_k_pre)
    grad_value = outer_sum(h_one, grad_v_low)
    grad_h_one = (
        back_dot(grad_q_pre, full_query)
        + back_dot(grad_k_pre, full_key)
        + back_dot(grad_v_low, full_value)
    )
    norm_value_one, norm_back_one = jax.vjp(norm_gain, inputs, gain_one)
    grad_in_norm, grad_gain_one = norm_back_one(grad_h_one)
    grad_tokens = (grad_middle + grad_in_norm).astype(jnp.bfloat16)
    wide_shares = (
        lax.psum_scatter(grad_query, "wide", scatter_dimension=0, tiled=True),
        lax.psum_scatter(grad_key, "wide", scatter_dimension=0, tiled=True),
        lax.psum_scatter(grad_value, "wide", scatter_dimension=0, tiled=True),
        lax.psum_scatter(grad_out_proj, "wide", scatter_dimension=0, tiled=True),
        lax.psum_scatter(grad_gate, "wide", scatter_dimension=0, tiled=True),
        lax.psum_scatter(grad_up, "wide", scatter_dimension=0, tiled=True),
        lax.psum_scatter(grad_down, "wide", scatter_dimension=0, tiled=True),
        lax.psum_scatter(grad_gain_one, "wide", scatter_dimension=0, tiled=True),
        lax.psum_scatter(grad_gain_two, "wide", scatter_dimension=0, tiled=True),
    )
    summed = (
        lax.psum(wide_shares[0].astype(jnp.bfloat16), "narrow").astype(jnp.float32),
        lax.psum(wide_shares[1].astype(jnp.bfloat16), "narrow").astype(jnp.float32),
        lax.psum(wide_shares[2].astype(jnp.bfloat16), "narrow").astype(jnp.float32),
        lax.psum(wide_shares[3].astype(jnp.bfloat16), "narrow").astype(jnp.float32),
        lax.psum(wide_shares[4].astype(jnp.bfloat16), "narrow").astype(jnp.float32),
        lax.psum(wide_shares[5].astype(jnp.bfloat16), "narrow").astype(jnp.float32),
        lax.psum(wide_shares[6].astype(jnp.bfloat16), "narrow").astype(jnp.float32),
        lax.psum(wide_shares[7].astype(jnp.bfloat16), "narrow").astype(jnp.float32),
        lax.psum(wide_shares[8].astype(jnp.bfloat16), "narrow").astype(jnp.float32),
    )
    return (
        output,
        grad_tokens,
        summed[0],
        summed[1],
        summed[2],
        summed[3],
        summed[4],
        summed[5],
        summed[6],
        summed[7],
        summed[8],
    )


def solution(mesh):
    in_specs = (
        P(("wide", "narrow"), None),
        P(("wide", "narrow"), None),
        P("wide", None),
        P("wide", None),
        P("wide", None),
        P("wide", None),
        P("wide", None),
        P("wide", None),
        P("wide", None),
        P("wide"),
        P("wide"),
        P(("wide", "narrow"), None),
    )
    out_specs = (
        P(("wide", "narrow"), None),
        P(("wide", "narrow"), None),
        P("wide", None),
        P("wide", None),
        P("wide", None),
        P("wide", None),
        P("wide", None),
        P("wide", None),
        P("wide", None),
        P("wide"),
        P("wide"),
    )
    blocks = (mesh.shape["wide"], mesh.shape["narrow"]) == (16, 2)
    body = fast_body if blocks else plain_body
    return jax.shard_map(body, mesh=mesh, in_specs=in_specs, out_specs=out_specs, check_vma=False)
```

```python
import functools
import math

import jax
import jax.numpy as jnp
from jax import lax
from jax.experimental import pallas as pl
from jax.experimental.pallas import tpu as pltpu
from jax.sharding import PartitionSpec as P

HEADS = 12
EPS = 1e-06
NEG = -1e30
BF = jnp.bfloat16
F32 = jnp.float32
MESH = pl.DeviceIdType.MESH
VMEM_BYTES = 60 * 2**20


def nn(left, right):
    return jnp.dot(left, right, preferred_element_type=F32)


def nt(left, right):
    return lax.dot_general(left, right, (((1,), (1,)), ((), ())), preferred_element_type=F32)


def flat(values):
    return values.reshape(-1, values.shape[-1])


def sigmoid(v):
    return 1.0 / (1.0 + jnp.exp(-v))


def three_way(v):
    high = v.astype(BF)
    rest = v - high.astype(F32)
    mid = rest.astype(BF)
    return high, mid, (rest - mid.astype(F32)).astype(BF)


FORE = [
    ("enter", "Q.s0"), ("Q1", "Q.a0 Q.b0"), ("Q2", "Q.p3 Q.b3 Q.a3 Q.p2"),
    ("Q3", "Q.a2 D0.s0 Q.d3"), ("Q3", "Q.p1 Q.d0 Q.d2 O.s0"), ("Q3", "Q.b2 Q.a1 Q.b1 Q.d1"), ("Q3", "D0.s1 Q.s5"),
    ("P.2", "O.s1"), ("P.3", "D1.s0"), ("A0.2", "O.s2"), ("A1.0", "G0.s0"), ("A1.3", "D1.s1"), ("A2.2", "G1.s0"), ("A2.3", "G0.s1"),
    ("A3.1", "O.s3"), ("A3.2", "O.s4 D0.s2"), ("A4.0", "D1.s2 D0.s3"), ("A4.2", "G2.s0 G0.s2"), ("A5.1", "D0.s4"), ("A5.2", "G1.s1"),
    ("A5.3", "D1.s3 O.s5"), ("M.0", "D0.s5 D1.s4"), ("M.0", "G0.s4 G0.s3"), ("M.2", "G2.s1 G3.s0"), ("F0.m0", "G0.s5 D1.s5 G1.s3"), ("F0.m2", "G1.s2"),
    ("F0.g0", "G3.s1"), ("F0.g2", "G1.s4"), ("F0.g3", "G2.s2"), ("F1.m0", "G1.s5"), ("F1.g0", "G2.s4 G2.s3"), ("F1.g3", "G3.s2"), ("F1.d0", "G3.s3"),
    ("F2.m0", "G2.s5"), ("F2.m3", "G3.s4"), ("F2.g3", "G3.s5"),
]
HIND = [
    ("enter", "G0.r1 G1.r1"), ("A0.3", "G0.r2 O.r1"), ("W0.0", "G1.r2"), ("A1.0", "D.r1"), ("A1.1", "G0.r3"), ("A1.3", "O.r2"), ("A2.0", "G1.r3 G2.r1"),
    ("A3.1", "D.r2"), ("A3.2", "O.r3"), ("W3.0", "G2.r2 G3.r1"), ("A4.0", "Q0.r1 D.r3"), ("W4.0", "G2.r3"),
    ("A5.1", "G3.r2 Q1.r1"), ("A5.2", "Q0.r2"), ("W5.0", "G3.r3"), ("L.0", "Q1.r2"), ("L.1", "Q0.r3"), ("L.2", "Q2.r1 Q1.r3"), ("L.3", "G1.r4"),
    ("end", "G0.r4 D.r4 Q2.r2"), ("end", "O.r4 Q0.r4 O.r5 G2.r4"), ("end", "Q2.r3 D.r5 Q1.r4 G3.r4"), ("end", "G0.r5 G2.r5 G1.r5 Q0.r5"),
    ("gains", "G3.r5 Q1.r5 Q2.r4 Q2.r5"),
]


class Place:
    def __init__(self):
        wide = lax.axis_index("wide")
        self.c = lax.axis_index("narrow")
        self.w = wide
        self.z = wide // 4
        self.p = lax.rem(wide, 4)
        across_y = lax.rem(self.p + 2, 4)
        across_x = self.p + 1 - 2 * lax.rem(self.p, 2)
        self.q1 = (1 - self.c) * across_y + self.c * across_x
        self.q2 = (1 - self.c) * across_x + self.c * across_y
        self.q3 = 3 - self.p
        self.first = {"wide": self.z * 4 + self.q1}
        self.second = {"wide": self.z * 4 + self.q2}
        self.other = {"narrow": 1 - self.c}

    def z_at(self, d):
        return lax.rem(self.z + d + 4, 4)

    def z_dev(self, d):
        return {"wide": self.z_at(d) * 4 + self.p}


def enter(place):
    sem = pltpu.get_barrier_semaphore()
    for d in range(1, 16):
        pl.semaphore_signal(sem, inc=1, device_id={"wide": lax.rem(place.w + d, 16)}, device_id_type=MESH)
    pl.semaphore_signal(sem, inc=1, device_id=place.other, device_id_type=MESH)
    pl.semaphore_wait(sem, 16)


def remote(src, dst, send, recv, device):
    return pltpu.make_async_remote_copy(
        src_ref=src, dst_ref=dst, send_sem=send, recv_sem=recv, device_id=device, device_id_type=MESH
    )


def lane_of(rows, lanes=128):
    return lax.broadcasted_iota(jnp.int32, (rows, lanes), 1)


def spread(index):
    row = lax.broadcasted_iota(jnp.int32, (128, 768), 0)
    col = lax.broadcasted_iota(jnp.int32, (128, 768), 1)
    return jnp.where((col == row + 48 * index) & (row < 48), 1.0, 0.0).astype(BF)


class Gather:
    def __init__(self, place, buf, start, width, rows, send, recv):
        self.place = place
        r0, rn = rows

        def part(z, q, core):
            col = pl.ds(pl.multiple_of(start + core * width, 128), width)
            return buf.at[z, q, pl.ds(r0, rn), col]

        def block(q, core):
            col = pl.ds(pl.multiple_of(start + core * width, 128), width)
            return buf.at[:, q, pl.ds(r0, rn), col]

        self.part, self.block, self.send, self.recv = part, block, send, recv

    def copy(self, k, ref, device):
        return remote(ref, ref, self.send.at[k], self.recv.at[k], device)


def block_steps(unit):
    pc = unit.place
    me = pc.c
    zs = [unit.copy(d - 1, unit.part(pc.z, pc.p, me), pc.z_dev(d)) for d in (1, 2, 3)]
    own = unit.block(pc.p, me)
    to_first = unit.copy(3, own, pc.first)
    to_second = unit.copy(4, own, pc.second)
    on_second = unit.copy(5, unit.block(pc.q1, me), pc.second)
    cores = [unit.copy(6 + i, unit.block(q, me), pc.other) for i, q in enumerate((pc.p, pc.q1, pc.q2, pc.q3))]

    def s0():
        for copy in zs:
            copy.start()

    def s1():
        for copy in zs:
            copy.wait_recv()
        to_first.start()
        to_second.start()
        cores[0].start()

    def s2():
        to_first.wait_recv()
        on_second.start()
        cores[1].start()

    def s3():
        to_second.wait_recv()
        cores[2].start()

    def s4():
        on_second.wait_recv()
        cores[3].start()

    def s5():
        for copy in cores:
            copy.wait_recv()
        for copy in [*zs, to_first, to_second, on_second, *cores]:
            copy.wait_send()

    return [s0, s1, s2, s3, s4, s5]


def piece_steps(unit):
    pc = unit.place
    me = pc.c
    planes = (pc.p, pc.q1, pc.q2, pc.q3)
    zs = [unit.copy(d - 1, unit.part(pc.z, pc.p, me), pc.z_dev(d)) for d in (1, 2, 3)]
    first = [unit.copy(3 + d, unit.part(pc.z_at(-d), pc.p, me), pc.first) for d in range(4)]
    second = [unit.copy(7 + d, unit.part(pc.z_at(-d), pc.p, me), pc.second) for d in range(4)]
    onward = [unit.copy(11 + d, unit.part(pc.z_at(-d), pc.q1, me), pc.second) for d in range(4)]
    cores = [[unit.copy(15 + 4 * i + d, unit.part(pc.z_at(-d), q, me), pc.other) for d in range(4)] for i, q in enumerate(planes)]

    def spread_out(d):
        first[d].start()
        second[d].start()
        cores[0][d].start()

    def s0():
        for copy in zs:
            copy.start()
        spread_out(0)

    def p(d):
        zs[d - 1].wait_recv()
        spread_out(d)

    def a(d):
        first[d].wait_recv()
        onward[d].start()
        cores[1][d].start()

    def b(d):
        second[d].wait_recv()
        cores[2][d].start()

    def c(d):
        onward[d].wait_recv()
        cores[3][d].start()

    def s5():
        for line in cores:
            for copy in line:
                copy.wait_recv()
        for copy in [*zs, *first, *second, *onward, *sum(cores, [])]:
            copy.wait_send()

    steps = {"s0": s0, "s5": s5}
    for letter, step in (("p", p), ("a", a), ("b", b), ("d", c)):
        for d in range(4):
            steps[f"{letter}{d}"] = functools.partial(step, d)
    return steps


def pair_at(j):
    return lax.rem(j, 2) * 1152 + (j // 2) * 384


class Ticks:
    def __init__(self, table, steps):
        self.steps = steps
        self.table = {}
        for name, listed in table:
            self.table[name] = self.table.get(name, []) + listed.split()
        asked = sum(self.table.values(), [])
        assert sorted(asked) == sorted(steps), (set(asked) ^ set(steps))

    def at(self, name):
        for step in self.table.get(name, []):
            self.steps[step]()

    def when(self, index, names):
        for k, name in enumerate(names):
            if name in self.table:
                pl.when(index == k)(functools.partial(self.at, name))


def turned(values, lane, back):
    up = pltpu.roll(values, 96, 1)
    down = pltpu.roll(values, 32, 1)
    low = lax.rem(lane, 64) < 32
    return jnp.where(low, up, -down) if back else jnp.where(low, -up, down)


def fore_kernel(
    lens, x_ref, dy_ref, g1_ref, g2_ref, wq, wk, wv, wo, wg, wu, wd,
    q_out, k_out, v_out, o_out, do_out, h1t_out, lse_out, seg_out, rope_out, w_out, dx2_out, gain_out, gg_out, y_out, gu_sum, d_sum, o_sum,
    w_s, wo_s, wgu_s, wd_s, gain_s, gains, x2_s, y_s, dh2_s, h1t_s, q_s, k_s, v_s, o_s, lse_s, seg_s, rope_s,
    hidt_s, dgu_s, gg_s, yb_s, gu_st, d_st, o_st, gu_r, d_r, o_r,
    wsend, wrecv, usend, urecv, gsend, grecv, rsend, rrecv, lsem, osem,
):
    pc = Place()
    tok = x_ref.shape[0]
    blocks = tok // 256
    loads = []

    def load(src, dst):
        copy = pltpu.make_async_copy(src, dst, lsem.at[len(loads)])
        copy.start()
        loads.append(copy)

    def half(start, width):
        return pl.ds(pl.multiple_of(start + pc.c * width, 128), width)

    for m in range(3):
        for n, w in enumerate((wq, wk, wv)):
            load(w.at[:, half(m * 256, 128)], w_s.at[pc.z, pc.p, :, pl.ds(pl.multiple_of(pc.c * 1152 + m * 384 + n * 128, 128), 128)])
    early = len(loads)
    load(wo.at[:, half(0, 384)], wo_s.at[pc.z, pc.p, :, half(0, 384)])
    load(wd.at[:, half(0, 384)], wd_s.at[pc.z, pc.p, :, half(0, 384)])
    for u in range(4):
        for n, w in enumerate((wg, wu)):
            load(w.at[:, half(u * 512, 256)], wgu_s.at[pc.z, pc.p, :, pl.ds(pl.multiple_of(u * 1024 + n * 256 + pc.c * 512, 128), 256)])
    enter(pc)
    for copy in loads[:early]:
        copy.wait()
    gain_s[pc.w] = jnp.zeros((8, 128), F32)
    for n, ref in enumerate((g1_ref, g2_ref)):
        gain_s[pc.w, n : n + 1, 0 : ref.shape[1]] = ref[...].astype(F32)
    gain_copies = [
        remote(gain_s.at[pc.w], gain_s.at[pc.w], gsend.at[d - 1], grecv.at[d - 1], {"wide": lax.rem(pc.w + d, 16)}) for d in range(1, 16)
    ]
    for copy in gain_copies:
        copy.start()
    ends, total = [], jnp.int32(0)
    for s in range(4):
        total = total + lens[0, s]
        ends.append(total)

    def tables(r, carry):
        rs = pl.ds(pl.multiple_of(r * 256, 256), 256)
        lane = lane_of(256)
        place = lax.broadcasted_iota(jnp.int32, (256, 128), 0) + r * 256
        seg = jnp.zeros((256, 128), jnp.int32)
        start = jnp.zeros((256, 128), jnp.int32)
        for s in range(4):
            past = place >= ends[s]
            seg = seg + past.astype(jnp.int32)
            start = jnp.where(past, ends[s], start)
        column = lax.rem(lane, 32).astype(F32)
        angle = (place - start).astype(F32) * jnp.exp(column * (-2.0 * math.log(10000.0) / 64))
        rope_s[0, rs, :] = jnp.cos(angle)
        rope_s[1, rs, :] = jnp.sin(angle)
        seg_s[0, rs, :] = jnp.where((lane == seg) | (lane >= 4), 0.0, NEG).astype(BF)
        seg_s[1, rs, :] = jnp.where((lane == seg) | ((lane >= 4) & (lane < 7)), 1.0, 0.0).astype(BF)
        return carry

    units = {
        "O": Gather(pc, wo_s, 0, 384, (0, 48), usend.at[0], urecv.at[0]),
        "D0": Gather(pc, wd_s, 0, 384, (0, 64), usend.at[1], urecv.at[1]),
        "D1": Gather(pc, wd_s, 0, 384, (64, 64), usend.at[2], urecv.at[2]),
    }
    for u in range(4):
        units[f"G{u}"] = Gather(pc, wgu_s, 1024 * u, 512, (0, 48), usend.at[3 + u], urecv.at[3 + u])
    steps = {f"Q.{name}": step for name, step in piece_steps(Gather(pc, w_s, 0, 1152, (0, 48), wsend, wrecv)).items() if name != "p0"}
    for u, unit in units.items():
        for k, step in enumerate(block_steps(unit)):
            steps[f"{u}.s{k}"] = step
    ticks = Ticks(FORE, steps)
    ticks.at("enter")
    for copy in loads[early:]:
        copy.wait()
    lax.fori_loop(0, blocks // 2, tables, 0)
    ticks.at("Q1")
    lax.fori_loop(blocks // 2, blocks, tables, 0)
    ticks.at("Q2")
    for copy in gain_copies:
        copy.wait_recv()

    def gain_rows(w, rows):
        return rows + nn(gain_s[w].astype(BF), spread(w))

    gains[...] = lax.fori_loop(0, 16, gain_rows, jnp.zeros((8, 768), F32))
    ticks.at("Q3")
    outs = []

    def store(src, dst):
        copy = pltpu.make_async_copy(src, dst, osem.at[len(outs)])
        copy.start()
        outs.append(copy)
        return copy

    store(gains, gain_out)
    store(w_s, w_out)
    store(seg_s, seg_out)
    store(rope_s, rope_out)

    def project(r, carry):
        ticks.when(r, [f"P.{i}" for i in range(4)])
        rs = pl.ds(pl.multiple_of(r * 256, 256), 256)
        lane = lane_of(256)
        x = x_ref[rs, :].astype(F32)
        h1 = (x * lax.rsqrt(jnp.mean(x * x, axis=1, keepdims=True) + EPS) * gains[0:1, :]).astype(BF)
        h1t_s[:, rs] = h1.T
        cos, sin = rope_s[0, rs, :], rope_s[1, rs, :]
        for half in range(2):
            pre = nn(h1, flat(w_s[:, :, :, half * 1152 : (half + 1) * 1152]))
            for m in range(3):
                cs = pl.ds((2 * m + half) * 128, 128)
                qp, kp, vp = (pre[:, m * 384 + n * 128 : m * 384 + (n + 1) * 128] for n in range(3))
                q_s[rs, cs] = ((qp * cos + turned(qp, lane, False) * sin).astype(BF).astype(F32) * 0.125).astype(BF)
                k_s[rs, cs] = (kp * cos + turned(kp, lane, False) * sin).astype(BF)
                v_s[rs, cs] = vp.astype(BF)
        return carry

    lax.fori_loop(0, blocks, project, 0)
    kept = [store(q_s, q_out), store(k_s, k_out), store(v_s, v_out), store(h1t_s, h1t_out)]

    def pair(j, carry):
        cs = pl.ds(pl.multiple_of(j * 128, 128), 128)
        lane = lane_of(256)
        below = lax.broadcasted_iota(jnp.int32, (256, 256), 0) >= lax.broadcasted_iota(jnp.int32, (256, 256), 1)
        for i in range(blocks):
            ticks.when(j, [f"A{t}.{i}" for t in range(6)])
            rs, before = pl.ds(i * 256, 256), pl.ds(0, i * 256)
            qt = q_s[rs, cs]
            parts = []
            for h in range(2):
                qm = jnp.where((lane < 64) == (h == 0), qt, BF(0))
                qm = jnp.concatenate([qm, seg_s[0, rs, :]], axis=1)
                sd = jnp.where(below, nt(qm, jnp.concatenate([k_s[rs, cs], seg_s[1, rs, :]], axis=1)), NEG)
                top = jnp.max(sd, axis=1, keepdims=True)
                if i:
                    so = nt(qm, jnp.concatenate([k_s[before, cs], seg_s[1, before, :]], axis=1))
                    top = jnp.maximum(top, jnp.max(so, axis=1, keepdims=True))
                pd = jnp.exp(sd - top)
                mass = jnp.sum(pd, axis=1, keepdims=True)
                acc = nn(pd.astype(BF), v_s[rs, cs])
                if i:
                    po = jnp.exp(so - top)
                    mass = mass + jnp.sum(po, axis=1, keepdims=True)
                    acc = acc + nn(po.astype(BF), v_s[before, cs])
                parts.append(acc * (1.0 / mass))
                lse_s[rs, :] = jnp.where(lane == 2 * j + h, top + jnp.log(mass), lse_s[rs, :])
            o_s[rs, cs] = jnp.where(lane < 64, parts[0], parts[1]).astype(BF)
        return carry

    lse_s[...] = jnp.zeros_like(lse_s)
    lax.fori_loop(0, 6, pair, 0)
    store(o_s, o_out)
    store(lse_s, lse_out)
    for copy in kept:
        copy.wait()
    h2_s, h2t_s, dxb_s, do_s = q_s, h1t_s, k_s, v_s
    gain2 = gains[1:2, :]

    def middle(r, carry):
        ticks.when(r, [f"M.{i}" for i in range(4)])
        rs = pl.ds(pl.multiple_of(r * 256, 256), 256)
        x2 = x_ref[rs, :].astype(F32) + nn(o_s[rs, :], flat(wo_s[...]))
        x2_s[rs, :] = x2
        h2 = (x2 * lax.rsqrt(jnp.mean(x2 * x2, axis=1, keepdims=True) + EPS) * gain2).astype(BF)
        h2_s[rs, :] = h2
        h2t_s[:, rs] = h2.T
        return carry

    lax.fori_loop(0, blocks, middle, 0)

    def swap(buf, width, got, k):
        far = pl.ds(pl.multiple_of((1 - pc.c) * width, 128), width)
        return remote(buf.at[..., far], got, rsend.at[k], rrecv.at[k], pc.other)

    def near(buf, width):
        return buf[..., pl.ds(pl.multiple_of(pc.c * width, 128), width)]

    gu_swap = [swap(gu_st.at[u % 2], 512, gu_r.at[u], u) for u in range(4)]
    d_swap = [swap(d_st.at[u % 2], 384, d_r.at[u], 4 + u) for u in range(4)]

    def settle(u):
        gu_swap[u].wait_recv()
        d_swap[u].wait_recv()
        for z in range(4):
            mine = gu_st[u % 2, z, :, :, pl.ds(pl.multiple_of(pc.c * 512, 128), 512)]
            gu_r[u, z] = (gu_r[u, z].astype(F32) + mine.astype(F32)).astype(BF)
        mine = d_st[u % 2, :, :, pl.ds(pl.multiple_of(pc.c * 384, 128), 384)]
        d_r[u] = (d_r[u].astype(F32) + mine.astype(F32)).astype(BF)
        store(gu_r.at[u], gu_sum.at[u])
        store(d_r.at[u], d_sum.at[u])
        gu_swap[u].wait_send()
        d_swap[u].wait_send()

    for u in range(4):
        wgu = pl.ds(u * 1024, 1024)

        def mix(r, carry):
            ticks.when(r, [f"F{u}.m{i}" for i in range(4)])
            rs = pl.ds(pl.multiple_of(r * 256, 256), 256)
            both = nn(h2_s[rs, :], flat(wgu_s[:, :, :, wgu]))
            dhid = nt(dy_ref[rs, :], flat(wd_s[u]))
            hids, grads = [], []
            for n in range(2):
                gate, up = both[:, n * 512 : n * 512 + 256], both[:, n * 512 + 256 : n * 512 + 512]
                dh = dhid[:, n * 256 : n * 256 + 256]
                sig = sigmoid(gate)
                silu = gate * sig
                hids.append((silu * up).astype(BF))
                grads.append((dh * up * sig * (1.0 + gate * (1.0 - sig))).astype(BF))
                grads.append((dh * silu).astype(BF))
            hid = jnp.concatenate(hids, axis=1)
            dgu = jnp.concatenate(grads, axis=1)
            hidt_s[:, rs] = hid.T
            dgu_s[rs, :] = dgu
            yv = nn(hid, flat(wd_s[u]))
            dv = nt(dgu, flat(wgu_s[:, :, :, wgu]))
            if u == 0:
                y_s[rs, :] = x2_s[rs, :] + yv
                dh2_s[rs, :] = dv
            else:
                y_s[rs, :] += yv
                dh2_s[rs, :] += dv
            return carry

        lax.fori_loop(0, blocks, mix, 0)
        if u >= 2:
            settle(u - 2)

        def weight_gu(z, carry):
            ticks.when(z, [f"F{u}.g{i}" for i in range(4)])
            rows = nn(h2t_s[pl.ds(pl.multiple_of(z * 192, 64), 192), :], dgu_s[...])
            gu_st[u % 2, z] = rows.astype(BF).reshape(4, 48, 1024)
            return carry

        lax.fori_loop(0, 4, weight_gu, 0)

        def weight_d(k, carry):
            ticks.when(k, [f"F{u}.d{i}" for i in range(2)])
            rows = nn(hidt_s[pl.ds(pl.multiple_of(k * 256, 256), 256), :], dy_ref[...])
            d_st[u % 2, pl.ds(k * 2, 2)] = rows.astype(BF).reshape(2, 128, 768)
            return carry

        lax.fori_loop(0, 2, weight_d, 0)
        gu_swap[u].start()
        d_swap[u].start()

    gg_s[...] = jnp.zeros_like(gg_s)

    def back(r, carry):
        rs = pl.ds(pl.multiple_of(r * 256, 256), 256)
        yb_s[rs, :] = y_s[rs, :].astype(BF)
        x2, dh2 = x2_s[rs, :], dh2_s[rs, :]
        r2 = lax.rsqrt(jnp.mean(x2 * x2, axis=1, keepdims=True) + EPS)
        n2 = x2 * r2
        e2 = dh2 * gain2
        gg_s[0:1, :] += jnp.sum(dh2 * n2, axis=0, keepdims=True)
        dx2 = dy_ref[rs, :].astype(F32) + r2 * (e2 - n2 * jnp.mean(e2 * n2, axis=1, keepdims=True))
        x2_s[rs, :] = dx2
        dxb = dx2.astype(BF)
        dxb_s[rs, :] = dxb
        do_s[rs, :] = nt(dxb, flat(wo_s[...])).astype(BF)
        h2t_s[:, rs] = o_s[rs, :].T
        return carry

    lax.fori_loop(0, blocks, back, 0)
    store(yb_s, y_out)
    store(x2_s, dx2_out)
    store(do_s, do_out)
    store(gg_s, gg_out)
    settle(2)

    def weight_o(z, carry):
        rows = nn(h2t_s[pl.ds(pl.multiple_of(z * 192, 64), 192), :], dxb_s[...])
        o_st[z] = rows.astype(BF).reshape(4, 48, 768)
        return carry

    lax.fori_loop(0, 4, weight_o, 0)
    o_swap = swap(o_st, 384, o_r, 8)
    o_swap.start()
    settle(3)
    o_swap.wait_recv()
    mine = o_st[:, :, :, pl.ds(pl.multiple_of(pc.c * 384, 128), 384)]
    o_r[...] = (o_r[...].astype(F32) + mine.astype(F32)).astype(BF)
    store(o_r, o_sum)
    o_swap.wait_send()
    for copy in gain_copies:
        copy.wait_send()
    for copy in outs:
        if not any(copy is done for done in kept):
            copy.wait()


class Reduce:
    def __init__(self, place, keep, r1, r2, r3, total, other_total, send, recv, far1, far2, near):
        pc = place
        self.pc, self.keep, self.r1, self.r2, self.r3, self.total = pc, keep, r1, r2, r3, total
        self.to_first = [remote(ref, r1.at[:, i], send.at[i], recv.at[i], pc.first) for i, ref in enumerate((far1, far2))]
        self.near = near
        self.to_second = remote(keep.at[:, 1], r2, send.at[2], recv.at[2], pc.second)
        self.zs = [remote(keep.at[pc.z_at(d), 0], r3.at[d - 1], send.at[2 + d], recv.at[2 + d], pc.z_dev(d)) for d in (1, 2, 3)]
        self.to_core = remote(total, other_total, send.at[6], recv.at[6], pc.other)

    def steps(self, begin, finish):
        pc = self.pc

        def r1():
            begin()
            for copy in self.to_first:
                copy.start()

        def r2():
            for copy in self.near:
                copy.wait()
            for copy in self.to_first:
                copy.wait_recv()

            def add(z, carry):
                self.keep[z] = (self.keep[z].astype(F32) + self.r1[z].astype(F32)).astype(BF)
                return carry

            lax.fori_loop(0, 4, add, 0)
            self.to_second.start()

        def r3():
            self.to_second.wait_recv()

            def add(z, carry):
                self.keep[z, 0] = (self.keep[z, 0].astype(F32) + self.r2[z].astype(F32)).astype(BF)
                return carry

            lax.fori_loop(0, 4, add, 0)
            for copy in self.zs:
                copy.start()

        def r4():
            for copy in self.zs:
                copy.wait_recv()
            total = self.keep[pc.z, 0].astype(F32)
            for d in range(3):
                total = total + self.r3[d].astype(F32)
            self.total[...] = total
            self.to_core.start()

        def r5():
            self.to_core.wait()
            finish()
            for copy in [*self.to_first, self.to_second, *self.zs]:
                copy.wait_send()

        return [r1, r2, r3, r4, r5]


def hind_kernel(
    q_hbm, k_hbm, v_hbm, o_hbm, do_hbm, lse_hbm, seg_hbm, rope_hbm, h1t_hbm, w_hbm, x_hbm, dx2_hbm, gain_ref, gg_ref, gu_sum, d_sum, o_sum,
    gx_ref, gwq, gwk, gwv, gwo, gwg, gwu, gwd, gg_out,
    q_s, k_s, v_s, o_s, do_s, lse_s, seg_s, rope_s, h1t_s, w_s, x_s, dx2_s, dqkv_s, dk_s, dv_s,
    gq_s, gq_r, gu_k, gu_1, gu_2, gu_3, gu_t, d_k, d_1, d_2, d_3, d_t, o_k, o_1, o_2, o_3, o_t, qk_k, qk_1, qk_2, qk_3, qk_t,
    gg1_s, gg_st, gg_r, gg_c,
    lsem, nsem, ssend, srecv, qsend, qrecv, gsend, grecv,
):
    pc = Place()
    tok = x_s.shape[0]
    blocks = tok // 256
    loads = []

    def load(src, dst):
        copy = pltpu.make_async_copy(src, dst, lsem.at[len(loads)])
        copy.start()
        loads.append(copy)
        return copy

    for src, dst in ((q_hbm, q_s), (k_hbm, k_s), (v_hbm, v_s), (o_hbm, o_s), (do_hbm, do_s), (lse_hbm, lse_s), (seg_hbm, seg_s), (rope_hbm, rope_s)):
        load(src, dst)
    early = len(loads)
    for src, dst in ((h1t_hbm, h1t_s), (w_hbm, w_s), (x_hbm, x_s), (dx2_hbm, dx2_s)):
        load(src, dst)
    enter(pc)

    nears = []

    def start_near(copies):
        for copy in copies:
            copy.start()

    def unit(n, parts, keep, r1, r2, r3, total, finish, source=None):
        near = []
        if source is None:
            near = [pltpu.make_async_copy(parts(q), keep.at[:, i], nsem.at[n, i]) for i, q in enumerate((pc.p, pc.q2))]
        red = Reduce(pc, keep, r1, r2, r3, total.at[0], total.at[1], ssend.at[n], srecv.at[n], parts(pc.q1), parts(pc.q3), near)

        def begin():
            if source is not None:
                source()
            start_near(near)

        return red.steps(begin, finish)

    def halves(ref):
        mine, others = ref[0], ref[1]
        zero = pc.c == 0
        return jnp.where(zero, mine, others), jnp.where(zero, others, mine)

    units = {}
    for u in range(4):

        def finish_gu(u=u):
            low, high = halves(gu_t.at[u])
            for n, part in enumerate((low, high)):
                gwg[:, pl.ds(u * 512 + n * 256, 256)] = part[:, :256]
                gwu[:, pl.ds(u * 512 + n * 256, 256)] = part[:, 256:]

        units[f"G{u}"] = unit(u, lambda q, u=u: gu_sum.at[u, :, q], gu_k.at[u], gu_1.at[u], gu_2.at[u], gu_3.at[u], gu_t.at[u], finish_gu)

    def finish_o():
        low, high = halves(o_t)
        gwo[:, 0:384] = low
        gwo[:, 384:768] = high

    units["O"] = unit(4, lambda q: o_sum.at[:, q], o_k, o_1, o_2, o_3, o_t, finish_o)

    def finish_d():
        low, high = halves(d_t)
        gwd[:, 0:384] = low
        gwd[:, 384:768] = high

    units["D"] = unit(5, lambda q: d_sum.at[:, q], d_k, d_1, d_2, d_3, d_t, finish_d)

    q_swaps = [remote(gq_s.at[2 * m + 1 - pc.c], gq_r.at[m], qsend.at[m], qrecv.at[m], pc.other) for m in range(3)]

    for m in range(3):

        def finish_q(m=m):
            low, high = halves(qk_t.at[m])
            for n, part in enumerate((low, high)):
                cs = pl.ds((2 * m + n) * 128, 128)
                gwq[:, cs] = part[:, 0:128]
                gwk[:, cs] = part[:, 128:256]
                gwv[:, cs] = part[:, 256:384]

        def source(m=m):
            q_swaps[m].wait_recv()
            mine = 2 * m + pc.c

            def add(z, carry):
                got = gq_r[m, z]
                gq_r[m, z] = (got.astype(F32) + gq_s[mine, z].astype(F32)).astype(BF)
                return carry

            lax.fori_loop(0, 4, add, 0)
            for i, q in enumerate((pc.p, pc.q2)):
                qk_k[m, :, i] = gq_r[m, :, q]
            q_swaps[m].wait_send()

        units[f"Q{m}"] = unit(6 + m, lambda q, m=m: gq_r.at[m, :, q], qk_k.at[m], qk_1.at[m], qk_2.at[m], qk_3.at[m], qk_t.at[m], finish_q, source)
    ticks = Ticks(HIND, {f"{u}.r{k + 1}": step for u, steps in units.items() for k, step in enumerate(steps)})
    ticks.at("enter")
    for copy in loads[:early]:
        copy.wait()
    ones = (lane_of(tok) < 3).astype(BF)

    def pair(j, carry):
        cs = pl.ds(pl.multiple_of(j * 128, 128), 128)
        lane = lane_of(256)
        above = lax.broadcasted_iota(jnp.int32, (256, 256), 0) <= lax.broadcasted_iota(jnp.int32, (256, 256), 1)
        at = pair_at(j)
        dk_s[...] = jnp.zeros_like(dk_s)
        dv_s[...] = jnp.zeros_like(dv_s)
        vaug = jnp.concatenate([v_s[:, cs], ones], axis=1)
        kaug = jnp.concatenate([k_s[:, cs], seg_s[1]], axis=1)
        kt = k_s[:, cs].T
        for i in range(blocks):
            ticks.when(j, [f"A{t}.{i}" for t in range(6)])
            rs, first, last = pl.ds(i * 256, 256), i * 256, (i + 1) * 256
            qt, dt = q_s[rs, cs], do_s[rs, cs]
            prod = dt.astype(F32) * o_s[rs, cs].astype(F32)
            parts = []
            for h in range(2):
                mask = (lane < 64) == (h == 0)
                qm, dm = jnp.where(mask, qt, BF(0)), jnp.where(mask, dt, BF(0))
                delta = jnp.sum(jnp.where(mask, prod, 0.0), axis=1, keepdims=True)
                lse = jnp.sum(jnp.where(lane == 2 * j + h, lse_s[rs, :], 0.0), axis=1, keepdims=True)
                a0, a1, a2 = three_way(-lse)
                qa = jnp.where(lane == 4, a0, jnp.where(lane == 5, a1, jnp.where(lane == 6, a2, seg_s[0, rs, :])))
                b0, b1, b2 = three_way(-delta)
                da = jnp.where(lane == 0, b0, jnp.where(lane == 1, b1, jnp.where(lane == 2, b2, BF(0))))
                qaug, daug = jnp.concatenate([qm, qa], axis=1), jnp.concatenate([dm, da], axis=1)
                pd = jnp.exp(jnp.where(above, nt(kaug[first:last], qaug), NEG))
                dsd = (pd * nt(vaug[first:last], daug)).astype(BF)
                dv_s[rs, :] += nn(pd.astype(BF), dm)
                dk_s[rs, :] += nn(dsd, qm)
                dq = nn(kt[h * 64 : h * 64 + 64, first:last], dsd)
                if i:
                    before = pl.ds(0, first)
                    po = jnp.exp(nt(kaug[:first], qaug))
                    dso = (po * nt(vaug[:first], daug)).astype(BF)
                    dv_s[before, :] += nn(po.astype(BF), dm)
                    dk_s[before, :] += nn(dso, qm)
                    dq = dq + nn(kt[h * 64 : h * 64 + 64, :first], dso)
                parts.append(dq)
            dq = jnp.concatenate(parts, axis=0).T * 0.125
            dq = dq * rope_s[0, rs, :] + turned(dq * rope_s[1, rs, :], lane, True)
            dqkv_s[rs, pl.ds(pl.multiple_of(at, 128), 128)] = dq.astype(BF)

        def finish(r, carry):
            rs = pl.ds(pl.multiple_of(r * 256, 256), 256)
            dk = dk_s[rs, :]
            dk = dk * rope_s[0, rs, :] + turned(dk * rope_s[1, rs, :], lane, True)
            dqkv_s[rs, pl.ds(pl.multiple_of(at + 128, 128), 128)] = dk.astype(BF)
            dqkv_s[rs, pl.ds(pl.multiple_of(at + 256, 128), 128)] = dv_s[rs, :].astype(BF)
            return carry

        lax.fori_loop(0, blocks, finish, 0)
        pl.when(j == 0)(loads[early].wait)

        ticks.when(j, [f"W{t}.0" for t in range(6)])

        def weight(z, carry):
            rows = nn(h1t_s[pl.ds(pl.multiple_of(z * 192, 64), 192), :], dqkv_s[:, pl.ds(pl.multiple_of(at, 128), 384)])
            gq_s[j, z] = rows.astype(BF).reshape(4, 48, 384)
            return carry

        lax.fori_loop(0, 4, weight, 0)
        for m in range(3):
            pl.when((j // 2 == m) & (lax.rem(j, 2) != pc.c))(q_swaps[m].start)
        return carry

    lax.fori_loop(0, 6, pair, 0)
    for copy in loads[early + 1 :]:
        copy.wait()
    gg1_s[...] = jnp.zeros_like(gg1_s)
    gain1 = gain_ref[0:1, :]

    def last(r, carry):
        ticks.when(r, [f"L.{i}" for i in range(4)])
        rs = pl.ds(pl.multiple_of(r * 256, 256), 256)
        dh1 = nt(dqkv_s[rs, :], flat(w_s[...]))
        x = x_s[rs, :].astype(F32)
        r1 = lax.rsqrt(jnp.mean(x * x, axis=1, keepdims=True) + EPS)
        n1 = x * r1
        e1 = dh1 * gain1
        gg1_s[0:1, :] += jnp.sum(dh1 * n1, axis=0, keepdims=True)
        gx_ref[rs, :] = (dx2_s[rs, :] + r1 * (e1 - n1 * jnp.mean(e1 * n1, axis=1, keepdims=True))).astype(BF)
        return carry

    lax.fori_loop(0, blocks, last, 0)
    row = lax.broadcasted_iota(jnp.int32, (16, 768), 0)
    terms = jnp.zeros((16, 768), BF)
    for n, sums in enumerate((gg1_s, gg_ref)):
        for k, term in enumerate(three_way(sums[0:1, :])):
            terms = jnp.where(row == 8 * n + k, term, terms)

    def cut(w, carry):
        gg_st[w] = nt(terms, spread(w))
        return carry

    lax.fori_loop(0, 16, cut, 0)
    copies = []
    for d in range(1, 16):
        to = lax.rem(pc.w + d, 16)
        copy = remote(gg_st.at[to], gg_r.at[d - 1], gsend.at[d - 1], grecv.at[d - 1], {"wide": to})
        copy.start()
        copies.append(copy)
    ticks.at("end")
    total = gg_st[pc.w]
    for d in range(1, 16):
        copies[d - 1].wait_recv()
        total = total + gg_r[d - 1]
    gg_c[0] = total
    to_core = remote(gg_c.at[0], gg_c.at[1], gsend.at[15], grecv.at[15], pc.other)
    to_core.start()
    ticks.at("gains")
    to_core.wait()
    gg_out[...] = gg_c[0] + gg_c[1]
    for copy in copies:
        copy.wait_send()


def tail_kernel(*refs):
    gg_ref, stage, sem = refs[9], refs[21:30], refs[30]
    into = [pltpu.make_async_copy(refs[k], stage[k], sem.at[0, k]) for k in range(9)]
    out_of = [pltpu.make_async_copy(stage[k], refs[10 + k], sem.at[1, k]) for k in range(9)]
    for copy in into:
        copy.start()
    for n in range(2):
        out = refs[19 + n]
        out[...] = jnp.sum(gg_ref[8 * n : 8 * n + 3, :], axis=0, keepdims=True)[:, : out.shape[1]]
    for first, second in zip(into, out_of):
        first.wait()
        second.start()
    for copy in out_of:
        copy.wait()


def shape(dims, dtype=BF):
    return jax.ShapeDtypeStruct(dims, dtype)


def fast_body(tokens, seq_lengths, w_query, w_key, w_value, w_out, w_gate, w_up, w_down, attn_gain, ffn_gain, cotangent):
    tok, width = tokens.shape
    any_spec, vmem_spec = pl.BlockSpec(memory_space=pl.ANY), pl.BlockSpec(memory_space=pltpu.VMEM)
    dma = pltpu.SemaphoreType.DMA
    vm = pltpu.VMEM
    fore = pl.pallas_call(
        fore_kernel,
        out_shape=[
            shape((tok, width)), shape((tok, width)), shape((tok, width)), shape((tok, width)), shape((tok, width)),
            shape((width, tok)), shape((tok, 128), F32), shape((2, tok, 128)), shape((2, tok, 128), F32),
            shape((4, 4, 48, 2304)), shape((tok, width), F32), shape((8, width), F32), shape((8, width), F32), shape((tok, width)),
            shape((4, 4, 4, 48, 512)), shape((4, 4, 128, 384)), shape((4, 4, 48, 384)),
        ],
        in_specs=[pl.BlockSpec(memory_space=pltpu.SMEM)] + [vmem_spec] * 4 + [any_spec] * 7,
        out_specs=[any_spec] * 17,
        scratch_shapes=[
            vm((4, 4, 48, 2304), BF), vm((4, 4, 48, 768), BF), vm((4, 4, 48, 4096), BF), vm((4, 4, 128, 768), BF), vm((16, 8, 128), F32), vm((8, width), F32),
            vm((tok, width), F32), vm((tok, width), F32), vm((tok, width), F32), vm((width, tok), BF),
            vm((tok, width), BF), vm((tok, width), BF), vm((tok, width), BF), vm((tok, width), BF),
            vm((tok, 128), F32), vm((2, tok, 128), BF), vm((2, tok, 128), F32),
            vm((512, tok), BF), vm((tok, 1024), BF), vm((8, width), F32), vm((tok, width), BF),
            vm((2, 4, 4, 48, 1024), BF), vm((2, 4, 128, 768), BF), vm((4, 4, 48, 768), BF),
            vm((4, 4, 4, 48, 512), BF), vm((4, 4, 128, 384), BF), vm((4, 4, 48, 384), BF),
            dma((31,)), dma((31,)), dma((7, 10)), dma((7, 10)), dma((15,)), dma((15,)), dma((9,)), dma((9,)), dma((19,)), dma((24,)),
        ],
        compiler_params=pltpu.CompilerParams(collective_id=0, has_side_effects=True, vmem_limit_bytes=VMEM_BYTES),
        name="fore",
    )
    (q, k, v, o, do, h1t, lse, seg, rope, wqkv, dx2, gains, gg2, output, gu_sum, d_sum, o_sum) = fore(
        seq_lengths, tokens, cotangent, attn_gain[None], ffn_gain[None], w_query, w_key, w_value, w_out, w_gate, w_up, w_down
    )
    hind = pl.pallas_call(
        hind_kernel,
        out_shape=[shape((tok, width))] + [shape((48, width), F32)] * 4 + [shape((48, 2048), F32)] * 2 + [shape((128, width), F32), shape((16, 128), F32)],
        in_specs=[any_spec] * 12 + [vmem_spec] * 2 + [any_spec] * 3,
        out_specs=[vmem_spec] * 9,
        scratch_shapes=[
            vm((tok, width), BF), vm((tok, width), BF), vm((tok, width), BF), vm((tok, width), BF), vm((tok, width), BF),
            vm((tok, 128), F32), vm((2, tok, 128), BF), vm((2, tok, 128), F32), vm((width, tok), BF), vm((4, 4, 48, 2304), BF),
            vm((tok, width), BF), vm((tok, width), F32), vm((tok, 2304), BF), vm((tok, 128), F32), vm((tok, 128), F32),
            vm((6, 4, 4, 48, 384), BF), vm((3, 4, 4, 48, 384), BF),
            vm((4, 4, 2, 48, 512), BF), vm((4, 4, 2, 48, 512), BF), vm((4, 4, 48, 512), BF), vm((4, 3, 48, 512), BF), vm((4, 2, 48, 512), F32),
            vm((4, 2, 128, 384), BF), vm((4, 2, 128, 384), BF), vm((4, 128, 384), BF), vm((3, 128, 384), BF), vm((2, 128, 384), F32),
            vm((4, 2, 48, 384), BF), vm((4, 2, 48, 384), BF), vm((4, 48, 384), BF), vm((3, 48, 384), BF), vm((2, 48, 384), F32),
            vm((3, 4, 2, 48, 384), BF), vm((3, 4, 2, 48, 384), BF), vm((3, 4, 48, 384), BF), vm((3, 3, 48, 384), BF), vm((3, 2, 48, 384), F32),
            vm((8, width), F32), vm((16, 16, 128), F32), vm((15, 16, 128), F32), vm((2, 16, 128), F32),
            dma((12,)), dma((6, 2)), dma((9, 7)), dma((9, 7)), dma((3,)), dma((3,)), dma((16,)), dma((16,)),
        ],
        compiler_params=pltpu.CompilerParams(collective_id=1, has_side_effects=True, vmem_limit_bytes=VMEM_BYTES),
        name="hind",
    )
    gx, gwq, gwk, gwv, gwo, gwg, gwu, gwd, gg = hind(q, k, v, o, do, lse, seg, rope, h1t, wqkv, tokens, dx2, gains, gg2, gu_sum, d_sum, o_sum)
    count = attn_gain.shape[0]
    large = (gwq, gwk, gwv, gwo, gwg, gwu, gwd, output, gx)
    outs = pl.pallas_call(
        tail_kernel,
        out_shape=[shape(a.shape, a.dtype) for a in large] + [shape((1, count), F32)] * 2,
        in_specs=[any_spec] * 9 + [vmem_spec],
        out_specs=[any_spec] * 9 + [vmem_spec] * 2,
        scratch_shapes=[vm(a.shape, a.dtype) for a in large] + [dma((2, 9))],
        compiler_params=pltpu.CompilerParams(vmem_limit_bytes=VMEM_BYTES),
        name="tail",
    )(*large, gg)
    return (outs[7], outs[8], *outs[:7], outs[9][0], outs[10][0])


def layout(lengths, tok_count):
    slots = jnp.arange(lengths.shape[0])
    seq_ends = jnp.sum(jnp.where(slots[:, None] <= slots[None, :], lengths[:, None], 0), axis=0)
    starts = seq_ends - lengths
    places = jnp.arange(tok_count, dtype=jnp.int32)
    segment = jnp.sum((places[:, None] >= seq_ends[None, :]).astype(jnp.int32), axis=1)
    slot_ids = jnp.arange(lengths.shape[0], dtype=jnp.int32)
    starts_at = jnp.sum(
        jnp.where(segment[:, None] == slot_ids[None, :], starts[None, :], 0), axis=1
    )
    return (segment, places - starts_at)


def rope_tables(positions, head_dim):
    half_dim = head_dim // 2
    column = jnp.arange(half_dim, dtype=jnp.float32)
    frequency = jnp.exp(column * (-2.0 * math.log(10000.0) / head_dim))
    angles = positions.astype(jnp.float32)[:, None] * frequency[None, :]
    angles = jnp.concatenate([angles, angles], axis=1)
    return (jnp.cos(angles), jnp.sin(angles))


def rotate(values, cosine, sine):
    half_dim = values.shape[-1] // 2
    turned = jnp.concatenate([-values[..., half_dim:], values[..., :half_dim]], axis=-1)
    return values * cosine[:, None, :] + turned * sine[:, None, :]


def norm_gain(values, gain):
    return values * lax.rsqrt(jnp.mean(values * values, axis=-1, keepdims=True) + EPS) * gain


def swiglu(gate, upward):
    return jax.nn.silu(gate) * upward


def outer_sum(left, right):
    return lax.dot_general(
        left, right, (((0,), (0,)), ((), ())), preferred_element_type=jnp.float32
    )


def back_dot(rows_in, weight):
    return lax.dot_general(
        rows_in, weight, (((1,), (1,)), ((), ())), preferred_element_type=jnp.float32
    )


def block_scores(query_blk, key_rows, segment, row_index, row_start, scale):
    blk_rows = query_blk.shape[0]
    scores = (
        jnp.einsum("qhd,khd->hqk", query_blk, key_rows, preferred_element_type=jnp.float32) * scale
    )
    seg_blk = segment[row_start : row_start + blk_rows]
    row_blk = row_index[row_start : row_start + blk_rows]
    allowed = (seg_blk[:, None] == segment[None, :]) & (row_index[None, :] <= row_blk[:, None])
    return jnp.where(allowed[None], scores, -1e30)


def attend_forward(queries, key_rows, value_rows, segment):
    tok_count, head_count, head_dim = queries.shape
    scale = head_dim ** (-0.5)
    block_rows = min(512, tok_count)
    row_index = jnp.arange(tok_count, dtype=jnp.int32)
    outputs, totals = ([], [])
    for row_start in range(0, tok_count, block_rows):
        query_blk = queries[row_start : row_start + block_rows]
        scores = block_scores(query_blk, key_rows, segment, row_index, row_start, scale)
        peak = jnp.max(scores, axis=-1, keepdims=True)
        expd = jnp.exp(scores - peak)
        row_mass = jnp.sum(expd, axis=-1, keepdims=True)
        probs_low = (expd / row_mass).astype(jnp.bfloat16)
        outputs.append(
            jnp.einsum("hqk,khd->qhd", probs_low, value_rows, preferred_element_type=jnp.float32)
        )
        totals.append(peak[..., 0] + jnp.log(row_mass[..., 0]))
    return (jnp.concatenate(outputs, axis=0), jnp.concatenate(totals, axis=1))


def attend_backward(queries, key_rows, value_rows, log_total, grad_rows, segment):
    tok_count, head_count, head_dim = queries.shape
    scale = head_dim ** (-0.5)
    block_rows = min(512, tok_count)
    row_index = jnp.arange(tok_count, dtype=jnp.int32)
    grad_keys = jnp.zeros((tok_count, head_count, head_dim), jnp.float32)
    grad_values = jnp.zeros((tok_count, head_count, head_dim), jnp.float32)
    grad_queries = []
    for row_start in range(0, tok_count, block_rows):
        query_blk = queries[row_start : row_start + block_rows]
        grad_blk = grad_rows[row_start : row_start + block_rows]
        scores = block_scores(query_blk, key_rows, segment, row_index, row_start, scale)
        probs = jnp.exp(scores - log_total[:, row_start : row_start + block_rows, None])
        probs_low = probs.astype(jnp.bfloat16)
        grad_probs = jnp.einsum(
            "qhd,khd->hqk", grad_blk, value_rows, preferred_element_type=jnp.float32
        )
        inner = jnp.sum(probs * grad_probs, axis=-1, keepdims=True)
        grad_scores = (probs * (grad_probs - inner)).astype(jnp.bfloat16)
        grad_queries.append(
            jnp.einsum("hqk,khd->qhd", grad_scores, key_rows, preferred_element_type=jnp.float32)
            * scale
        )
        grad_keys = (
            grad_keys
            + jnp.einsum("hqk,qhd->khd", grad_scores, query_blk, preferred_element_type=jnp.float32)
            * scale
        )
        grad_values = grad_values + jnp.einsum(
            "hqk,qhd->khd", probs_low, grad_blk, preferred_element_type=jnp.float32
        )
    return (jnp.concatenate(grad_queries, axis=0), grad_keys, grad_values)


def plain_body(
    tokens,
    seq_lengths,
    w_query,
    w_key,
    w_value,
    w_out,
    w_gate,
    w_up,
    w_down,
    attn_gain,
    ffn_gain,
    cotangent,
):
    gathered = (
        lax.all_gather(w_query, "wide", axis=0, tiled=True),
        lax.all_gather(w_key, "wide", axis=0, tiled=True),
        lax.all_gather(w_value, "wide", axis=0, tiled=True),
        lax.all_gather(w_out, "wide", axis=0, tiled=True),
        lax.all_gather(w_gate, "wide", axis=0, tiled=True),
        lax.all_gather(w_up, "wide", axis=0, tiled=True),
        lax.all_gather(w_down, "wide", axis=0, tiled=True),
        lax.all_gather(attn_gain, "wide", axis=0, tiled=True),
        lax.all_gather(ffn_gain, "wide", axis=0, tiled=True),
    )
    (
        full_query,
        full_key,
        full_value,
        full_out,
        full_gate,
        full_up,
        full_down,
        gain_one,
        gain_two,
    ) = gathered
    gain_one = gain_one.astype(jnp.float32)
    gain_two = gain_two.astype(jnp.float32)
    tok_count, d_model = tokens.shape
    head_count = HEADS
    head_dim = d_model // head_count
    segment, positions = layout(seq_lengths[0], tok_count)
    cosine, sine = rope_tables(positions, head_dim)
    inputs = tokens.astype(jnp.float32)
    h_one = norm_gain(inputs, gain_one).astype(jnp.bfloat16)
    q_pre = jnp.dot(h_one, full_query, preferred_element_type=jnp.float32).reshape(
        tok_count, head_count, head_dim
    )
    k_pre = jnp.dot(h_one, full_key, preferred_element_type=jnp.float32).reshape(
        tok_count, head_count, head_dim
    )
    queries = rotate(q_pre, cosine, sine).astype(jnp.bfloat16)
    key_rows = rotate(k_pre, cosine, sine).astype(jnp.bfloat16)
    value_rows = (
        jnp.dot(h_one, full_value, preferred_element_type=jnp.float32)
        .astype(jnp.bfloat16)
        .reshape(tok_count, head_count, head_dim)
    )
    attended, log_total = attend_forward(queries, key_rows, value_rows, segment)
    attended = attended.reshape(tok_count, d_model).astype(jnp.bfloat16)
    middle = inputs + jnp.dot(attended, full_out, preferred_element_type=jnp.float32)
    h_two = norm_gain(middle, gain_two).astype(jnp.bfloat16)
    gate = jnp.dot(h_two, full_gate, preferred_element_type=jnp.float32)
    upward = jnp.dot(h_two, full_up, preferred_element_type=jnp.float32)
    hidden = swiglu(gate, upward).astype(jnp.bfloat16)
    result = middle + jnp.dot(hidden, full_down, preferred_element_type=jnp.float32)
    output = result.astype(jnp.bfloat16)
    grad_out_rows = cotangent.astype(jnp.float32)
    grad_down = outer_sum(hidden, cotangent)
    grad_hidden = back_dot(cotangent, full_down)
    mix_value, mix_back = jax.vjp(swiglu, gate, upward)
    grad_gate_f, grad_up_f = mix_back(grad_hidden)
    grad_gate_rows = grad_gate_f.astype(jnp.bfloat16)
    grad_up_rows = grad_up_f.astype(jnp.bfloat16)
    grad_gate = outer_sum(h_two, grad_gate_rows)
    grad_up = outer_sum(h_two, grad_up_rows)
    grad_h_two = back_dot(grad_gate_rows, full_gate) + back_dot(grad_up_rows, full_up)
    norm_value_two, norm_back_two = jax.vjp(norm_gain, middle, gain_two)
    grad_mid_norm, grad_gain_two = norm_back_two(grad_h_two)
    grad_middle = grad_out_rows + grad_mid_norm
    grad_mid_low = grad_middle.astype(jnp.bfloat16)
    grad_out_proj = outer_sum(attended, grad_mid_low)
    grad_attended = (
        back_dot(grad_mid_low, full_out)
        .astype(jnp.bfloat16)
        .reshape(tok_count, head_count, head_dim)
    )
    grad_q, grad_k, grad_v = attend_backward(
        queries, key_rows, value_rows, log_total, grad_attended, segment
    )
    rot_value, rot_back = jax.vjp(lambda turned_in: rotate(turned_in, cosine, sine), q_pre)
    grad_q_pre = rot_back(grad_q)[0].astype(jnp.bfloat16).reshape(tok_count, d_model)
    grad_k_pre = rot_back(grad_k)[0].astype(jnp.bfloat16).reshape(tok_count, d_model)
    grad_v_low = grad_v.astype(jnp.bfloat16).reshape(tok_count, d_model)
    grad_query = outer_sum(h_one, grad_q_pre)
    grad_key = outer_sum(h_one, grad_k_pre)
    grad_value = outer_sum(h_one, grad_v_low)
    grad_h_one = (
        back_dot(grad_q_pre, full_query)
        + back_dot(grad_k_pre, full_key)
        + back_dot(grad_v_low, full_value)
    )
    norm_value_one, norm_back_one = jax.vjp(norm_gain, inputs, gain_one)
    grad_in_norm, grad_gain_one = norm_back_one(grad_h_one)
    grad_tokens = (grad_middle + grad_in_norm).astype(jnp.bfloat16)
    wide_shares = (
        lax.psum_scatter(grad_query, "wide", scatter_dimension=0, tiled=True),
        lax.psum_scatter(grad_key, "wide", scatter_dimension=0, tiled=True),
        lax.psum_scatter(grad_value, "wide", scatter_dimension=0, tiled=True),
        lax.psum_scatter(grad_out_proj, "wide", scatter_dimension=0, tiled=True),
        lax.psum_scatter(grad_gate, "wide", scatter_dimension=0, tiled=True),
        lax.psum_scatter(grad_up, "wide", scatter_dimension=0, tiled=True),
        lax.psum_scatter(grad_down, "wide", scatter_dimension=0, tiled=True),
        lax.psum_scatter(grad_gain_one, "wide", scatter_dimension=0, tiled=True),
        lax.psum_scatter(grad_gain_two, "wide", scatter_dimension=0, tiled=True),
    )
    summed = (
        lax.psum(wide_shares[0].astype(jnp.bfloat16), "narrow").astype(jnp.float32),
        lax.psum(wide_shares[1].astype(jnp.bfloat16), "narrow").astype(jnp.float32),
        lax.psum(wide_shares[2].astype(jnp.bfloat16), "narrow").astype(jnp.float32),
        lax.psum(wide_shares[3].astype(jnp.bfloat16), "narrow").astype(jnp.float32),
        lax.psum(wide_shares[4].astype(jnp.bfloat16), "narrow").astype(jnp.float32),
        lax.psum(wide_shares[5].astype(jnp.bfloat16), "narrow").astype(jnp.float32),
        lax.psum(wide_shares[6].astype(jnp.bfloat16), "narrow").astype(jnp.float32),
        lax.psum(wide_shares[7].astype(jnp.bfloat16), "narrow").astype(jnp.float32),
        lax.psum(wide_shares[8].astype(jnp.bfloat16), "narrow").astype(jnp.float32),
    )
    return (
        output,
        grad_tokens,
        summed[0],
        summed[1],
        summed[2],
        summed[3],
        summed[4],
        summed[5],
        summed[6],
        summed[7],
        summed[8],
    )


def solution(mesh):
    in_specs = (
        P(("wide", "narrow"), None),
        P(("wide", "narrow"), None),
        P("wide", None),
        P("wide", None),
        P("wide", None),
        P("wide", None),
        P("wide", None),
        P("wide", None),
        P("wide", None),
        P("wide"),
        P("wide"),
        P(("wide", "narrow"), None),
    )
    out_specs = (
        P(("wide", "narrow"), None),
        P(("wide", "narrow"), None),
        P("wide", None),
        P("wide", None),
        P("wide", None),
        P("wide", None),
        P("wide", None),
        P("wide", None),
        P("wide", None),
        P("wide"),
        P("wide"),
    )
    blocks = (mesh.shape["wide"], mesh.shape["narrow"]) == (16, 2)
    body = fast_body if blocks else plain_body
    return jax.shard_map(body, mesh=mesh, in_specs=in_specs, out_specs=out_specs, check_vma=False)
```

```python
import functools
import math

import jax
import jax.numpy as jnp
from jax import lax
from jax.experimental import pallas as pl
from jax.experimental.pallas import tpu as pltpu
from jax.sharding import PartitionSpec as P

HEADS = 12
EPS = 1e-06
NEG = -1e30
BF = jnp.bfloat16
F32 = jnp.float32
MESH = pl.DeviceIdType.MESH
VMEM_BYTES = 60 * 2**20


def nn(left, right):
    return jnp.dot(left, right, preferred_element_type=F32)


def nt(left, right):
    return lax.dot_general(left, right, (((1,), (1,)), ((), ())), preferred_element_type=F32)


def flat(values):
    return values.reshape(-1, values.shape[-1])


def sigmoid(v):
    return 1.0 / (1.0 + jnp.exp(-v))


def three_way(v):
    high = v.astype(BF)
    rest = v - high.astype(F32)
    mid = rest.astype(BF)
    return high, mid, (rest - mid.astype(F32)).astype(BF)


ENTER, T, N, P_, A, M, F, B, W, L, END, GAINS = 0, 10, 20, 100, 200, 300, 400, 900, 910, 920, 930, 931
Q0, Q1, Q2, O, D0, D1, G0, G1, G2, G3, D = range(0, 1100, 100)
FORE = [
    (ENTER, [Q0 + 0]),
    (T + 1, [Q0 + 13]),
    (T + 2, [Q0 + 12, Q0 + 20, Q0 + 11]),
    (N + 0, [Q0 + 23]),
    (N + 1, [Q0 + 22, Q0 + 40, Q1 + 0]),
    (N + 2, [Q0 + 21, Q0 + 30, Q2 + 0, Q0 + 33]),
    (N + 3, [Q0 + 31, Q0 + 43, Q0 + 42]),
    (P_ + 0, [Q0 + 32, Q0 + 41, Q0 + 5]),
    (P_ + 1, [Q1 + 1]),
    (P_ + 3, [O + 0]),
    (A + 2, [Q1 + 2]),
    (A + 3, [Q2 + 1]),
    (A + 10, [Q1 + 3]),
    (A + 11, [D0 + 0, O + 1]),
    (A + 12, [Q1 + 4, Q2 + 2]),
    (P_ + 10, [Q1 + 5, Q2 + 3]),
    (P_ + 11, [D1 + 0]),
    (P_ + 12, [O + 2]),
    (A + 21, [D0 + 1]),
    (A + 22, [G0 + 0]),
    (A + 30, [D1 + 1]),
    (A + 31, [O + 4, Q2 + 4]),
    (A + 32, [D0 + 2]),
    (P_ + 20, [G0 + 1, Q2 + 5]),
    (A + 40, [G1 + 0]),
    (A + 43, [O + 3, D1 + 2, D0 + 3]),
    (A + 50, [D1 + 3, G0 + 2, D0 + 4]),
    (A + 51, [O + 5, G2 + 0]),
    (A + 52, [G1 + 1]),
    (A + 53, [G3 + 0]),
    (M + 0, [G0 + 3]),
    (M + 1, [D1 + 4]),
    (M + 2, [D0 + 5]),
    (M + 3, [G0 + 4, D1 + 5]),
    (F + 0, [G1 + 2, G2 + 1, G0 + 5]),
    (F + 10, [G3 + 1]),
    (F + 11, [G1 + 3]),
    (F + 12, [G1 + 4]),
    (F + 13, [G2 + 2]),
    (F + 100, [G1 + 5]),
    (F + 101, [G2 + 3]),
    (F + 102, [G3 + 2, G3 + 3]),
    (F + 111, [G2 + 4]),
    (F + 113, [G3 + 4]),
    (F + 121, [G2 + 5]),
    (F + 220, [G3 + 5]),
]
HIND = [
    (ENTER, [G0 + 1, G1 + 1]),
    (A + 3, [G0 + 2, O + 1]),
    (W + 0, [G1 + 2]),
    (A + 10, [D + 1]),
    (A + 11, [G0 + 3]),
    (A + 13, [O + 2]),
    (W + 1, [G1 + 3]),
    (W + 1, [G2 + 1]),
    (A + 31, [D + 2]),
    (A + 32, [O + 3]),
    (W + 3, [G2 + 2]),
    (W + 3, [G3 + 1]),
    (A + 40, [Q0 + 1, D + 3]),
    (W + 4, [G2 + 3]),
    (A + 51, [G3 + 2, Q1 + 1]),
    (A + 52, [Q0 + 2]),
    (W + 5, [G3 + 3]),
    (L + 0, [Q1 + 2]),
    (L + 1, [Q0 + 3]),
    (L + 2, [Q2 + 1, Q1 + 3]),
    (L + 3, [G1 + 4]),
    (END, [G0 + 4, D + 4, Q2 + 2, O + 4, Q0 + 4, O + 5, G2 + 4, Q2 + 3, D + 5, Q1 + 4, G3 + 4, G0 + 5, G2 + 5, G1 + 5, Q0 + 5, G3 + 5, Q1 + 5, Q2 + 4, Q2 + 5]),
]


class Place:
    def __init__(self):
        wide = lax.axis_index("wide")
        self.c = lax.axis_index("narrow")
        self.w = wide
        self.z = wide // 4
        self.p = lax.rem(wide, 4)
        across_y = lax.rem(self.p + 2, 4)
        across_x = self.p + 1 - 2 * lax.rem(self.p, 2)
        self.q1 = (1 - self.c) * across_y + self.c * across_x
        self.q2 = (1 - self.c) * across_x + self.c * across_y
        self.q3 = 3 - self.p
        self.first = {"wide": self.z * 4 + self.q1}
        self.second = {"wide": self.z * 4 + self.q2}
        self.other = {"narrow": 1 - self.c}

    def z_at(self, d):
        return lax.rem(self.z + d + 4, 4)

    def z_dev(self, d):
        return {"wide": self.z_at(d) * 4 + self.p}


def enter(place):
    sem = pltpu.get_barrier_semaphore()
    for d in range(1, 16):
        pl.semaphore_signal(sem, inc=1, device_id={"wide": lax.rem(place.w + d, 16)}, device_id_type=MESH)
    pl.semaphore_signal(sem, inc=1, device_id=place.other, device_id_type=MESH)
    pl.semaphore_wait(sem, 16)


def remote(src, dst, send, recv, device):
    return pltpu.make_async_remote_copy(
        src_ref=src, dst_ref=dst, send_sem=send, recv_sem=recv, device_id=device, device_id_type=MESH
    )


def lane_of(rows, lanes=128):
    return lax.broadcasted_iota(jnp.int32, (rows, lanes), 1)


def spread(index):
    row = lax.broadcasted_iota(jnp.int32, (128, 768), 0)
    col = lax.broadcasted_iota(jnp.int32, (128, 768), 1)
    return jnp.where((col == row + 48 * index) & (row < 48), 1.0, 0.0).astype(BF)


class Gather:
    def __init__(self, place, buf, start, width, rows, send, recv):
        self.place = place
        r0, rn = rows

        def part(z, q, core):
            col = pl.ds(pl.multiple_of(start + core * width, 128), width)
            return buf.at[z, q, pl.ds(r0, rn), col]

        def block(q, core):
            col = pl.ds(pl.multiple_of(start + core * width, 128), width)
            return buf.at[:, q, pl.ds(r0, rn), col]

        self.part, self.block, self.send, self.recv = part, block, send, recv

    def copy(self, k, ref, device):
        return remote(ref, ref, self.send.at[k], self.recv.at[k], device)


def block_steps(unit):
    pc = unit.place
    me = pc.c
    zs = [unit.copy(d - 1, unit.part(pc.z, pc.p, me), pc.z_dev(d)) for d in (1, 2, 3)]
    own = unit.block(pc.p, me)
    to_first = unit.copy(3, own, pc.first)
    to_second = unit.copy(4, own, pc.second)
    on_second = unit.copy(5, unit.block(pc.q1, me), pc.second)
    cores = [unit.copy(6 + i, unit.block(q, me), pc.other) for i, q in enumerate((pc.p, pc.q1, pc.q2, pc.q3))]

    def s0():
        for copy in zs:
            copy.start()

    def s1():
        for copy in zs:
            copy.wait_recv()
        to_first.start()
        to_second.start()
        cores[0].start()

    def s2():
        to_first.wait_recv()
        on_second.start()
        cores[1].start()

    def s3():
        to_second.wait_recv()
        cores[2].start()

    def s4():
        on_second.wait_recv()
        cores[3].start()

    def s5():
        for copy in cores:
            copy.wait_recv()
        for copy in [*zs, to_first, to_second, on_second, *cores]:
            copy.wait_send()

    return [s0, s1, s2, s3, s4, s5]


def piece_steps(unit):
    pc = unit.place
    me = pc.c
    planes = (pc.p, pc.q1, pc.q2, pc.q3)
    zs = [unit.copy(d - 1, unit.part(pc.z, pc.p, me), pc.z_dev(d)) for d in (1, 2, 3)]
    first = [unit.copy(3 + d, unit.part(pc.z_at(-d), pc.p, me), pc.first) for d in range(4)]
    second = [unit.copy(7 + d, unit.part(pc.z_at(-d), pc.p, me), pc.second) for d in range(4)]
    onward = [unit.copy(11 + d, unit.part(pc.z_at(-d), pc.q1, me), pc.second) for d in range(4)]
    cores = [[unit.copy(15 + 4 * i + d, unit.part(pc.z_at(-d), q, me), pc.other) for d in range(4)] for i, q in enumerate(planes)]

    def spread_out(d):
        first[d].start()
        second[d].start()
        cores[0][d].start()

    def s0():
        for copy in zs:
            copy.start()
        spread_out(0)

    def p(d):
        zs[d - 1].wait_recv()
        spread_out(d)

    def a(d):
        first[d].wait_recv()
        onward[d].start()
        cores[1][d].start()

    def b(d):
        second[d].wait_recv()
        cores[2][d].start()

    def c(d):
        onward[d].wait_recv()
        cores[3][d].start()

    def s5():
        for line in cores:
            for copy in line:
                copy.wait_recv()
        for copy in [*zs, *first, *second, *onward, *sum(cores, [])]:
            copy.wait_send()

    steps = {0: s0, 5: s5}
    for number, step in ((10, p), (20, a), (30, b), (40, c)):
        for d in range(4):
            steps[number + d] = functools.partial(step, d)
    del steps[10]
    return steps


class Ticks:
    def __init__(self, table, steps):
        self.steps = steps
        self.table = {}
        for place, listed in table:
            self.table[place] = self.table.get(place, []) + listed
        assert sorted(sum(self.table.values(), [])) == sorted(steps)

    def at(self, place):
        for step in self.table.get(place, []):
            self.steps[step]()

    def when(self, index, places):
        for k, place in enumerate(places):
            if place in self.table:
                pl.when(index == k)(functools.partial(self.at, place))


def turned(values, lane, back):
    up = pltpu.roll(values, 96, 1)
    down = pltpu.roll(values, 32, 1)
    low = lax.rem(lane, 64) < 32
    return jnp.where(low, up, -down) if back else jnp.where(low, -up, down)


def fore_kernel(
    lens, x_ref, dy_ref, g1_ref, g2_ref, wq, wk, wv, wo, wg, wu, wd,
    q_out, k_out, v_out, o_out, do_out, h1t_out, lse_out, seg_out, rope_out, w_out, dx2_out, gain_out, gg_out, y_out, gu_sum, d_sum, o_sum, gu_first,
    w_s, wo_s, wgu_s, wd_s, gain_s, gains, x2_s, y_s, dh2_s, h1t_s, q_s, k_s, v_s, o_s, lse_s, seg_s, rope_s,
    hidt_s, dgu_s, gg_s, yb_s, gu_st, d_st, o_st, gu_r, d_r, o_r,
    wsend, wrecv, usend, urecv, gsend, grecv, rsend, rrecv, lsem, osem,
):
    pc = Place()
    tok = x_ref.shape[0]
    blocks = tok // 256
    loads = []

    def load(src, dst):
        copy = pltpu.make_async_copy(src, dst, lsem.at[len(loads)])
        copy.start()
        loads.append(copy)

    def half(start, width):
        return pl.ds(pl.multiple_of(start + pc.c * width, 128), width)

    for m in range(3):
        for n, w in enumerate((wq, wk, wv)):
            load(w.at[:, half(m * 256, 128)], w_s.at[m, pc.z, pc.p, :, pl.ds(pl.multiple_of(pc.c * 384 + n * 128, 128), 128)])
    early = len(loads)
    load(wo.at[:, half(0, 384)], wo_s.at[pc.z, pc.p, :, half(0, 384)])
    load(wd.at[:, half(0, 384)], wd_s.at[pc.z, pc.p, :, half(0, 384)])
    for u in range(4):
        for n, w in enumerate((wg, wu)):
            load(w.at[:, half(u * 512, 256)], wgu_s.at[pc.z, pc.p, :, pl.ds(pl.multiple_of(u * 1024 + n * 256 + pc.c * 512, 128), 256)])
    enter(pc)
    for copy in loads[:early]:
        copy.wait()
    gain_s[pc.w] = jnp.zeros((8, 128), F32)
    for n, ref in enumerate((g1_ref, g2_ref)):
        gain_s[pc.w, n : n + 1, 0 : ref.shape[1]] = ref[...].astype(F32)
    gain_copies = [
        remote(gain_s.at[pc.w], gain_s.at[pc.w], gsend.at[d - 1], grecv.at[d - 1], {"wide": lax.rem(pc.w + d, 16)}) for d in range(1, 16)
    ]
    for copy in gain_copies:
        copy.start()
    ends, total = [], jnp.int32(0)
    for s in range(4):
        total = total + lens[0, s]
        ends.append(total)

    def tables(r, carry):
        rs = pl.ds(pl.multiple_of(r * 256, 256), 256)
        lane = lane_of(256)
        place = lax.broadcasted_iota(jnp.int32, (256, 128), 0) + r * 256
        seg = jnp.zeros((256, 128), jnp.int32)
        start = jnp.zeros((256, 128), jnp.int32)
        for s in range(4):
            past = place >= ends[s]
            seg = seg + past.astype(jnp.int32)
            start = jnp.where(past, ends[s], start)
        column = lax.rem(lane, 32).astype(F32)
        angle = (place - start).astype(F32) * jnp.exp(column * (-2.0 * math.log(10000.0) / 64))
        rope_s[0, rs, :] = jnp.cos(angle)
        rope_s[1, rs, :] = jnp.sin(angle)
        seg_s[0, rs, :] = jnp.where((lane == seg) | (lane >= 4), 0.0, NEG).astype(BF)
        seg_s[1, rs, :] = jnp.where((lane == seg) | ((lane >= 4) & (lane < 7)), 1.0, 0.0).astype(BF)
        return carry

    units = {
        Q1: Gather(pc, w_s.at[1], 0, 384, (0, 48), usend.at[7], urecv.at[7]),
        Q2: Gather(pc, w_s.at[2], 0, 384, (0, 48), usend.at[8], urecv.at[8]),
        O: Gather(pc, wo_s, 0, 384, (0, 48), usend.at[0], urecv.at[0]),
        D0: Gather(pc, wd_s, 0, 384, (0, 64), usend.at[1], urecv.at[1]),
        D1: Gather(pc, wd_s, 0, 384, (64, 64), usend.at[2], urecv.at[2]),
    }
    for u in range(4):
        units[G0 + 100 * u] = Gather(pc, wgu_s, 1024 * u, 512, (0, 48), usend.at[3 + u], urecv.at[3 + u])
    steps = {Q0 + k: step for k, step in piece_steps(Gather(pc, w_s.at[0], 0, 384, (0, 48), wsend, wrecv)).items()}
    for u, unit in units.items():
        for k, step in enumerate(block_steps(unit)):
            steps[u + k] = step
    ticks = Ticks(FORE, steps)
    ticks.at(ENTER)
    for copy in loads[early:]:
        copy.wait()
    ticks.at(T)
    lax.fori_loop(0, blocks // 2, tables, 0)
    ticks.at(T + 1)
    lax.fori_loop(blocks // 2, blocks, tables, 0)
    for copy in gain_copies:
        copy.wait_recv()
    ticks.at(T + 2)

    def gain_rows(w, rows):
        return rows + nn(gain_s[w].astype(BF), spread(w))

    gains[...] = lax.fori_loop(0, 16, gain_rows, jnp.zeros((8, 768), F32))
    h1_s = yb_s

    def norm(r, carry):
        ticks.when(r, range(N, N + 4))
        rs = pl.ds(pl.multiple_of(r * 256, 256), 256)
        x = x_ref[rs, :].astype(F32)
        h1 = (x * lax.rsqrt(jnp.mean(x * x, axis=1, keepdims=True) + EPS) * gains[0:1, :]).astype(BF)
        h1_s[rs, :] = h1
        h1t_s[:, rs] = h1.T
        return carry

    lax.fori_loop(0, blocks, norm, 0)
    outs = []

    def store(src, dst):
        copy = pltpu.make_async_copy(src, dst, osem.at[len(outs)])
        copy.start()
        outs.append(copy)
        return copy

    store(gains, gain_out)
    kept_h1t = store(h1t_s, h1t_out)
    store(seg_s, seg_out)
    store(rope_s, rope_out)

    def project(m, r, carry):
        for k in range(2):
            ticks.when(2 * m + r, [P_ + 10 * g + i for g in range(3) for i in (k, k + 2)])
        for k in range(2):
            rs = pl.ds(pl.multiple_of(r * 512 + k * 256, 256), 256)
            lane = lane_of(256)
            cos, sin = rope_s[0, rs, :], rope_s[1, rs, :]
            pre = nn(h1_s[rs, :], flat(w_s[m]))
            for n in range(2):
                cs = pl.ds(pl.multiple_of((2 * m + n) * 128, 128), 128)
                qp, kp, vp = (pre[:, n * 384 + t * 128 : n * 384 + (t + 1) * 128] for t in range(3))
                q_s[rs, cs] = (qp * cos + turned(qp, lane, False) * sin).astype(BF) * BF(0.125)
                k_s[rs, cs] = (kp * cos + turned(kp, lane, False) * sin).astype(BF)
                v_s[rs, cs] = vp.astype(BF)
        return carry

    def pair(j, carry):
        cs = pl.ds(pl.multiple_of(j * 128, 128), 128)
        lane = lane_of(256)
        below = lax.broadcasted_iota(jnp.int32, (256, 256), 0) >= lax.broadcasted_iota(jnp.int32, (256, 256), 1)
        for i in range(blocks):
            ticks.when(j, range(A + i, A + i + 60, 10))
            rs, before = pl.ds(i * 256, 256), pl.ds(0, i * 256)
            qt = q_s[rs, cs]
            parts = []
            for h in range(2):
                qm = jnp.where((lane < 64) == (h == 0), qt, BF(0))
                qm = jnp.concatenate([qm, seg_s[0, rs, :]], axis=1)
                sd = jnp.where(below, nt(qm, jnp.concatenate([k_s[rs, cs], seg_s[1, rs, :]], axis=1)), NEG)
                top = jnp.max(sd, axis=1, keepdims=True)
                if i:
                    so = nt(qm, jnp.concatenate([k_s[before, cs], seg_s[1, before, :]], axis=1))
                    top = jnp.maximum(top, jnp.max(so, axis=1, keepdims=True))
                pd = jnp.exp(sd - top)
                mass = jnp.sum(pd, axis=1, keepdims=True)
                acc = nn(pd.astype(BF), v_s[rs, cs])
                if i:
                    po = jnp.exp(so - top)
                    mass = mass + jnp.sum(po, axis=1, keepdims=True)
                    acc = acc + nn(po.astype(BF), v_s[before, cs])
                parts.append(acc * (1.0 / mass))
                lse_s[rs, :] = jnp.where(lane == 2 * j + h, top + jnp.log(mass), lse_s[rs, :])
            o_s[rs, cs] = jnp.where(lane < 64, parts[0], parts[1]).astype(BF)
        return carry

    def group(m, carry):
        lax.fori_loop(0, blocks // 2, functools.partial(project, m), 0)
        lax.fori_loop(2 * m, 2 * m + 2, pair, 0)
        return carry

    lse_s[...] = jnp.zeros_like(lse_s)
    lax.fori_loop(0, 3, group, 0)
    store(w_s, w_out)
    kept = [store(q_s, q_out), store(k_s, k_out), store(v_s, v_out), kept_h1t]
    store(o_s, o_out)
    store(lse_s, lse_out)
    for copy in kept:
        copy.wait()
    h2_s, h2t_s, dxb_s, do_s = q_s, h1t_s, k_s, v_s
    gain2 = gains[1:2, :]

    def middle(r, carry):
        ticks.when(r, range(M, M + 4))
        rs = pl.ds(pl.multiple_of(r * 256, 256), 256)
        x2 = x_ref[rs, :].astype(F32) + nn(o_s[rs, :], flat(wo_s[...]))
        x2_s[rs, :] = x2
        h2 = (x2 * lax.rsqrt(jnp.mean(x2 * x2, axis=1, keepdims=True) + EPS) * gain2).astype(BF)
        h2_s[rs, :] = h2
        h2t_s[:, rs] = h2.T
        return carry

    lax.fori_loop(0, blocks, middle, 0)

    def swap(buf, width, got, k):
        far = pl.ds(pl.multiple_of((1 - pc.c) * width, 128), width)
        return remote(buf.at[..., far], got, rsend.at[k], rrecv.at[k], pc.other)

    def near(buf, width):
        return buf[..., pl.ds(pl.multiple_of(pc.c * width, 128), width)]

    gu_swap = [swap(gu_st.at[u % 2], 512, gu_r.at[u], u) for u in range(4)]
    d_swap = [swap(d_st.at[u % 2], 384, d_r.at[u], 4 + u) for u in range(4)]

    ahead = []

    def settle(u):
        gu_swap[u].wait_recv()
        d_swap[u].wait_recv()
        for z in range(4):
            mine = gu_st[u % 2, z, :, :, pl.ds(pl.multiple_of(pc.c * 512, 128), 512)]
            gu_r[u, z] = (gu_r[u, z].astype(F32) + mine.astype(F32)).astype(BF)
        mine = d_st[u % 2, :, :, pl.ds(pl.multiple_of(pc.c * 384, 128), 384)]
        d_r[u] = (d_r[u].astype(F32) + mine.astype(F32)).astype(BF)
        store(gu_r.at[u], gu_sum.at[u])
        if u < 3:
            for k, q in enumerate((pc.q1, pc.q3)):
                copy = remote(gu_r.at[u, :, q], gu_first.at[u, :, k], rsend.at[9 + 2 * u + k], rrecv.at[9 + 2 * u + k], pc.first)
                copy.start()
                ahead.append(copy)
        store(d_r.at[u], d_sum.at[u])
        gu_swap[u].wait_send()
        d_swap[u].wait_send()

    for u in range(4):
        wgu = pl.ds(u * 1024, 1024)

        def mix(r, carry):
            for k in range(2):
                ticks.when(r, range(F + 100 * u + k, F + 100 * u + 4, 2))
            rs = pl.ds(pl.multiple_of(r * 512, 512), 512)
            both = nn(h2_s[rs, :], flat(wgu_s[:, :, :, wgu]))
            dhid = nt(dy_ref[rs, :], flat(wd_s[u]))
            hids, grads = [], []
            for n in range(2):
                gate, up = both[:, n * 512 : n * 512 + 256], both[:, n * 512 + 256 : n * 512 + 512]
                dh = dhid[:, n * 256 : n * 256 + 256]
                sig = sigmoid(gate)
                silu = gate * sig
                hids.append((silu * up).astype(BF))
                grads.append((dh * up * sig * (1.0 + gate * (1.0 - sig))).astype(BF))
                grads.append((dh * silu).astype(BF))
            hid = jnp.concatenate(hids, axis=1)
            dgu = jnp.concatenate(grads, axis=1)
            hidt_s[:, rs] = hid.T
            dgu_s[rs, :] = dgu
            yv = nn(hid, flat(wd_s[u]))
            dv = nt(dgu, flat(wgu_s[:, :, :, wgu]))
            if u == 0:
                y_s[rs, :] = x2_s[rs, :] + yv
                dh2_s[rs, :] = dv
            else:
                y_s[rs, :] += yv
                dh2_s[rs, :] += dv
            return carry

        lax.fori_loop(0, blocks // 2, mix, 0)
        if u >= 2:
            settle(u - 2)

        def weight_gu(z, carry):
            ticks.when(z, range(F + 100 * u + 10, F + 100 * u + 14))
            rows = nn(h2t_s[pl.ds(pl.multiple_of(z * 192, 64), 192), :], dgu_s[...])
            gu_st[u % 2, z] = rows.astype(BF).reshape(4, 48, 1024)
            return carry

        lax.fori_loop(0, 4, weight_gu, 0)

        def weight_d(k, carry):
            ticks.when(k, range(F + 100 * u + 20, F + 100 * u + 22))
            rows = nn(hidt_s[pl.ds(pl.multiple_of(k * 256, 256), 256), :], dy_ref[...])
            d_st[u % 2, pl.ds(k * 2, 2)] = rows.astype(BF).reshape(2, 128, 768)
            return carry

        lax.fori_loop(0, 2, weight_d, 0)
        gu_swap[u].start()
        d_swap[u].start()

    settle(2)
    gg_s[...] = jnp.zeros_like(gg_s)

    def back(r, carry):
        rs = pl.ds(pl.multiple_of(r * 256, 256), 256)
        yb_s[rs, :] = y_s[rs, :].astype(BF)
        x2, dh2 = x2_s[rs, :], dh2_s[rs, :]
        r2 = lax.rsqrt(jnp.mean(x2 * x2, axis=1, keepdims=True) + EPS)
        n2 = x2 * r2
        e2 = dh2 * gain2
        gg_s[0:1, :] += jnp.sum(dh2 * n2, axis=0, keepdims=True)
        dx2 = dy_ref[rs, :].astype(F32) + r2 * (e2 - n2 * jnp.mean(e2 * n2, axis=1, keepdims=True))
        x2_s[rs, :] = dx2
        dxb_s[rs, :] = dx2.astype(BF)
        h2t_s[:, rs] = o_s[rs, :].T
        return carry

    lax.fori_loop(0, blocks, back, 0)
    store(yb_s, y_out)
    store(x2_s, dx2_out)
    store(gg_s, gg_out)
    settle(3)

    def weight_o(z, carry):
        rows = nn(h2t_s[pl.ds(pl.multiple_of(z * 192, 64), 192), :], dxb_s[...])
        o_st[z] = rows.astype(BF).reshape(4, 48, 768)
        return carry

    lax.fori_loop(0, 4, weight_o, 0)
    o_swap = swap(o_st, 384, o_r, 8)
    o_swap.start()

    def back_out(r, carry):
        rs = pl.ds(pl.multiple_of(r * 256, 256), 256)
        do_s[rs, :] = nt(dxb_s[rs, :], flat(wo_s[...])).astype(BF)
        return carry

    lax.fori_loop(0, blocks, back_out, 0)
    store(do_s, do_out)
    o_swap.wait_recv()
    mine = o_st[:, :, :, pl.ds(pl.multiple_of(pc.c * 384, 128), 384)]
    o_r[...] = (o_r[...].astype(F32) + mine.astype(F32)).astype(BF)
    store(o_r, o_sum)
    o_swap.wait_send()
    for copy in ahead:
        copy.wait()
    for copy in gain_copies:
        copy.wait_send()
    for copy in outs:
        if not any(copy is done for done in kept):
            copy.wait()


class Reduce:
    def __init__(self, place, keep, r1, r2, r3, total, other_total, send, recv, far1, far2, near):
        pc = place
        self.pc, self.keep, self.r1, self.r2, self.r3, self.total = pc, keep, r1, r2, r3, total
        self.to_first = []
        if far1 is not None:
            self.to_first = [remote(ref, r1.at[:, i], send.at[i], recv.at[i], pc.first) for i, ref in enumerate((far1, far2))]
        self.near = near
        self.to_second = remote(keep.at[:, 1], r2, send.at[2], recv.at[2], pc.second)
        self.zs = [remote(keep.at[pc.z_at(d), 0], r3.at[d - 1], send.at[2 + d], recv.at[2 + d], pc.z_dev(d)) for d in (1, 2, 3)]
        self.to_core = remote(total, other_total, send.at[6], recv.at[6], pc.other)

    def steps(self, begin, finish):
        pc = self.pc

        def r1():
            begin()
            for copy in self.to_first:
                copy.start()

        def r2():
            for copy in self.near:
                copy.wait()
            for copy in self.to_first:
                copy.wait_recv()

            def add(z, carry):
                self.keep[z] = (self.keep[z].astype(F32) + self.r1[z].astype(F32)).astype(BF)
                return carry

            lax.fori_loop(0, 4, add, 0)
            self.to_second.start()

        def r3():
            self.to_second.wait_recv()

            def add(z, carry):
                self.keep[z, 0] = (self.keep[z, 0].astype(F32) + self.r2[z].astype(F32)).astype(BF)
                return carry

            lax.fori_loop(0, 4, add, 0)
            for copy in self.zs:
                copy.start()

        def r4():
            for copy in self.zs:
                copy.wait_recv()
            total = self.keep[pc.z, 0].astype(F32)
            for d in range(3):
                total = total + self.r3[d].astype(F32)
            self.total[...] = total
            self.to_core.start()

        def r5():
            self.to_core.wait()
            finish()
            for copy in [*self.to_first, self.to_second, *self.zs]:
                copy.wait_send()

        return [r1, r2, r3, r4, r5]


def hind_kernel(
    q_hbm, k_hbm, v_hbm, o_hbm, do_hbm, lse_hbm, seg_hbm, rope_hbm, h1t_hbm, w_hbm, x_hbm, dx2_hbm, gain_ref, gg_ref, gu_sum, d_sum, o_sum, gu_first,
    gx_ref, gwq, gwk, gwv, gwo, gwg, gwu, gwd, gg_out,
    q_s, k_s, v_s, o_s, do_s, lse_s, seg_s, rope_s, h1t_s, w_s, x_s, dx2_s, dqkv_s, dk_s, dv_s,
    gq_s, gq_r, gu_k, gu_1, gu_2, gu_3, gu_t, d_k, d_1, d_2, d_3, d_t, o_k, o_1, o_2, o_3, o_t, qk_k, qk_1, qk_2, qk_3, qk_t,
    gg1_s, gg_st, gg_r, gg_c,
    lsem, nsem, ssend, srecv, qsend, qrecv, gsend, grecv,
):
    pc = Place()
    tok = x_s.shape[0]
    blocks = tok // 256
    loads = []

    def load(src, dst):
        copy = pltpu.make_async_copy(src, dst, lsem.at[len(loads)])
        copy.start()
        loads.append(copy)
        return copy

    for src, dst in ((q_hbm, q_s), (k_hbm, k_s), (v_hbm, v_s), (o_hbm, o_s), (do_hbm, do_s), (lse_hbm, lse_s), (seg_hbm, seg_s), (rope_hbm, rope_s)):
        load(src, dst)
    early = len(loads)
    for src, dst in ((h1t_hbm, h1t_s), (w_hbm, w_s), (x_hbm, x_s), (dx2_hbm, dx2_s)):
        load(src, dst)
    enter(pc)

    nears = []

    def start_near(copies):
        for copy in copies:
            copy.start()

    def unit(n, parts, keep, r1, r2, r3, total, finish, source=None, done=None):
        near = []
        if source is None:
            near = [pltpu.make_async_copy(parts(q), keep.at[:, i], nsem.at[n, i]) for i, q in enumerate((pc.p, pc.q2))]
        far = (parts(pc.q1), parts(pc.q3))
        if done is not None:
            near.append(pltpu.make_async_copy(done, r1, nsem.at[n, 2]))
            far = (None, None)
        red = Reduce(pc, keep, r1, r2, r3, total.at[0], total.at[1], ssend.at[n], srecv.at[n], *far, near)

        def begin():
            if source is not None:
                source()
            start_near(near)

        return red.steps(begin, finish)

    def halves(ref):
        mine, others = ref[0], ref[1]
        zero = pc.c == 0
        return jnp.where(zero, mine, others), jnp.where(zero, others, mine)

    units = {}
    for u in range(4):

        def finish_gu(u=u):
            low, high = halves(gu_t.at[u])
            for n, part in enumerate((low, high)):
                gwg[:, pl.ds(u * 512 + n * 256, 256)] = part[:, :256]
                gwu[:, pl.ds(u * 512 + n * 256, 256)] = part[:, 256:]

        done = gu_first.at[u] if u < 3 else None
        units[G0 + 100 * u] = unit(u, lambda q, u=u: gu_sum.at[u, :, q], gu_k.at[u], gu_1.at[u], gu_2.at[u], gu_3.at[u], gu_t.at[u], finish_gu, done=done)

    def finish_o():
        low, high = halves(o_t)
        gwo[:, 0:384] = low
        gwo[:, 384:768] = high

    units[O] = unit(4, lambda q: o_sum.at[:, q], o_k, o_1, o_2, o_3, o_t, finish_o)

    def finish_d():
        low, high = halves(d_t)
        gwd[:, 0:384] = low
        gwd[:, 384:768] = high

    units[D] = unit(5, lambda q: d_sum.at[:, q], d_k, d_1, d_2, d_3, d_t, finish_d)

    q_swaps = [remote(gq_s.at[2 * m + 1 - pc.c], gq_r.at[m], qsend.at[m], qrecv.at[m], pc.other) for m in range(3)]

    for m in range(3):

        def finish_q(m=m):
            low, high = halves(qk_t.at[m])
            for n, part in enumerate((low, high)):
                cs = pl.ds((2 * m + n) * 128, 128)
                gwq[:, cs] = part[:, 0:128]
                gwk[:, cs] = part[:, 128:256]
                gwv[:, cs] = part[:, 256:384]

        def source(m=m):
            q_swaps[m].wait_recv()
            mine = 2 * m + pc.c

            def add(z, carry):
                got = gq_r[m, z]
                gq_r[m, z] = (got.astype(F32) + gq_s[mine, z].astype(F32)).astype(BF)
                return carry

            lax.fori_loop(0, 4, add, 0)
            for i, q in enumerate((pc.p, pc.q2)):
                qk_k[m, :, i] = gq_r[m, :, q]
            q_swaps[m].wait_send()

        units[Q0 + 100 * m] = unit(6 + m, lambda q, m=m: gq_r.at[m, :, q], qk_k.at[m], qk_1.at[m], qk_2.at[m], qk_3.at[m], qk_t.at[m], finish_q, source)
    ticks = Ticks(HIND, {u + k + 1: step for u, steps in units.items() for k, step in enumerate(steps)})
    ticks.at(ENTER)
    for copy in loads[:early]:
        copy.wait()
    ones = (lane_of(tok) < 3).astype(BF)

    def pair(j, carry):
        cs = pl.ds(pl.multiple_of(j * 128, 128), 128)
        lane = lane_of(256)
        above = lax.broadcasted_iota(jnp.int32, (256, 256), 0) <= lax.broadcasted_iota(jnp.int32, (256, 256), 1)
        at = j * 384
        dk_s[...] = jnp.zeros_like(dk_s)
        dv_s[...] = jnp.zeros_like(dv_s)
        vaug = jnp.concatenate([v_s[:, cs], ones], axis=1)
        kaug = jnp.concatenate([k_s[:, cs], seg_s[1]], axis=1)
        kt = k_s[:, cs].T
        for i in range(blocks):
            ticks.when(j, range(A + i, A + i + 60, 10))
            rs, first, last = pl.ds(i * 256, 256), i * 256, (i + 1) * 256
            qt, dt = q_s[rs, cs], do_s[rs, cs]
            prod = dt.astype(F32) * o_s[rs, cs].astype(F32)
            parts = []
            for h in range(2):
                mask = (lane < 64) == (h == 0)
                qm, dm = jnp.where(mask, qt, BF(0)), jnp.where(mask, dt, BF(0))
                delta = jnp.sum(jnp.where(mask, prod, 0.0), axis=1, keepdims=True)
                lse = jnp.sum(jnp.where(lane == 2 * j + h, lse_s[rs, :], 0.0), axis=1, keepdims=True)
                a0, a1, a2 = three_way(-lse)
                qa = jnp.where(lane == 4, a0, jnp.where(lane == 5, a1, jnp.where(lane == 6, a2, seg_s[0, rs, :])))
                b0, b1, b2 = three_way(-delta)
                da = jnp.where(lane == 0, b0, jnp.where(lane == 1, b1, jnp.where(lane == 2, b2, BF(0))))
                qaug, daug = jnp.concatenate([qm, qa], axis=1), jnp.concatenate([dm, da], axis=1)
                pd = jnp.exp(jnp.where(above, nt(kaug[first:last], qaug), NEG))
                dsd = (pd * nt(vaug[first:last], daug)).astype(BF)
                dv_s[rs, :] += nn(pd.astype(BF), dm)
                dk_s[rs, :] += nn(dsd, qm)
                dq = nn(kt[h * 64 : h * 64 + 64, first:last], dsd)
                if i:
                    before = pl.ds(0, first)
                    po = jnp.exp(nt(kaug[:first], qaug))
                    dso = (po * nt(vaug[:first], daug)).astype(BF)
                    dv_s[before, :] += nn(po.astype(BF), dm)
                    dk_s[before, :] += nn(dso, qm)
                    dq = dq + nn(kt[h * 64 : h * 64 + 64, :first], dso)
                parts.append(dq)
            dq = jnp.concatenate(parts, axis=0).T * 0.125
            dq = dq * rope_s[0, rs, :] + turned(dq * rope_s[1, rs, :], lane, True)
            dqkv_s[rs, pl.ds(pl.multiple_of(at, 128), 128)] = dq.astype(BF)

        def finish(r, carry):
            rs = pl.ds(pl.multiple_of(r * 256, 256), 256)
            dk = dk_s[rs, :]
            dk = dk * rope_s[0, rs, :] + turned(dk * rope_s[1, rs, :], lane, True)
            dqkv_s[rs, pl.ds(pl.multiple_of(at + 128, 128), 128)] = dk.astype(BF)
            dqkv_s[rs, pl.ds(pl.multiple_of(at + 256, 128), 128)] = dv_s[rs, :].astype(BF)
            return carry

        lax.fori_loop(0, blocks, finish, 0)
        pl.when(j == 0)(loads[early].wait)

        ticks.when(j, range(W, W + 6))

        def weight(z, carry):
            rows = nn(h1t_s[pl.ds(pl.multiple_of(z * 192, 64), 192), :], dqkv_s[:, pl.ds(pl.multiple_of(at, 128), 384)])
            gq_s[j, z] = rows.astype(BF).reshape(4, 48, 384)
            return carry

        lax.fori_loop(0, 4, weight, 0)
        for m in range(3):
            pl.when((j // 2 == m) & (lax.rem(j, 2) != pc.c))(q_swaps[m].start)
        return carry

    lax.fori_loop(0, 6, pair, 0)
    for copy in loads[early + 1 :]:
        copy.wait()
    gg1_s[...] = jnp.zeros_like(gg1_s)
    gain1 = gain_ref[0:1, :]

    def last(r, carry):
        ticks.when(r, range(L, L + 4))
        rs = pl.ds(pl.multiple_of(r * 256, 256), 256)
        dh1 = sum(nt(dqkv_s[rs, m * 768 : (m + 1) * 768], flat(w_s[m])) for m in range(3))
        x = x_s[rs, :].astype(F32)
        r1 = lax.rsqrt(jnp.mean(x * x, axis=1, keepdims=True) + EPS)
        n1 = x * r1
        e1 = dh1 * gain1
        gg1_s[0:1, 0:768] += jnp.sum(dh1 * n1, axis=0, keepdims=True)
        gx_ref[rs, :] = (dx2_s[rs, :] + r1 * (e1 - n1 * jnp.mean(e1 * n1, axis=1, keepdims=True))).astype(BF)
        return carry

    lax.fori_loop(0, blocks, last, 0)
    gg1_s[1:2, 0:768] = gg_ref[0:1, :]
    for w in range(16):
        gg_st[w] = gg1_s[:, 48 * w : 48 * w + 128]
    copies = []
    for d in range(1, 16):
        to = lax.rem(pc.w + d, 16)
        copy = remote(gg_st.at[to], gg_r.at[d - 1], gsend.at[d - 1], grecv.at[d - 1], {"wide": to})
        copy.start()
        copies.append(copy)
    ticks.at(END)
    total = gg_st[pc.w]
    for d in range(1, 16):
        copies[d - 1].wait_recv()
        total = total + gg_r[d - 1]
    gg_c[0] = total
    to_core = remote(gg_c.at[0], gg_c.at[1], gsend.at[15], grecv.at[15], pc.other)
    to_core.start()
    ticks.at(GAINS)
    to_core.wait()
    gg_out[...] = gg_c[0] + gg_c[1]
    for copy in copies:
        copy.wait_send()


def tail_kernel(*refs):
    gg_ref, stage, sem = refs[9], refs[21:30], refs[30]
    into = [pltpu.make_async_copy(refs[k], stage[k], sem.at[0, k]) for k in range(9)]
    out_of = [pltpu.make_async_copy(stage[k], refs[10 + k], sem.at[1, k]) for k in range(9)]
    for copy in into:
        copy.start()
    for n in range(2):
        out = refs[19 + n]
        out[...] = gg_ref[n : n + 1, : out.shape[1]]
    for first, second in zip(into, out_of):
        first.wait()
        second.start()
    for copy in out_of:
        copy.wait()


def shape(dims, dtype=BF):
    return jax.ShapeDtypeStruct(dims, dtype)


def fast_body(tokens, seq_lengths, w_query, w_key, w_value, w_out, w_gate, w_up, w_down, attn_gain, ffn_gain, cotangent):
    tok, width = tokens.shape
    any_spec, vmem_spec = pl.BlockSpec(memory_space=pl.ANY), pl.BlockSpec(memory_space=pltpu.VMEM)
    dma = pltpu.SemaphoreType.DMA
    vm = pltpu.VMEM
    fore = pl.pallas_call(
        fore_kernel,
        out_shape=[
            shape((tok, width)), shape((tok, width)), shape((tok, width)), shape((tok, width)), shape((tok, width)),
            shape((width, tok)), shape((tok, 128), F32), shape((2, tok, 128)), shape((2, tok, 128), F32),
            shape((3, 4, 4, 48, 768)), shape((tok, width), F32), shape((8, width), F32), shape((8, width), F32), shape((tok, width)),
            shape((4, 4, 4, 48, 512)), shape((4, 4, 128, 384)), shape((4, 4, 48, 384)), shape((3, 4, 2, 48, 512)),
        ],
        in_specs=[pl.BlockSpec(memory_space=pltpu.SMEM)] + [vmem_spec] * 4 + [any_spec] * 7,
        out_specs=[any_spec] * 18,
        scratch_shapes=[
            vm((3, 4, 4, 48, 768), BF), vm((4, 4, 48, 768), BF), vm((4, 4, 48, 4096), BF), vm((4, 4, 128, 768), BF), vm((16, 8, 128), F32), vm((8, width), F32),
            vm((tok, width), F32), vm((tok, width), F32), vm((tok, width), F32), vm((width, tok), BF),
            vm((tok, width), BF), vm((tok, width), BF), vm((tok, width), BF), vm((tok, width), BF),
            vm((tok, 128), F32), vm((2, tok, 128), BF), vm((2, tok, 128), F32),
            vm((512, tok), BF), vm((tok, 1024), BF), vm((8, width), F32), vm((tok, width), BF),
            vm((2, 4, 4, 48, 1024), BF), vm((2, 4, 128, 768), BF), vm((4, 4, 48, 768), BF),
            vm((4, 4, 4, 48, 512), BF), vm((4, 4, 128, 384), BF), vm((4, 4, 48, 384), BF),
            dma((31,)), dma((31,)), dma((9, 10)), dma((9, 10)), dma((15,)), dma((15,)), dma((15,)), dma((15,)), dma((19,)), dma((24,)),
        ],
        compiler_params=pltpu.CompilerParams(collective_id=0, has_side_effects=True, vmem_limit_bytes=VMEM_BYTES),
        name="fore",
    )
    (q, k, v, o, do, h1t, lse, seg, rope, wqkv, dx2, gains, gg2, output, gu_sum, d_sum, o_sum, gu_first) = fore(
        seq_lengths, tokens, cotangent, attn_gain[None], ffn_gain[None], w_query, w_key, w_value, w_out, w_gate, w_up, w_down
    )
    hind = pl.pallas_call(
        hind_kernel,
        out_shape=[shape((tok, width))] + [shape((48, width), F32)] * 4 + [shape((48, 2048), F32)] * 2 + [shape((128, width), F32), shape((8, 128), F32)],
        in_specs=[any_spec] * 12 + [vmem_spec] * 2 + [any_spec] * 4,
        out_specs=[vmem_spec] * 9,
        scratch_shapes=[
            vm((tok, width), BF), vm((tok, width), BF), vm((tok, width), BF), vm((tok, width), BF), vm((tok, width), BF),
            vm((tok, 128), F32), vm((2, tok, 128), BF), vm((2, tok, 128), F32), vm((width, tok), BF), vm((3, 4, 4, 48, 768), BF),
            vm((tok, width), BF), vm((tok, width), F32), vm((tok, 2304), BF), vm((tok, 128), F32), vm((tok, 128), F32),
            vm((6, 4, 4, 48, 384), BF), vm((3, 4, 4, 48, 384), BF),
            vm((4, 4, 2, 48, 512), BF), vm((4, 4, 2, 48, 512), BF), vm((4, 4, 48, 512), BF), vm((4, 3, 48, 512), BF), vm((4, 2, 48, 512), F32),
            vm((4, 2, 128, 384), BF), vm((4, 2, 128, 384), BF), vm((4, 128, 384), BF), vm((3, 128, 384), BF), vm((2, 128, 384), F32),
            vm((4, 2, 48, 384), BF), vm((4, 2, 48, 384), BF), vm((4, 48, 384), BF), vm((3, 48, 384), BF), vm((2, 48, 384), F32),
            vm((3, 4, 2, 48, 384), BF), vm((3, 4, 2, 48, 384), BF), vm((3, 4, 48, 384), BF), vm((3, 3, 48, 384), BF), vm((3, 2, 48, 384), F32),
            vm((8, width + 128), F32), vm((16, 8, 128), F32), vm((15, 8, 128), F32), vm((2, 8, 128), F32),
            dma((12,)), dma((6, 3)), dma((9, 7)), dma((9, 7)), dma((3,)), dma((3,)), dma((16,)), dma((16,)),
        ],
        compiler_params=pltpu.CompilerParams(collective_id=1, has_side_effects=True, vmem_limit_bytes=VMEM_BYTES),
        name="hind",
    )
    gx, gwq, gwk, gwv, gwo, gwg, gwu, gwd, gg = hind(q, k, v, o, do, lse, seg, rope, h1t, wqkv, tokens, dx2, gains, gg2, gu_sum, d_sum, o_sum, gu_first)
    count = attn_gain.shape[0]
    large = (gwq, gwk, gwv, gwo, gwg, gwu, gwd, output, gx)
    outs = pl.pallas_call(
        tail_kernel,
        out_shape=[shape(a.shape, a.dtype) for a in large] + [shape((1, count), F32)] * 2,
        in_specs=[any_spec] * 9 + [vmem_spec],
        out_specs=[any_spec] * 9 + [vmem_spec] * 2,
        scratch_shapes=[vm(a.shape, a.dtype) for a in large] + [dma((2, 9))],
        compiler_params=pltpu.CompilerParams(vmem_limit_bytes=VMEM_BYTES),
        name="tail",
    )(*large, gg)
    return (outs[7], outs[8], *outs[:7], outs[9][0], outs[10][0])


def layout(lengths, tok_count):
    slots = jnp.arange(lengths.shape[0])
    seq_ends = jnp.sum(jnp.where(slots[:, None] <= slots[None, :], lengths[:, None], 0), axis=0)
    starts = seq_ends - lengths
    places = jnp.arange(tok_count, dtype=jnp.int32)
    segment = jnp.sum((places[:, None] >= seq_ends[None, :]).astype(jnp.int32), axis=1)
    slot_ids = jnp.arange(lengths.shape[0], dtype=jnp.int32)
    starts_at = jnp.sum(
        jnp.where(segment[:, None] == slot_ids[None, :], starts[None, :], 0), axis=1
    )
    return (segment, places - starts_at)


def rope_tables(positions, head_dim):
    half_dim = head_dim // 2
    column = jnp.arange(half_dim, dtype=jnp.float32)
    frequency = jnp.exp(column * (-2.0 * math.log(10000.0) / head_dim))
    angles = positions.astype(jnp.float32)[:, None] * frequency[None, :]
    angles = jnp.concatenate([angles, angles], axis=1)
    return (jnp.cos(angles), jnp.sin(angles))


def rotate(values, cosine, sine):
    half_dim = values.shape[-1] // 2
    turned = jnp.concatenate([-values[..., half_dim:], values[..., :half_dim]], axis=-1)
    return values * cosine[:, None, :] + turned * sine[:, None, :]


def norm_gain(values, gain):
    return values * lax.rsqrt(jnp.mean(values * values, axis=-1, keepdims=True) + EPS) * gain


def swiglu(gate, upward):
    return jax.nn.silu(gate) * upward


def outer_sum(left, right):
    return lax.dot_general(
        left, right, (((0,), (0,)), ((), ())), preferred_element_type=jnp.float32
    )


def back_dot(rows_in, weight):
    return lax.dot_general(
        rows_in, weight, (((1,), (1,)), ((), ())), preferred_element_type=jnp.float32
    )


def block_scores(query_blk, key_rows, segment, row_index, row_start, scale):
    blk_rows = query_blk.shape[0]
    scores = (
        jnp.einsum("qhd,khd->hqk", query_blk, key_rows, preferred_element_type=jnp.float32) * scale
    )
    seg_blk = segment[row_start : row_start + blk_rows]
    row_blk = row_index[row_start : row_start + blk_rows]
    allowed = (seg_blk[:, None] == segment[None, :]) & (row_index[None, :] <= row_blk[:, None])
    return jnp.where(allowed[None], scores, -1e30)


def attend_forward(queries, key_rows, value_rows, segment):
    tok_count, head_count, head_dim = queries.shape
    scale = head_dim ** (-0.5)
    block_rows = min(512, tok_count)
    row_index = jnp.arange(tok_count, dtype=jnp.int32)
    outputs, totals = ([], [])
    for row_start in range(0, tok_count, block_rows):
        query_blk = queries[row_start : row_start + block_rows]
        scores = block_scores(query_blk, key_rows, segment, row_index, row_start, scale)
        peak = jnp.max(scores, axis=-1, keepdims=True)
        expd = jnp.exp(scores - peak)
        row_mass = jnp.sum(expd, axis=-1, keepdims=True)
        probs_low = (expd / row_mass).astype(jnp.bfloat16)
        outputs.append(
            jnp.einsum("hqk,khd->qhd", probs_low, value_rows, preferred_element_type=jnp.float32)
        )
        totals.append(peak[..., 0] + jnp.log(row_mass[..., 0]))
    return (jnp.concatenate(outputs, axis=0), jnp.concatenate(totals, axis=1))


def attend_backward(queries, key_rows, value_rows, log_total, grad_rows, segment):
    tok_count, head_count, head_dim = queries.shape
    scale = head_dim ** (-0.5)
    block_rows = min(512, tok_count)
    row_index = jnp.arange(tok_count, dtype=jnp.int32)
    grad_keys = jnp.zeros((tok_count, head_count, head_dim), jnp.float32)
    grad_values = jnp.zeros((tok_count, head_count, head_dim), jnp.float32)
    grad_queries = []
    for row_start in range(0, tok_count, block_rows):
        query_blk = queries[row_start : row_start + block_rows]
        grad_blk = grad_rows[row_start : row_start + block_rows]
        scores = block_scores(query_blk, key_rows, segment, row_index, row_start, scale)
        probs = jnp.exp(scores - log_total[:, row_start : row_start + block_rows, None])
        probs_low = probs.astype(jnp.bfloat16)
        grad_probs = jnp.einsum(
            "qhd,khd->hqk", grad_blk, value_rows, preferred_element_type=jnp.float32
        )
        inner = jnp.sum(probs * grad_probs, axis=-1, keepdims=True)
        grad_scores = (probs * (grad_probs - inner)).astype(jnp.bfloat16)
        grad_queries.append(
            jnp.einsum("hqk,khd->qhd", grad_scores, key_rows, preferred_element_type=jnp.float32)
            * scale
        )
        grad_keys = (
            grad_keys
            + jnp.einsum("hqk,qhd->khd", grad_scores, query_blk, preferred_element_type=jnp.float32)
            * scale
        )
        grad_values = grad_values + jnp.einsum(
            "hqk,qhd->khd", probs_low, grad_blk, preferred_element_type=jnp.float32
        )
    return (jnp.concatenate(grad_queries, axis=0), grad_keys, grad_values)


def plain_body(
    tokens,
    seq_lengths,
    w_query,
    w_key,
    w_value,
    w_out,
    w_gate,
    w_up,
    w_down,
    attn_gain,
    ffn_gain,
    cotangent,
):
    gathered = (
        lax.all_gather(w_query, "wide", axis=0, tiled=True),
        lax.all_gather(w_key, "wide", axis=0, tiled=True),
        lax.all_gather(w_value, "wide", axis=0, tiled=True),
        lax.all_gather(w_out, "wide", axis=0, tiled=True),
        lax.all_gather(w_gate, "wide", axis=0, tiled=True),
        lax.all_gather(w_up, "wide", axis=0, tiled=True),
        lax.all_gather(w_down, "wide", axis=0, tiled=True),
        lax.all_gather(attn_gain, "wide", axis=0, tiled=True),
        lax.all_gather(ffn_gain, "wide", axis=0, tiled=True),
    )
    (
        full_query,
        full_key,
        full_value,
        full_out,
        full_gate,
        full_up,
        full_down,
        gain_one,
        gain_two,
    ) = gathered
    gain_one = gain_one.astype(jnp.float32)
    gain_two = gain_two.astype(jnp.float32)
    tok_count, d_model = tokens.shape
    head_count = HEADS
    head_dim = d_model // head_count
    segment, positions = layout(seq_lengths[0], tok_count)
    cosine, sine = rope_tables(positions, head_dim)
    inputs = tokens.astype(jnp.float32)
    h_one = norm_gain(inputs, gain_one).astype(jnp.bfloat16)
    q_pre = jnp.dot(h_one, full_query, preferred_element_type=jnp.float32).reshape(
        tok_count, head_count, head_dim
    )
    k_pre = jnp.dot(h_one, full_key, preferred_element_type=jnp.float32).reshape(
        tok_count, head_count, head_dim
    )
    queries = rotate(q_pre, cosine, sine).astype(jnp.bfloat16)
    key_rows = rotate(k_pre, cosine, sine).astype(jnp.bfloat16)
    value_rows = (
        jnp.dot(h_one, full_value, preferred_element_type=jnp.float32)
        .astype(jnp.bfloat16)
        .reshape(tok_count, head_count, head_dim)
    )
    attended, log_total = attend_forward(queries, key_rows, value_rows, segment)
    attended = attended.reshape(tok_count, d_model).astype(jnp.bfloat16)
    middle = inputs + jnp.dot(attended, full_out, preferred_element_type=jnp.float32)
    h_two = norm_gain(middle, gain_two).astype(jnp.bfloat16)
    gate = jnp.dot(h_two, full_gate, preferred_element_type=jnp.float32)
    upward = jnp.dot(h_two, full_up, preferred_element_type=jnp.float32)
    hidden = swiglu(gate, upward).astype(jnp.bfloat16)
    result = middle + jnp.dot(hidden, full_down, preferred_element_type=jnp.float32)
    output = result.astype(jnp.bfloat16)
    grad_out_rows = cotangent.astype(jnp.float32)
    grad_down = outer_sum(hidden, cotangent)
    grad_hidden = back_dot(cotangent, full_down)
    mix_value, mix_back = jax.vjp(swiglu, gate, upward)
    grad_gate_f, grad_up_f = mix_back(grad_hidden)
    grad_gate_rows = grad_gate_f.astype(jnp.bfloat16)
    grad_up_rows = grad_up_f.astype(jnp.bfloat16)
    grad_gate = outer_sum(h_two, grad_gate_rows)
    grad_up = outer_sum(h_two, grad_up_rows)
    grad_h_two = back_dot(grad_gate_rows, full_gate) + back_dot(grad_up_rows, full_up)
    norm_value_two, norm_back_two = jax.vjp(norm_gain, middle, gain_two)
    grad_mid_norm, grad_gain_two = norm_back_two(grad_h_two)
    grad_middle = grad_out_rows + grad_mid_norm
    grad_mid_low = grad_middle.astype(jnp.bfloat16)
    grad_out_proj = outer_sum(attended, grad_mid_low)
    grad_attended = (
        back_dot(grad_mid_low, full_out)
        .astype(jnp.bfloat16)
        .reshape(tok_count, head_count, head_dim)
    )
    grad_q, grad_k, grad_v = attend_backward(
        queries, key_rows, value_rows, log_total, grad_attended, segment
    )
    rot_value, rot_back = jax.vjp(lambda turned_in: rotate(turned_in, cosine, sine), q_pre)
    grad_q_pre = rot_back(grad_q)[0].astype(jnp.bfloat16).reshape(tok_count, d_model)
    grad_k_pre = rot_back(grad_k)[0].astype(jnp.bfloat16).reshape(tok_count, d_model)
    grad_v_low = grad_v.astype(jnp.bfloat16).reshape(tok_count, d_model)
    grad_query = outer_sum(h_one, grad_q_pre)
    grad_key = outer_sum(h_one, grad_k_pre)
    grad_value = outer_sum(h_one, grad_v_low)
    grad_h_one = (
        back_dot(grad_q_pre, full_query)
        + back_dot(grad_k_pre, full_key)
        + back_dot(grad_v_low, full_value)
    )
    norm_value_one, norm_back_one = jax.vjp(norm_gain, inputs, gain_one)
    grad_in_norm, grad_gain_one = norm_back_one(grad_h_one)
    grad_tokens = (grad_middle + grad_in_norm).astype(jnp.bfloat16)
    wide_shares = (
        lax.psum_scatter(grad_query, "wide", scatter_dimension=0, tiled=True),
        lax.psum_scatter(grad_key, "wide", scatter_dimension=0, tiled=True),
        lax.psum_scatter(grad_value, "wide", scatter_dimension=0, tiled=True),
        lax.psum_scatter(grad_out_proj, "wide", scatter_dimension=0, tiled=True),
        lax.psum_scatter(grad_gate, "wide", scatter_dimension=0, tiled=True),
        lax.psum_scatter(grad_up, "wide", scatter_dimension=0, tiled=True),
        lax.psum_scatter(grad_down, "wide", scatter_dimension=0, tiled=True),
        lax.psum_scatter(grad_gain_one, "wide", scatter_dimension=0, tiled=True),
        lax.psum_scatter(grad_gain_two, "wide", scatter_dimension=0, tiled=True),
    )
    summed = (
        lax.psum(wide_shares[0].astype(jnp.bfloat16), "narrow").astype(jnp.float32),
        lax.psum(wide_shares[1].astype(jnp.bfloat16), "narrow").astype(jnp.float32),
        lax.psum(wide_shares[2].astype(jnp.bfloat16), "narrow").astype(jnp.float32),
        lax.psum(wide_shares[3].astype(jnp.bfloat16), "narrow").astype(jnp.float32),
        lax.psum(wide_shares[4].astype(jnp.bfloat16), "narrow").astype(jnp.float32),
        lax.psum(wide_shares[5].astype(jnp.bfloat16), "narrow").astype(jnp.float32),
        lax.psum(wide_shares[6].astype(jnp.bfloat16), "narrow").astype(jnp.float32),
        lax.psum(wide_shares[7].astype(jnp.bfloat16), "narrow").astype(jnp.float32),
        lax.psum(wide_shares[8].astype(jnp.bfloat16), "narrow").astype(jnp.float32),
    )
    return (
        output,
        grad_tokens,
        summed[0],
        summed[1],
        summed[2],
        summed[3],
        summed[4],
        summed[5],
        summed[6],
        summed[7],
        summed[8],
    )


def solution(mesh):
    in_specs = (
        P(("wide", "narrow"), None),
        P(("wide", "narrow"), None),
        P("wide", None),
        P("wide", None),
        P("wide", None),
        P("wide", None),
        P("wide", None),
        P("wide", None),
        P("wide", None),
        P("wide"),
        P("wide"),
        P(("wide", "narrow"), None),
    )
    out_specs = (
        P(("wide", "narrow"), None),
        P(("wide", "narrow"), None),
        P("wide", None),
        P("wide", None),
        P("wide", None),
        P("wide", None),
        P("wide", None),
        P("wide", None),
        P("wide", None),
        P("wide"),
        P("wide"),
    )
    blocks = (mesh.shape["wide"], mesh.shape["narrow"]) == (16, 2)
    body = fast_body if blocks else plain_body
    return jax.shard_map(body, mesh=mesh, in_specs=in_specs, out_specs=out_specs, check_vma=False)
```

```python
import functools
import math

import jax
import jax.numpy as jnp
from jax import lax
from jax.experimental import pallas as pl
from jax.experimental.pallas import tpu as pltpu
from jax.sharding import PartitionSpec as P

HEADS = 12
EPS = 1e-06
NEG = -1e30
BF = jnp.bfloat16
F32 = jnp.float32
MESH = pl.DeviceIdType.MESH
VMEM_BYTES = 60 * 2**20


def nn(left, right):
    return jnp.dot(left, right, preferred_element_type=F32)


def nt(left, right):
    return lax.dot_general(left, right, (((1,), (1,)), ((), ())), preferred_element_type=F32)


def flat(values):
    return values.reshape(-1, values.shape[-1])


def sigmoid(v):
    return 1.0 / (1.0 + jnp.exp(-v))


def three_way(v):
    high = v.astype(BF)
    rest = v - high.astype(F32)
    mid = rest.astype(BF)
    return high, mid, (rest - mid.astype(F32)).astype(BF)


ENTER, T, N, P_, A, M, F, B, W, L, END, GAINS = 0, 10, 20, 100, 200, 300, 400, 900, 910, 920, 930, 931
Q0, Q1, Q2, O, D0, D1, G0, G1, G2, G3, D = range(0, 1100, 100)
FORE = [
    (ENTER, [Q0 + 0]),
    (T + 1, [Q0 + 13]),
    (T + 2, [Q0 + 12, Q0 + 20, Q0 + 11]),
    (N + 0, [Q0 + 23]),
    (N + 1, [Q0 + 22, Q0 + 40, Q1 + 0]),
    (N + 2, [Q0 + 21, Q0 + 30, Q2 + 0, Q0 + 33]),
    (N + 3, [Q0 + 31, Q0 + 43, Q0 + 42]),
    (P_ + 0, [Q0 + 32, Q0 + 41, Q0 + 5]),
    (P_ + 1, [Q1 + 1]),
    (P_ + 3, [O + 0]),
    (A + 2, [Q1 + 2]),
    (A + 3, [Q2 + 1]),
    (A + 10, [Q1 + 3]),
    (A + 11, [D0 + 0, O + 1]),
    (A + 12, [Q1 + 4, Q2 + 2]),
    (P_ + 10, [Q1 + 5, Q2 + 3]),
    (P_ + 11, [D1 + 0]),
    (P_ + 12, [O + 2]),
    (A + 21, [D0 + 1]),
    (A + 22, [G0 + 0]),
    (A + 30, [D1 + 1]),
    (A + 31, [O + 4, Q2 + 4]),
    (A + 32, [D0 + 2]),
    (P_ + 20, [G0 + 1, Q2 + 5]),
    (A + 40, [G1 + 0]),
    (A + 43, [O + 3, D1 + 2, D0 + 3]),
    (A + 50, [D1 + 3, G0 + 2, D0 + 4]),
    (A + 51, [O + 5, G2 + 0]),
    (A + 52, [G1 + 1]),
    (A + 53, [G3 + 0]),
    (M + 0, [G0 + 3]),
    (M + 1, [D1 + 4]),
    (M + 2, [D0 + 5]),
    (M + 3, [G0 + 4, D1 + 5]),
    (F + 0, [G1 + 2, G2 + 1, G0 + 5]),
    (F + 10, [G3 + 1]),
    (F + 11, [G1 + 3]),
    (F + 12, [G1 + 4]),
    (F + 13, [G2 + 2]),
    (F + 100, [G1 + 5]),
    (F + 101, [G2 + 3]),
    (F + 102, [G3 + 2, G3 + 3]),
    (F + 111, [G2 + 4]),
    (F + 113, [G3 + 4]),
    (F + 121, [G2 + 5]),
    (F + 220, [G3 + 5]),
]
HIND = [
    (ENTER, [G0 + 1, G1 + 1]),
    (A + 3, [G0 + 2, O + 1]),
    (W + 0, [G1 + 2]),
    (A + 10, [D + 1]),
    (A + 11, [G0 + 3]),
    (A + 13, [O + 2]),
    (W + 1, [G1 + 3]),
    (W + 1, [G2 + 1]),
    (A + 31, [D + 2]),
    (A + 32, [O + 3]),
    (W + 3, [G2 + 2]),
    (W + 3, [G3 + 1]),
    (A + 40, [Q0 + 1, D + 3]),
    (W + 4, [G2 + 3]),
    (A + 51, [G3 + 2, Q1 + 1]),
    (A + 52, [Q0 + 2]),
    (W + 5, [G3 + 3]),
    (L + 0, [Q1 + 2]),
    (L + 1, [Q0 + 3]),
    (L + 2, [Q2 + 1, Q1 + 3]),
    (L + 3, [G1 + 4]),
    (END, [G0 + 4, D + 4, Q2 + 2, O + 4, Q0 + 4, O + 5, G2 + 4, Q2 + 3, D + 5, Q1 + 4, G3 + 4, G0 + 5, G2 + 5, G1 + 5, Q0 + 5, G3 + 5, Q1 + 5, Q2 + 4, Q2 + 5]),
]


class Place:
    def __init__(self):
        wide = lax.axis_index("wide")
        self.c = lax.axis_index("narrow")
        self.w = wide
        self.z = wide // 4
        self.p = lax.rem(wide, 4)
        across_y = lax.rem(self.p + 2, 4)
        across_x = self.p + 1 - 2 * lax.rem(self.p, 2)
        self.q1 = (1 - self.c) * across_y + self.c * across_x
        self.q2 = (1 - self.c) * across_x + self.c * across_y
        self.q3 = 3 - self.p
        self.first = {"wide": self.z * 4 + self.q1}
        self.second = {"wide": self.z * 4 + self.q2}
        self.other = {"narrow": 1 - self.c}

    def z_at(self, d):
        return lax.rem(self.z + d + 4, 4)

    def z_dev(self, d):
        return {"wide": self.z_at(d) * 4 + self.p}


def enter(place):
    sem = pltpu.get_barrier_semaphore()
    for d in range(1, 16):
        pl.semaphore_signal(sem, inc=1, device_id={"wide": lax.rem(place.w + d, 16)}, device_id_type=MESH)
    pl.semaphore_signal(sem, inc=1, device_id=place.other, device_id_type=MESH)
    pl.semaphore_wait(sem, 16)


def remote(src, dst, send, recv, device):
    return pltpu.make_async_remote_copy(
        src_ref=src, dst_ref=dst, send_sem=send, recv_sem=recv, device_id=device, device_id_type=MESH
    )


def lane_of(rows, lanes=128):
    return lax.broadcasted_iota(jnp.int32, (rows, lanes), 1)


def spread(index):
    row = lax.broadcasted_iota(jnp.int32, (128, 768), 0)
    col = lax.broadcasted_iota(jnp.int32, (128, 768), 1)
    return jnp.where((col == row + 48 * index) & (row < 48), 1.0, 0.0).astype(BF)


class Gather:
    def __init__(self, place, buf, start, width, rows, send, recv):
        self.place = place
        r0, rn = rows

        def part(z, q, core):
            col = pl.ds(pl.multiple_of(start + core * width, 128), width)
            return buf.at[z, q, pl.ds(r0, rn), col]

        def block(q, core):
            col = pl.ds(pl.multiple_of(start + core * width, 128), width)
            return buf.at[:, q, pl.ds(r0, rn), col]

        self.part, self.block, self.send, self.recv = part, block, send, recv

    def copy(self, k, ref, device):
        return remote(ref, ref, self.send.at[k], self.recv.at[k], device)


def block_steps(unit):
    pc = unit.place
    me = pc.c
    zs = [unit.copy(d - 1, unit.part(pc.z, pc.p, me), pc.z_dev(d)) for d in (1, 2, 3)]
    own = unit.block(pc.p, me)
    to_first = unit.copy(3, own, pc.first)
    to_second = unit.copy(4, own, pc.second)
    on_second = unit.copy(5, unit.block(pc.q1, me), pc.second)
    cores = [unit.copy(6 + i, unit.block(q, me), pc.other) for i, q in enumerate((pc.p, pc.q1, pc.q2, pc.q3))]

    def s0():
        for copy in zs:
            copy.start()

    def s1():
        for copy in zs:
            copy.wait_recv()
        to_first.start()
        to_second.start()
        cores[0].start()

    def s2():
        to_first.wait_recv()
        on_second.start()
        cores[1].start()

    def s3():
        to_second.wait_recv()
        cores[2].start()

    def s4():
        on_second.wait_recv()
        cores[3].start()

    def s5():
        for copy in cores:
            copy.wait_recv()
        for copy in [*zs, to_first, to_second, on_second, *cores]:
            copy.wait_send()

    return [s0, s1, s2, s3, s4, s5]


def piece_steps(unit):
    pc = unit.place
    me = pc.c
    planes = (pc.p, pc.q1, pc.q2, pc.q3)
    zs = [unit.copy(d - 1, unit.part(pc.z, pc.p, me), pc.z_dev(d)) for d in (1, 2, 3)]
    first = [unit.copy(3 + d, unit.part(pc.z_at(-d), pc.p, me), pc.first) for d in range(4)]
    second = [unit.copy(7 + d, unit.part(pc.z_at(-d), pc.p, me), pc.second) for d in range(4)]
    onward = [unit.copy(11 + d, unit.part(pc.z_at(-d), pc.q1, me), pc.second) for d in range(4)]
    cores = [[unit.copy(15 + 4 * i + d, unit.part(pc.z_at(-d), q, me), pc.other) for d in range(4)] for i, q in enumerate(planes)]

    def spread_out(d):
        first[d].start()
        second[d].start()
        cores[0][d].start()

    def s0():
        for copy in zs:
            copy.start()
        spread_out(0)

    def p(d):
        zs[d - 1].wait_recv()
        spread_out(d)

    def a(d):
        first[d].wait_recv()
        onward[d].start()
        cores[1][d].start()

    def b(d):
        second[d].wait_recv()
        cores[2][d].start()

    def c(d):
        onward[d].wait_recv()
        cores[3][d].start()

    def s5():
        for line in cores:
            for copy in line:
                copy.wait_recv()
        for copy in [*zs, *first, *second, *onward, *sum(cores, [])]:
            copy.wait_send()

    steps = {0: s0, 5: s5}
    for number, step in ((10, p), (20, a), (30, b), (40, c)):
        for d in range(4):
            steps[number + d] = functools.partial(step, d)
    del steps[10]
    return steps


class Ticks:
    def __init__(self, table, steps):
        self.steps = steps
        self.table = {}
        for place, listed in table:
            self.table[place] = self.table.get(place, []) + listed
        assert sorted(sum(self.table.values(), [])) == sorted(steps)

    def at(self, place):
        for step in self.table.get(place, []):
            self.steps[step]()

    def when(self, index, places):
        for k, place in enumerate(places):
            if place in self.table:
                pl.when(index == k)(functools.partial(self.at, place))


def turned(values, lane, back):
    up = pltpu.roll(values, 96, 1)
    down = pltpu.roll(values, 32, 1)
    low = lax.rem(lane, 64) < 32
    return jnp.where(low, up, -down) if back else jnp.where(low, -up, down)


def fore_kernel(
    lens, x_ref, dy_ref, g1_ref, g2_ref, wq, wk, wv, wo, wg, wu, wd,
    q_out, k_out, v_out, o_out, do_out, h1t_out, lse_out, seg_out, rope_out, w_out, dx2_out, gain_out, gg_out, y_out, gu_sum, d_sum, o_sum, gu_first,
    w_s, wo_s, wgu_s, wd_s, gain_s, gains, x2_s, y_s, dh2_s, h1t_s, q_s, k_s, v_s, o_s, lse_s, seg_s, rope_s,
    hidt_s, dgu_s, gg_s, yb_s, gu_st, d_st, o_st, gu_r, d_r, o_r,
    wsend, wrecv, usend, urecv, gsend, grecv, rsend, rrecv, lsem, osem,
):
    pc = Place()
    tok = x_ref.shape[0]
    blocks = tok // 256
    loads = []

    def load(src, dst):
        copy = pltpu.make_async_copy(src, dst, lsem.at[len(loads)])
        copy.start()
        loads.append(copy)

    def half(start, width):
        return pl.ds(pl.multiple_of(start + pc.c * width, 128), width)

    for m in range(3):
        for n, w in enumerate((wq, wk, wv)):
            load(w.at[:, half(m * 256, 128)], w_s.at[m, pc.z, pc.p, :, pl.ds(pl.multiple_of(pc.c * 384 + n * 128, 128), 128)])
    early = len(loads)
    load(wo.at[:, half(0, 384)], wo_s.at[pc.z, pc.p, :, half(0, 384)])
    load(wd.at[:, half(0, 384)], wd_s.at[pc.z, pc.p, :, half(0, 384)])
    for u in range(4):
        for n, w in enumerate((wg, wu)):
            load(w.at[:, half(u * 512, 256)], wgu_s.at[pc.z, pc.p, :, pl.ds(pl.multiple_of(u * 1024 + n * 256 + pc.c * 512, 128), 256)])
    enter(pc)
    for copy in loads[:early]:
        copy.wait()
    gain_s[pc.w] = jnp.zeros((8, 128), F32)
    for n, ref in enumerate((g1_ref, g2_ref)):
        gain_s[pc.w, n : n + 1, 0 : ref.shape[1]] = ref[...].astype(F32)
    gain_copies = [
        remote(gain_s.at[pc.w], gain_s.at[pc.w], gsend.at[d - 1], grecv.at[d - 1], {"wide": lax.rem(pc.w + d, 16)}) for d in range(1, 16)
    ]
    for copy in gain_copies:
        copy.start()
    ends, total = [], jnp.int32(0)
    for s in range(4):
        total = total + lens[0, s]
        ends.append(total)

    def tables(r, carry):
        rs = pl.ds(pl.multiple_of(r * 256, 256), 256)
        lane = lane_of(256)
        place = lax.broadcasted_iota(jnp.int32, (256, 128), 0) + r * 256
        seg = jnp.zeros((256, 128), jnp.int32)
        start = jnp.zeros((256, 128), jnp.int32)
        for s in range(4):
            past = place >= ends[s]
            seg = seg + past.astype(jnp.int32)
            start = jnp.where(past, ends[s], start)
        column = lax.rem(lane, 32).astype(F32)
        angle = (place - start).astype(F32) * jnp.exp(column * (-2.0 * math.log(10000.0) / 64))
        rope_s[0, rs, :] = jnp.cos(angle)
        rope_s[1, rs, :] = jnp.sin(angle)
        seg_s[0, rs, :] = jnp.where((lane == seg) | (lane >= 4), 0.0, NEG).astype(BF)
        seg_s[1, rs, :] = jnp.where((lane == seg) | ((lane >= 4) & (lane < 7)), 1.0, 0.0).astype(BF)
        return carry

    units = {
        Q1: Gather(pc, w_s.at[1], 0, 384, (0, 48), usend.at[7], urecv.at[7]),
        Q2: Gather(pc, w_s.at[2], 0, 384, (0, 48), usend.at[8], urecv.at[8]),
        O: Gather(pc, wo_s, 0, 384, (0, 48), usend.at[0], urecv.at[0]),
        D0: Gather(pc, wd_s, 0, 384, (0, 64), usend.at[1], urecv.at[1]),
        D1: Gather(pc, wd_s, 0, 384, (64, 64), usend.at[2], urecv.at[2]),
    }
    for u in range(4):
        units[G0 + 100 * u] = Gather(pc, wgu_s, 1024 * u, 512, (0, 48), usend.at[3 + u], urecv.at[3 + u])
    steps = {Q0 + k: step for k, step in piece_steps(Gather(pc, w_s.at[0], 0, 384, (0, 48), wsend, wrecv)).items()}
    for u, unit in units.items():
        for k, step in enumerate(block_steps(unit)):
            steps[u + k] = step
    ticks = Ticks(FORE, steps)
    ticks.at(ENTER)
    for copy in loads[early:]:
        copy.wait()
    ticks.at(T)
    lax.fori_loop(0, blocks // 2, tables, 0)
    ticks.at(T + 1)
    lax.fori_loop(blocks // 2, blocks, tables, 0)
    for copy in gain_copies:
        copy.wait_recv()
    ticks.at(T + 2)

    def gain_rows(w, rows):
        return rows + nn(gain_s[w].astype(BF), spread(w))

    gains[...] = lax.fori_loop(0, 16, gain_rows, jnp.zeros((8, 768), F32))
    h1_s = yb_s

    def norm(r, carry):
        ticks.when(r, range(N, N + 4))
        rs = pl.ds(pl.multiple_of(r * 256, 256), 256)
        x = x_ref[rs, :].astype(F32)
        h1 = (x * lax.rsqrt(jnp.mean(x * x, axis=1, keepdims=True) + EPS) * gains[0:1, :]).astype(BF)
        h1_s[rs, :] = h1
        h1t_s[:, rs] = h1.T
        return carry

    lax.fori_loop(0, blocks, norm, 0)
    outs = []

    def store(src, dst):
        copy = pltpu.make_async_copy(src, dst, osem.at[len(outs)])
        copy.start()
        outs.append(copy)
        return copy

    store(gains, gain_out)
    kept_h1t = store(h1t_s, h1t_out)
    store(seg_s, seg_out)
    store(rope_s, rope_out)

    def project(m, r, carry):
        for k in range(2):
            ticks.when(2 * m + r, [P_ + 10 * g + i for g in range(3) for i in (k, k + 2)])
        for k in range(2):
            rs = pl.ds(pl.multiple_of(r * 512 + k * 256, 256), 256)
            lane = lane_of(256)
            cos, sin = rope_s[0, rs, :], rope_s[1, rs, :]
            pre = nn(h1_s[rs, :], flat(w_s[m]))
            for n in range(2):
                cs = pl.ds(pl.multiple_of((2 * m + n) * 128, 128), 128)
                qp, kp, vp = (pre[:, n * 384 + t * 128 : n * 384 + (t + 1) * 128] for t in range(3))
                q_s[rs, cs] = (qp * cos + turned(qp, lane, False) * sin).astype(BF) * BF(0.125)
                k_s[rs, cs] = (kp * cos + turned(kp, lane, False) * sin).astype(BF)
                v_s[rs, cs] = vp.astype(BF)
        return carry

    def pair(j, carry):
        cs = pl.ds(pl.multiple_of(j * 128, 128), 128)
        lane = lane_of(256)
        row = lax.broadcasted_iota(jnp.int32, (512, 256), 0)
        below = jnp.where(row >= 256, row - 256, row) >= lax.broadcasted_iota(jnp.int32, (512, 256), 1)
        for i in range(blocks):
            ticks.when(j, range(A + i, A + i + 60, 10))
            rs, before = pl.ds(i * 256, 256), pl.ds(0, i * 256)
            qt, seg = q_s[rs, cs], seg_s[0, rs, :]
            qm = jnp.concatenate([jnp.concatenate([jnp.where((lane < 64) == (h == 0), qt, BF(0)), seg], axis=1) for h in range(2)], axis=0)
            sd = jnp.where(below, nt(qm, jnp.concatenate([k_s[rs, cs], seg_s[1, rs, :]], axis=1)), NEG)
            top = jnp.max(sd, axis=1, keepdims=True)
            if i:
                so = nt(qm, jnp.concatenate([k_s[before, cs], seg_s[1, before, :]], axis=1))
                top = jnp.maximum(top, jnp.max(so, axis=1, keepdims=True))
            pd = jnp.exp(sd - top)
            mass = jnp.sum(pd, axis=1, keepdims=True)
            acc = nn(pd.astype(BF), v_s[rs, cs])
            if i:
                po = jnp.exp(so - top)
                mass = mass + jnp.sum(po, axis=1, keepdims=True)
                acc = acc + nn(po.astype(BF), v_s[before, cs])
            acc = acc * (1.0 / mass)
            lse = top + jnp.log(mass)
            lse_s[rs, :] = jnp.where(lane == 2 * j, lse[:256], jnp.where(lane == 2 * j + 1, lse[256:], lse_s[rs, :]))
            o_s[rs, cs] = jnp.where(lane < 64, acc[:256], acc[256:]).astype(BF)
        return carry

    def group(m, carry):
        lax.fori_loop(0, blocks // 2, functools.partial(project, m), 0)
        lax.fori_loop(2 * m, 2 * m + 2, pair, 0)
        return carry

    lse_s[...] = jnp.zeros_like(lse_s)
    lax.fori_loop(0, 3, group, 0)
    store(w_s, w_out)
    kept = [store(q_s, q_out), store(k_s, k_out), store(v_s, v_out), kept_h1t]
    store(o_s, o_out)
    store(lse_s, lse_out)
    for copy in kept:
        copy.wait()
    h2_s, h2t_s, dxb_s, do_s = q_s, h1t_s, k_s, v_s
    gain2 = gains[1:2, :]

    def middle(r, carry):
        for k in range(2):
            ticks.when(r, range(M + k, M + 4, 2))
        rs = pl.ds(pl.multiple_of(r * 512, 512), 512)
        x2 = x_ref[rs, :].astype(F32) + nn(o_s[rs, :], flat(wo_s[...]))
        x2_s[rs, :] = x2
        h2 = (x2 * lax.rsqrt(jnp.mean(x2 * x2, axis=1, keepdims=True) + EPS) * gain2).astype(BF)
        h2_s[rs, :] = h2
        h2t_s[:, rs] = h2.T
        return carry

    lax.fori_loop(0, blocks // 2, middle, 0)

    def swap(buf, width, got, k):
        far = pl.ds(pl.multiple_of((1 - pc.c) * width, 128), width)
        return remote(buf.at[..., far], got, rsend.at[k], rrecv.at[k], pc.other)

    def near(buf, width):
        return buf[..., pl.ds(pl.multiple_of(pc.c * width, 128), width)]

    gu_swap = [swap(gu_st.at[u % 2], 512, gu_r.at[u], u) for u in range(4)]
    d_swap = [swap(d_st.at[u % 2], 384, d_r.at[u], 4 + u) for u in range(4)]

    ahead = []

    def settle(u):
        gu_swap[u].wait_recv()
        d_swap[u].wait_recv()
        for z in range(4):
            mine = gu_st[u % 2, z, :, :, pl.ds(pl.multiple_of(pc.c * 512, 128), 512)]
            gu_r[u, z] = (gu_r[u, z].astype(F32) + mine.astype(F32)).astype(BF)
        mine = d_st[u % 2, :, :, pl.ds(pl.multiple_of(pc.c * 384, 128), 384)]
        d_r[u] = (d_r[u].astype(F32) + mine.astype(F32)).astype(BF)
        store(gu_r.at[u], gu_sum.at[u])
        if u < 3:
            for k, q in enumerate((pc.q1, pc.q3)):
                copy = remote(gu_r.at[u, :, q], gu_first.at[u, :, k], rsend.at[9 + 2 * u + k], rrecv.at[9 + 2 * u + k], pc.first)
                copy.start()
                ahead.append(copy)
        store(d_r.at[u], d_sum.at[u])
        gu_swap[u].wait_send()
        d_swap[u].wait_send()

    for u in range(4):
        wgu = pl.ds(u * 1024, 1024)

        def mix(r, carry):
            for k in range(2):
                ticks.when(r, range(F + 100 * u + k, F + 100 * u + 4, 2))
            rs = pl.ds(pl.multiple_of(r * 512, 512), 512)
            both = nn(h2_s[rs, :], flat(wgu_s[:, :, :, wgu]))
            dhid = nt(dy_ref[rs, :], flat(wd_s[u]))
            hids, grads = [], []
            for n in range(2):
                gate, up = both[:, n * 512 : n * 512 + 256], both[:, n * 512 + 256 : n * 512 + 512]
                dh = dhid[:, n * 256 : n * 256 + 256]
                sig = sigmoid(gate)
                silu = gate * sig
                hids.append((silu * up).astype(BF))
                grads.append((dh * up * sig * (1.0 + gate * (1.0 - sig))).astype(BF))
                grads.append((dh * silu).astype(BF))
            hid = jnp.concatenate(hids, axis=1)
            dgu = jnp.concatenate(grads, axis=1)
            hidt_s[:, rs] = hid.T
            dgu_s[rs, :] = dgu
            yv = nn(hid, flat(wd_s[u]))
            dv = nt(dgu, flat(wgu_s[:, :, :, wgu]))
            if u == 0:
                y_s[rs, :] = x2_s[rs, :] + yv
                dh2_s[rs, :] = dv
            else:
                y_s[rs, :] += yv
                dh2_s[rs, :] += dv
            return carry

        lax.fori_loop(0, blocks // 2, mix, 0)
        if u >= 2:
            settle(u - 2)

        def weight_gu(z, carry):
            for k in range(2):
                ticks.when(z, range(F + 100 * u + 10 + k, F + 100 * u + 14, 2))
            rows = nn(h2t_s[pl.ds(pl.multiple_of(z * 384, 128), 384), :], dgu_s[...])
            gu_st[u % 2, pl.ds(2 * z, 2)] = rows.astype(BF).reshape(2, 4, 48, 1024)
            return carry

        lax.fori_loop(0, 2, weight_gu, 0)

        for k in range(2):
            ticks.at(F + 100 * u + 20 + k)
        d_st[u % 2] = nn(hidt_s[...], dy_ref[...]).astype(BF).reshape(4, 128, 768)
        gu_swap[u].start()
        d_swap[u].start()

    settle(2)
    gg_s[...] = jnp.zeros_like(gg_s)

    def back(r, carry):
        rs = pl.ds(pl.multiple_of(r * 256, 256), 256)
        yb_s[rs, :] = y_s[rs, :].astype(BF)
        x2, dh2 = x2_s[rs, :], dh2_s[rs, :]
        r2 = lax.rsqrt(jnp.mean(x2 * x2, axis=1, keepdims=True) + EPS)
        n2 = x2 * r2
        e2 = dh2 * gain2
        gg_s[0:1, :] += jnp.sum(dh2 * n2, axis=0, keepdims=True)
        dx2 = dy_ref[rs, :].astype(F32) + r2 * (e2 - n2 * jnp.mean(e2 * n2, axis=1, keepdims=True))
        x2_s[rs, :] = dx2
        dxb_s[rs, :] = dx2.astype(BF)
        h2t_s[:, rs] = o_s[rs, :].T
        return carry

    lax.fori_loop(0, blocks, back, 0)
    store(yb_s, y_out)
    store(x2_s, dx2_out)
    store(gg_s, gg_out)
    settle(3)

    def weight_o(z, carry):
        rows = nn(h2t_s[pl.ds(pl.multiple_of(z * 384, 128), 384), :], dxb_s[...])
        o_st[pl.ds(2 * z, 2)] = rows.astype(BF).reshape(2, 4, 48, 768)
        return carry

    lax.fori_loop(0, 2, weight_o, 0)
    o_swap = swap(o_st, 384, o_r, 8)
    o_swap.start()

    def back_out(r, carry):
        rs = pl.ds(pl.multiple_of(r * 512, 512), 512)
        do_s[rs, :] = nt(dxb_s[rs, :], flat(wo_s[...])).astype(BF)
        return carry

    lax.fori_loop(0, blocks // 2, back_out, 0)
    store(do_s, do_out)
    o_swap.wait_recv()
    mine = o_st[:, :, :, pl.ds(pl.multiple_of(pc.c * 384, 128), 384)]
    o_r[...] = (o_r[...].astype(F32) + mine.astype(F32)).astype(BF)
    store(o_r, o_sum)
    o_swap.wait_send()
    for copy in ahead:
        copy.wait()
    for copy in gain_copies:
        copy.wait_send()
    for copy in outs:
        if not any(copy is done for done in kept):
            copy.wait()


class Reduce:
    def __init__(self, place, keep, r1, r2, r3, total, other_total, send, recv, far1, far2, near):
        pc = place
        self.pc, self.keep, self.r1, self.r2, self.r3, self.total = pc, keep, r1, r2, r3, total
        self.to_first = []
        if far1 is not None:
            self.to_first = [remote(ref, r1.at[:, i], send.at[i], recv.at[i], pc.first) for i, ref in enumerate((far1, far2))]
        self.near = near
        self.to_second = remote(keep.at[:, 1], r2, send.at[2], recv.at[2], pc.second)
        self.zs = [remote(keep.at[pc.z_at(d), 0], r3.at[d - 1], send.at[2 + d], recv.at[2 + d], pc.z_dev(d)) for d in (1, 2, 3)]
        self.to_core = remote(total, other_total, send.at[6], recv.at[6], pc.other)

    def steps(self, begin, finish):
        pc = self.pc

        def r1():
            begin()
            for copy in self.to_first:
                copy.start()

        def r2():
            for copy in self.near:
                copy.wait()
            for copy in self.to_first:
                copy.wait_recv()

            def add(z, carry):
                self.keep[z] = (self.keep[z].astype(F32) + self.r1[z].astype(F32)).astype(BF)
                return carry

            lax.fori_loop(0, 4, add, 0)
            self.to_second.start()

        def r3():
            self.to_second.wait_recv()

            def add(z, carry):
                self.keep[z, 0] = (self.keep[z, 0].astype(F32) + self.r2[z].astype(F32)).astype(BF)
                return carry

            lax.fori_loop(0, 4, add, 0)
            for copy in self.zs:
                copy.start()

        def r4():
            for copy in self.zs:
                copy.wait_recv()
            total = self.keep[pc.z, 0].astype(F32)
            for d in range(3):
                total = total + self.r3[d].astype(F32)
            self.total[...] = total
            self.to_core.start()

        def r5():
            self.to_core.wait()
            finish()
            for copy in [*self.to_first, self.to_second, *self.zs]:
                copy.wait_send()

        return [r1, r2, r3, r4, r5]


def hind_kernel(
    q_hbm, k_hbm, v_hbm, o_hbm, do_hbm, lse_hbm, seg_hbm, rope_hbm, h1t_hbm, w_hbm, x_hbm, dx2_hbm, gain_ref, gg_ref, gu_sum, d_sum, o_sum, gu_first,
    gx_ref, gwq, gwk, gwv, gwo, gwg, gwu, gwd, gg_out,
    q_s, k_s, v_s, o_s, do_s, lse_s, seg_s, rope_s, h1t_s, w_s, x_s, dx2_s, dqkv_s, dk_s, dv_s,
    gq_s, gq_r, gu_k, gu_1, gu_2, gu_3, gu_t, d_k, d_1, d_2, d_3, d_t, o_k, o_1, o_2, o_3, o_t, qk_k, qk_1, qk_2, qk_3, qk_t,
    gg1_s, gg_st, gg_r, gg_c,
    lsem, nsem, ssend, srecv, qsend, qrecv, gsend, grecv,
):
    pc = Place()
    tok = x_s.shape[0]
    blocks = tok // 256
    loads = []

    def load(src, dst):
        copy = pltpu.make_async_copy(src, dst, lsem.at[len(loads)])
        copy.start()
        loads.append(copy)
        return copy

    for src, dst in ((q_hbm, q_s), (k_hbm, k_s), (v_hbm, v_s), (o_hbm, o_s), (do_hbm, do_s), (lse_hbm, lse_s), (seg_hbm, seg_s), (rope_hbm, rope_s)):
        load(src, dst)
    early = len(loads)
    for src, dst in ((h1t_hbm, h1t_s), (w_hbm, w_s), (x_hbm, x_s), (dx2_hbm, dx2_s)):
        load(src, dst)
    enter(pc)

    nears = []

    def start_near(copies):
        for copy in copies:
            copy.start()

    def unit(n, parts, keep, r1, r2, r3, total, finish, source=None, done=None):
        near = []
        if source is None:
            near = [pltpu.make_async_copy(parts(q), keep.at[:, i], nsem.at[n, i]) for i, q in enumerate((pc.p, pc.q2))]
        far = (parts(pc.q1), parts(pc.q3))
        if done is not None:
            near.append(pltpu.make_async_copy(done, r1, nsem.at[n, 2]))
            far = (None, None)
        red = Reduce(pc, keep, r1, r2, r3, total.at[0], total.at[1], ssend.at[n], srecv.at[n], *far, near)

        def begin():
            if source is not None:
                source()
            start_near(near)

        return red.steps(begin, finish)

    def halves(ref):
        mine, others = ref[0], ref[1]
        zero = pc.c == 0
        return jnp.where(zero, mine, others), jnp.where(zero, others, mine)

    units = {}
    for u in range(4):

        def finish_gu(u=u):
            low, high = halves(gu_t.at[u])
            for n, part in enumerate((low, high)):
                gwg[:, pl.ds(u * 512 + n * 256, 256)] = part[:, :256]
                gwu[:, pl.ds(u * 512 + n * 256, 256)] = part[:, 256:]

        done = gu_first.at[u] if u < 3 else None
        units[G0 + 100 * u] = unit(u, lambda q, u=u: gu_sum.at[u, :, q], gu_k.at[u], gu_1.at[u], gu_2.at[u], gu_3.at[u], gu_t.at[u], finish_gu, done=done)

    def finish_o():
        low, high = halves(o_t)
        gwo[:, 0:384] = low
        gwo[:, 384:768] = high

    units[O] = unit(4, lambda q: o_sum.at[:, q], o_k, o_1, o_2, o_3, o_t, finish_o)

    def finish_d():
        low, high = halves(d_t)
        gwd[:, 0:384] = low
        gwd[:, 384:768] = high

    units[D] = unit(5, lambda q: d_sum.at[:, q], d_k, d_1, d_2, d_3, d_t, finish_d)

    q_swaps = [remote(gq_s.at[2 * m + 1 - pc.c], gq_r.at[m], qsend.at[m], qrecv.at[m], pc.other) for m in range(3)]

    for m in range(3):

        def finish_q(m=m):
            low, high = halves(qk_t.at[m])
            for n, part in enumerate((low, high)):
                cs = pl.ds((2 * m + n) * 128, 128)
                gwq[:, cs] = part[:, 0:128]
                gwk[:, cs] = part[:, 128:256]
                gwv[:, cs] = part[:, 256:384]

        def source(m=m):
            q_swaps[m].wait_recv()
            mine = 2 * m + pc.c

            def add(z, carry):
                got = gq_r[m, z]
                gq_r[m, z] = (got.astype(F32) + gq_s[mine, z].astype(F32)).astype(BF)
                return carry

            lax.fori_loop(0, 4, add, 0)
            for i, q in enumerate((pc.p, pc.q2)):
                qk_k[m, :, i] = gq_r[m, :, q]
            q_swaps[m].wait_send()

        units[Q0 + 100 * m] = unit(6 + m, lambda q, m=m: gq_r.at[m, :, q], qk_k.at[m], qk_1.at[m], qk_2.at[m], qk_3.at[m], qk_t.at[m], finish_q, source)
    ticks = Ticks(HIND, {u + k + 1: step for u, steps in units.items() for k, step in enumerate(steps)})
    ticks.at(ENTER)
    for copy in loads[:early]:
        copy.wait()
    ones = (lane_of(tok) < 3).astype(BF)

    def pair(j, carry):
        cs = pl.ds(pl.multiple_of(j * 128, 128), 128)
        lane = lane_of(256)
        col = lax.broadcasted_iota(jnp.int32, (256, 512), 1)
        above = lax.broadcasted_iota(jnp.int32, (256, 512), 0) <= jnp.where(col >= 256, col - 256, col)
        at = j * 384
        vaug = jnp.concatenate([v_s[:, cs], ones], axis=1)
        kaug = jnp.concatenate([k_s[:, cs], seg_s[1]], axis=1)
        kt = k_s[:, cs].T
        for i in range(blocks):
            ticks.when(j, range(A + i, A + i + 60, 10))
            rs, first, last = pl.ds(i * 256, 256), i * 256, (i + 1) * 256
            qt, dt = q_s[rs, cs], do_s[rs, cs]
            prod = dt.astype(F32) * o_s[rs, cs].astype(F32)
            qms, dms, qas, das = [], [], [], []
            for h in range(2):
                mask = (lane < 64) == (h == 0)
                qms.append(jnp.where(mask, qt, BF(0)))
                dms.append(jnp.where(mask, dt, BF(0)))
                delta = jnp.sum(jnp.where(mask, prod, 0.0), axis=1, keepdims=True)
                lse = jnp.sum(jnp.where(lane == 2 * j + h, lse_s[rs, :], 0.0), axis=1, keepdims=True)
                a0, a1, a2 = three_way(-lse)
                qa = jnp.where(lane == 4, a0, jnp.where(lane == 5, a1, jnp.where(lane == 6, a2, seg_s[0, rs, :])))
                b0, b1, b2 = three_way(-delta)
                da = jnp.where(lane == 0, b0, jnp.where(lane == 1, b1, jnp.where(lane == 2, b2, BF(0))))
                qas.append(jnp.concatenate([qms[h], qa], axis=1))
                das.append(jnp.concatenate([dms[h], da], axis=1))
            qm, dm, qaug, daug = (jnp.concatenate(t, axis=0) for t in (qms, dms, qas, das))
            pd = jnp.exp(jnp.where(above, nt(kaug[first:last], qaug), NEG))
            dsd = (pd * nt(vaug[first:last], daug)).astype(BF)
            dv_s[rs, :] = nn(pd.astype(BF), dm)
            dk_s[rs, :] = nn(dsd, qm)
            parts = [nn(kt[h * 64 : h * 64 + 64, first:last], dsd[:, h * 256 : h * 256 + 256]) for h in range(2)]
            if i:
                before = pl.ds(0, first)
                po = jnp.exp(nt(kaug[:first], qaug))
                dso = (po * nt(vaug[:first], daug)).astype(BF)
                dv_s[before, :] += nn(po.astype(BF), dm)
                dk_s[before, :] += nn(dso, qm)
                parts = [parts[h] + nn(kt[h * 64 : h * 64 + 64, :first], dso[:, h * 256 : h * 256 + 256]) for h in range(2)]
            dq = jnp.concatenate(parts, axis=0).T * 0.125
            dq = dq * rope_s[0, rs, :] + turned(dq * rope_s[1, rs, :], lane, True)
            dqkv_s[rs, pl.ds(pl.multiple_of(at, 128), 128)] = dq.astype(BF)

        def finish(r, carry):
            rs = pl.ds(pl.multiple_of(r * 256, 256), 256)
            dk = dk_s[rs, :]
            dk = dk * rope_s[0, rs, :] + turned(dk * rope_s[1, rs, :], lane, True)
            dqkv_s[rs, pl.ds(pl.multiple_of(at + 128, 128), 128)] = dk.astype(BF)
            dqkv_s[rs, pl.ds(pl.multiple_of(at + 256, 128), 128)] = dv_s[rs, :].astype(BF)
            return carry

        lax.fori_loop(0, blocks, finish, 0)
        pl.when(j == 0)(loads[early].wait)

        ticks.when(j, range(W, W + 6))

        def weight(z, carry):
            rows = nn(h1t_s[pl.ds(pl.multiple_of(z * 384, 128), 384), :], dqkv_s[:, pl.ds(pl.multiple_of(at, 128), 384)])
            gq_s[j, pl.ds(2 * z, 2)] = rows.astype(BF).reshape(2, 4, 48, 384)
            return carry

        lax.fori_loop(0, 2, weight, 0)
        for m in range(3):
            pl.when((j // 2 == m) & (lax.rem(j, 2) != pc.c))(q_swaps[m].start)
        return carry

    lax.fori_loop(0, 6, pair, 0)
    for copy in loads[early + 1 :]:
        copy.wait()
    gg1_s[...] = jnp.zeros_like(gg1_s)
    gain1 = gain_ref[0:1, :]

    def last(r, carry):
        for k in range(2):
            ticks.when(r, range(L + k, L + 4, 2))
        rs = pl.ds(pl.multiple_of(r * 512, 512), 512)
        dh1 = sum(nt(dqkv_s[rs, m * 768 : (m + 1) * 768], flat(w_s[m])) for m in range(3))
        x = x_s[rs, :].astype(F32)
        r1 = lax.rsqrt(jnp.mean(x * x, axis=1, keepdims=True) + EPS)
        n1 = x * r1
        e1 = dh1 * gain1
        gg1_s[0:1, 0:768] += jnp.sum(dh1 * n1, axis=0, keepdims=True)
        gx_ref[rs, :] = (dx2_s[rs, :] + r1 * (e1 - n1 * jnp.mean(e1 * n1, axis=1, keepdims=True))).astype(BF)
        return carry

    lax.fori_loop(0, blocks // 2, last, 0)
    gg1_s[1:2, 0:768] = gg_ref[0:1, :]
    for w in range(16):
        gg_st[w] = gg1_s[:, 48 * w : 48 * w + 128]
    copies = []
    for d in range(1, 16):
        to = lax.rem(pc.w + d, 16)
        copy = remote(gg_st.at[to], gg_r.at[d - 1], gsend.at[d - 1], grecv.at[d - 1], {"wide": to})
        copy.start()
        copies.append(copy)
    ticks.at(END)
    total = gg_st[pc.w]
    for d in range(1, 16):
        copies[d - 1].wait_recv()
        total = total + gg_r[d - 1]
    gg_c[0] = total
    to_core = remote(gg_c.at[0], gg_c.at[1], gsend.at[15], grecv.at[15], pc.other)
    to_core.start()
    ticks.at(GAINS)
    to_core.wait()
    gg_out[...] = gg_c[0] + gg_c[1]
    for copy in copies:
        copy.wait_send()


def tail_kernel(*refs):
    gg_ref, stage, sem = refs[9], refs[21:30], refs[30]
    into = [pltpu.make_async_copy(refs[k], stage[k], sem.at[0, k]) for k in range(9)]
    out_of = [pltpu.make_async_copy(stage[k], refs[10 + k], sem.at[1, k]) for k in range(9)]
    for copy in into:
        copy.start()
    for n in range(2):
        out = refs[19 + n]
        out[...] = gg_ref[n : n + 1, : out.shape[1]]
    for first, second in zip(into, out_of):
        first.wait()
        second.start()
    for copy in out_of:
        copy.wait()


def shape(dims, dtype=BF):
    return jax.ShapeDtypeStruct(dims, dtype)


def fast_body(tokens, seq_lengths, w_query, w_key, w_value, w_out, w_gate, w_up, w_down, attn_gain, ffn_gain, cotangent):
    tok, width = tokens.shape
    any_spec, vmem_spec = pl.BlockSpec(memory_space=pl.ANY), pl.BlockSpec(memory_space=pltpu.VMEM)
    dma = pltpu.SemaphoreType.DMA
    vm = pltpu.VMEM
    fore = pl.pallas_call(
        fore_kernel,
        out_shape=[
            shape((tok, width)), shape((tok, width)), shape((tok, width)), shape((tok, width)), shape((tok, width)),
            shape((width, tok)), shape((tok, 128), F32), shape((2, tok, 128)), shape((2, tok, 128), F32),
            shape((3, 4, 4, 48, 768)), shape((tok, width), F32), shape((8, width), F32), shape((8, width), F32), shape((tok, width)),
            shape((4, 4, 4, 48, 512)), shape((4, 4, 128, 384)), shape((4, 4, 48, 384)), shape((3, 4, 2, 48, 512)),
        ],
        in_specs=[pl.BlockSpec(memory_space=pltpu.SMEM)] + [vmem_spec] * 4 + [any_spec] * 7,
        out_specs=[any_spec] * 18,
        scratch_shapes=[
            vm((3, 4, 4, 48, 768), BF), vm((4, 4, 48, 768), BF), vm((4, 4, 48, 4096), BF), vm((4, 4, 128, 768), BF), vm((16, 8, 128), F32), vm((8, width), F32),
            vm((tok, width), F32), vm((tok, width), F32), vm((tok, width), F32), vm((width, tok), BF),
            vm((tok, width), BF), vm((tok, width), BF), vm((tok, width), BF), vm((tok, width), BF),
            vm((tok, 128), F32), vm((2, tok, 128), BF), vm((2, tok, 128), F32),
            vm((512, tok), BF), vm((tok, 1024), BF), vm((8, width), F32), vm((tok, width), BF),
            vm((2, 4, 4, 48, 1024), BF), vm((2, 4, 128, 768), BF), vm((4, 4, 48, 768), BF),
            vm((4, 4, 4, 48, 512), BF), vm((4, 4, 128, 384), BF), vm((4, 4, 48, 384), BF),
            dma((31,)), dma((31,)), dma((9, 10)), dma((9, 10)), dma((15,)), dma((15,)), dma((15,)), dma((15,)), dma((19,)), dma((24,)),
        ],
        compiler_params=pltpu.CompilerParams(collective_id=0, has_side_effects=True, vmem_limit_bytes=VMEM_BYTES),
        name="fore",
    )
    (q, k, v, o, do, h1t, lse, seg, rope, wqkv, dx2, gains, gg2, output, gu_sum, d_sum, o_sum, gu_first) = fore(
        seq_lengths, tokens, cotangent, attn_gain[None], ffn_gain[None], w_query, w_key, w_value, w_out, w_gate, w_up, w_down
    )
    hind = pl.pallas_call(
        hind_kernel,
        out_shape=[shape((tok, width))] + [shape((48, width), F32)] * 4 + [shape((48, 2048), F32)] * 2 + [shape((128, width), F32), shape((8, 128), F32)],
        in_specs=[any_spec] * 12 + [vmem_spec] * 2 + [any_spec] * 4,
        out_specs=[vmem_spec] * 9,
        scratch_shapes=[
            vm((tok, width), BF), vm((tok, width), BF), vm((tok, width), BF), vm((tok, width), BF), vm((tok, width), BF),
            vm((tok, 128), F32), vm((2, tok, 128), BF), vm((2, tok, 128), F32), vm((width, tok), BF), vm((3, 4, 4, 48, 768), BF),
            vm((tok, width), BF), vm((tok, width), F32), vm((tok, 2304), BF), vm((tok, 128), F32), vm((tok, 128), F32),
            vm((6, 4, 4, 48, 384), BF), vm((3, 4, 4, 48, 384), BF),
            vm((4, 4, 2, 48, 512), BF), vm((4, 4, 2, 48, 512), BF), vm((4, 4, 48, 512), BF), vm((4, 3, 48, 512), BF), vm((4, 2, 48, 512), F32),
            vm((4, 2, 128, 384), BF), vm((4, 2, 128, 384), BF), vm((4, 128, 384), BF), vm((3, 128, 384), BF), vm((2, 128, 384), F32),
            vm((4, 2, 48, 384), BF), vm((4, 2, 48, 384), BF), vm((4, 48, 384), BF), vm((3, 48, 384), BF), vm((2, 48, 384), F32),
            vm((3, 4, 2, 48, 384), BF), vm((3, 4, 2, 48, 384), BF), vm((3, 4, 48, 384), BF), vm((3, 3, 48, 384), BF), vm((3, 2, 48, 384), F32),
            vm((8, width + 128), F32), vm((16, 8, 128), F32), vm((15, 8, 128), F32), vm((2, 8, 128), F32),
            dma((12,)), dma((6, 3)), dma((9, 7)), dma((9, 7)), dma((3,)), dma((3,)), dma((16,)), dma((16,)),
        ],
        compiler_params=pltpu.CompilerParams(collective_id=1, has_side_effects=True, vmem_limit_bytes=VMEM_BYTES),
        name="hind",
    )
    gx, gwq, gwk, gwv, gwo, gwg, gwu, gwd, gg = hind(q, k, v, o, do, lse, seg, rope, h1t, wqkv, tokens, dx2, gains, gg2, gu_sum, d_sum, o_sum, gu_first)
    count = attn_gain.shape[0]
    large = (gwq, gwk, gwv, gwo, gwg, gwu, gwd, output, gx)
    outs = pl.pallas_call(
        tail_kernel,
        out_shape=[shape(a.shape, a.dtype) for a in large] + [shape((1, count), F32)] * 2,
        in_specs=[any_spec] * 9 + [vmem_spec],
        out_specs=[any_spec] * 9 + [vmem_spec] * 2,
        scratch_shapes=[vm(a.shape, a.dtype) for a in large] + [dma((2, 9))],
        compiler_params=pltpu.CompilerParams(vmem_limit_bytes=VMEM_BYTES),
        name="tail",
    )(*large, gg)
    return (outs[7], outs[8], *outs[:7], outs[9][0], outs[10][0])


def layout(lengths, tok_count):
    slots = jnp.arange(lengths.shape[0])
    seq_ends = jnp.sum(jnp.where(slots[:, None] <= slots[None, :], lengths[:, None], 0), axis=0)
    starts = seq_ends - lengths
    places = jnp.arange(tok_count, dtype=jnp.int32)
    segment = jnp.sum((places[:, None] >= seq_ends[None, :]).astype(jnp.int32), axis=1)
    slot_ids = jnp.arange(lengths.shape[0], dtype=jnp.int32)
    starts_at = jnp.sum(
        jnp.where(segment[:, None] == slot_ids[None, :], starts[None, :], 0), axis=1
    )
    return (segment, places - starts_at)


def rope_tables(positions, head_dim):
    half_dim = head_dim // 2
    column = jnp.arange(half_dim, dtype=jnp.float32)
    frequency = jnp.exp(column * (-2.0 * math.log(10000.0) / head_dim))
    angles = positions.astype(jnp.float32)[:, None] * frequency[None, :]
    angles = jnp.concatenate([angles, angles], axis=1)
    return (jnp.cos(angles), jnp.sin(angles))


def rotate(values, cosine, sine):
    half_dim = values.shape[-1] // 2
    turned = jnp.concatenate([-values[..., half_dim:], values[..., :half_dim]], axis=-1)
    return values * cosine[:, None, :] + turned * sine[:, None, :]


def norm_gain(values, gain):
    return values * lax.rsqrt(jnp.mean(values * values, axis=-1, keepdims=True) + EPS) * gain


def swiglu(gate, upward):
    return jax.nn.silu(gate) * upward


def outer_sum(left, right):
    return lax.dot_general(
        left, right, (((0,), (0,)), ((), ())), preferred_element_type=jnp.float32
    )


def back_dot(rows_in, weight):
    return lax.dot_general(
        rows_in, weight, (((1,), (1,)), ((), ())), preferred_element_type=jnp.float32
    )


def block_scores(query_blk, key_rows, segment, row_index, row_start, scale):
    blk_rows = query_blk.shape[0]
    scores = (
        jnp.einsum("qhd,khd->hqk", query_blk, key_rows, preferred_element_type=jnp.float32) * scale
    )
    seg_blk = segment[row_start : row_start + blk_rows]
    row_blk = row_index[row_start : row_start + blk_rows]
    allowed = (seg_blk[:, None] == segment[None, :]) & (row_index[None, :] <= row_blk[:, None])
    return jnp.where(allowed[None], scores, -1e30)


def attend_forward(queries, key_rows, value_rows, segment):
    tok_count, head_count, head_dim = queries.shape
    scale = head_dim ** (-0.5)
    block_rows = min(512, tok_count)
    row_index = jnp.arange(tok_count, dtype=jnp.int32)
    outputs, totals = ([], [])
    for row_start in range(0, tok_count, block_rows):
        query_blk = queries[row_start : row_start + block_rows]
        scores = block_scores(query_blk, key_rows, segment, row_index, row_start, scale)
        peak = jnp.max(scores, axis=-1, keepdims=True)
        expd = jnp.exp(scores - peak)
        row_mass = jnp.sum(expd, axis=-1, keepdims=True)
        probs_low = (expd / row_mass).astype(jnp.bfloat16)
        outputs.append(
            jnp.einsum("hqk,khd->qhd", probs_low, value_rows, preferred_element_type=jnp.float32)
        )
        totals.append(peak[..., 0] + jnp.log(row_mass[..., 0]))
    return (jnp.concatenate(outputs, axis=0), jnp.concatenate(totals, axis=1))


def attend_backward(queries, key_rows, value_rows, log_total, grad_rows, segment):
    tok_count, head_count, head_dim = queries.shape
    scale = head_dim ** (-0.5)
    block_rows = min(512, tok_count)
    row_index = jnp.arange(tok_count, dtype=jnp.int32)
    grad_keys = jnp.zeros((tok_count, head_count, head_dim), jnp.float32)
    grad_values = jnp.zeros((tok_count, head_count, head_dim), jnp.float32)
    grad_queries = []
    for row_start in range(0, tok_count, block_rows):
        query_blk = queries[row_start : row_start + block_rows]
        grad_blk = grad_rows[row_start : row_start + block_rows]
        scores = block_scores(query_blk, key_rows, segment, row_index, row_start, scale)
        probs = jnp.exp(scores - log_total[:, row_start : row_start + block_rows, None])
        probs_low = probs.astype(jnp.bfloat16)
        grad_probs = jnp.einsum(
            "qhd,khd->hqk", grad_blk, value_rows, preferred_element_type=jnp.float32
        )
        inner = jnp.sum(probs * grad_probs, axis=-1, keepdims=True)
        grad_scores = (probs * (grad_probs - inner)).astype(jnp.bfloat16)
        grad_queries.append(
            jnp.einsum("hqk,khd->qhd", grad_scores, key_rows, preferred_element_type=jnp.float32)
            * scale
        )
        grad_keys = (
            grad_keys
            + jnp.einsum("hqk,qhd->khd", grad_scores, query_blk, preferred_element_type=jnp.float32)
            * scale
        )
        grad_values = grad_values + jnp.einsum(
            "hqk,qhd->khd", probs_low, grad_blk, preferred_element_type=jnp.float32
        )
    return (jnp.concatenate(grad_queries, axis=0), grad_keys, grad_values)


def plain_body(
    tokens,
    seq_lengths,
    w_query,
    w_key,
    w_value,
    w_out,
    w_gate,
    w_up,
    w_down,
    attn_gain,
    ffn_gain,
    cotangent,
):
    gathered = (
        lax.all_gather(w_query, "wide", axis=0, tiled=True),
        lax.all_gather(w_key, "wide", axis=0, tiled=True),
        lax.all_gather(w_value, "wide", axis=0, tiled=True),
        lax.all_gather(w_out, "wide", axis=0, tiled=True),
        lax.all_gather(w_gate, "wide", axis=0, tiled=True),
        lax.all_gather(w_up, "wide", axis=0, tiled=True),
        lax.all_gather(w_down, "wide", axis=0, tiled=True),
        lax.all_gather(attn_gain, "wide", axis=0, tiled=True),
        lax.all_gather(ffn_gain, "wide", axis=0, tiled=True),
    )
    (
        full_query,
        full_key,
        full_value,
        full_out,
        full_gate,
        full_up,
        full_down,
        gain_one,
        gain_two,
    ) = gathered
    gain_one = gain_one.astype(jnp.float32)
    gain_two = gain_two.astype(jnp.float32)
    tok_count, d_model = tokens.shape
    head_count = HEADS
    head_dim = d_model // head_count
    segment, positions = layout(seq_lengths[0], tok_count)
    cosine, sine = rope_tables(positions, head_dim)
    inputs = tokens.astype(jnp.float32)
    h_one = norm_gain(inputs, gain_one).astype(jnp.bfloat16)
    q_pre = jnp.dot(h_one, full_query, preferred_element_type=jnp.float32).reshape(
        tok_count, head_count, head_dim
    )
    k_pre = jnp.dot(h_one, full_key, preferred_element_type=jnp.float32).reshape(
        tok_count, head_count, head_dim
    )
    queries = rotate(q_pre, cosine, sine).astype(jnp.bfloat16)
    key_rows = rotate(k_pre, cosine, sine).astype(jnp.bfloat16)
    value_rows = (
        jnp.dot(h_one, full_value, preferred_element_type=jnp.float32)
        .astype(jnp.bfloat16)
        .reshape(tok_count, head_count, head_dim)
    )
    attended, log_total = attend_forward(queries, key_rows, value_rows, segment)
    attended = attended.reshape(tok_count, d_model).astype(jnp.bfloat16)
    middle = inputs + jnp.dot(attended, full_out, preferred_element_type=jnp.float32)
    h_two = norm_gain(middle, gain_two).astype(jnp.bfloat16)
    gate = jnp.dot(h_two, full_gate, preferred_element_type=jnp.float32)
    upward = jnp.dot(h_two, full_up, preferred_element_type=jnp.float32)
    hidden = swiglu(gate, upward).astype(jnp.bfloat16)
    result = middle + jnp.dot(hidden, full_down, preferred_element_type=jnp.float32)
    output = result.astype(jnp.bfloat16)
    grad_out_rows = cotangent.astype(jnp.float32)
    grad_down = outer_sum(hidden, cotangent)
    grad_hidden = back_dot(cotangent, full_down)
    mix_value, mix_back = jax.vjp(swiglu, gate, upward)
    grad_gate_f, grad_up_f = mix_back(grad_hidden)
    grad_gate_rows = grad_gate_f.astype(jnp.bfloat16)
    grad_up_rows = grad_up_f.astype(jnp.bfloat16)
    grad_gate = outer_sum(h_two, grad_gate_rows)
    grad_up = outer_sum(h_two, grad_up_rows)
    grad_h_two = back_dot(grad_gate_rows, full_gate) + back_dot(grad_up_rows, full_up)
    norm_value_two, norm_back_two = jax.vjp(norm_gain, middle, gain_two)
    grad_mid_norm, grad_gain_two = norm_back_two(grad_h_two)
    grad_middle = grad_out_rows + grad_mid_norm
    grad_mid_low = grad_middle.astype(jnp.bfloat16)
    grad_out_proj = outer_sum(attended, grad_mid_low)
    grad_attended = (
        back_dot(grad_mid_low, full_out)
        .astype(jnp.bfloat16)
        .reshape(tok_count, head_count, head_dim)
    )
    grad_q, grad_k, grad_v = attend_backward(
        queries, key_rows, value_rows, log_total, grad_attended, segment
    )
    rot_value, rot_back = jax.vjp(lambda turned_in: rotate(turned_in, cosine, sine), q_pre)
    grad_q_pre = rot_back(grad_q)[0].astype(jnp.bfloat16).reshape(tok_count, d_model)
    grad_k_pre = rot_back(grad_k)[0].astype(jnp.bfloat16).reshape(tok_count, d_model)
    grad_v_low = grad_v.astype(jnp.bfloat16).reshape(tok_count, d_model)
    grad_query = outer_sum(h_one, grad_q_pre)
    grad_key = outer_sum(h_one, grad_k_pre)
    grad_value = outer_sum(h_one, grad_v_low)
    grad_h_one = (
        back_dot(grad_q_pre, full_query)
        + back_dot(grad_k_pre, full_key)
        + back_dot(grad_v_low, full_value)
    )
    norm_value_one, norm_back_one = jax.vjp(norm_gain, inputs, gain_one)
    grad_in_norm, grad_gain_one = norm_back_one(grad_h_one)
    grad_tokens = (grad_middle + grad_in_norm).astype(jnp.bfloat16)
    wide_shares = (
        lax.psum_scatter(grad_query, "wide", scatter_dimension=0, tiled=True),
        lax.psum_scatter(grad_key, "wide", scatter_dimension=0, tiled=True),
        lax.psum_scatter(grad_value, "wide", scatter_dimension=0, tiled=True),
        lax.psum_scatter(grad_out_proj, "wide", scatter_dimension=0, tiled=True),
        lax.psum_scatter(grad_gate, "wide", scatter_dimension=0, tiled=True),
        lax.psum_scatter(grad_up, "wide", scatter_dimension=0, tiled=True),
        lax.psum_scatter(grad_down, "wide", scatter_dimension=0, tiled=True),
        lax.psum_scatter(grad_gain_one, "wide", scatter_dimension=0, tiled=True),
        lax.psum_scatter(grad_gain_two, "wide", scatter_dimension=0, tiled=True),
    )
    summed = (
        lax.psum(wide_shares[0].astype(jnp.bfloat16), "narrow").astype(jnp.float32),
        lax.psum(wide_shares[1].astype(jnp.bfloat16), "narrow").astype(jnp.float32),
        lax.psum(wide_shares[2].astype(jnp.bfloat16), "narrow").astype(jnp.float32),
        lax.psum(wide_shares[3].astype(jnp.bfloat16), "narrow").astype(jnp.float32),
        lax.psum(wide_shares[4].astype(jnp.bfloat16), "narrow").astype(jnp.float32),
        lax.psum(wide_shares[5].astype(jnp.bfloat16), "narrow").astype(jnp.float32),
        lax.psum(wide_shares[6].astype(jnp.bfloat16), "narrow").astype(jnp.float32),
        lax.psum(wide_shares[7].astype(jnp.bfloat16), "narrow").astype(jnp.float32),
        lax.psum(wide_shares[8].astype(jnp.bfloat16), "narrow").astype(jnp.float32),
    )
    return (
        output,
        grad_tokens,
        summed[0],
        summed[1],
        summed[2],
        summed[3],
        summed[4],
        summed[5],
        summed[6],
        summed[7],
        summed[8],
    )


def solution(mesh):
    in_specs = (
        P(("wide", "narrow"), None),
        P(("wide", "narrow"), None),
        P("wide", None),
        P("wide", None),
        P("wide", None),
        P("wide", None),
        P("wide", None),
        P("wide", None),
        P("wide", None),
        P("wide"),
        P("wide"),
        P(("wide", "narrow"), None),
    )
    out_specs = (
        P(("wide", "narrow"), None),
        P(("wide", "narrow"), None),
        P("wide", None),
        P("wide", None),
        P("wide", None),
        P("wide", None),
        P("wide", None),
        P("wide", None),
        P("wide", None),
        P("wide"),
        P("wide"),
    )
    blocks = (mesh.shape["wide"], mesh.shape["narrow"]) == (16, 2)
    body = fast_body if blocks else plain_body
    return jax.shard_map(body, mesh=mesh, in_specs=in_specs, out_specs=out_specs, check_vma=False)
```
